32 devices in a mesh: fsdp: 2 (over x), ctx: 4 (over z), tp: 4 (over y, core).
Axes of the slice: x: 2, y: 2, z: 4, core: 2. Of those that a mesh axis runs over, the one named last changes fastest.
Arguments:
- tokens: bfloat16 [16, 1040, 768], P('fsdp', ('ctx', 'tp')), may hold values from -6 to 6
- cotangent: bfloat16 [16, 1040, 768], P('fsdp', ('ctx', 'tp')), may hold values from -6 to 6
- layer_gains: float32 [4, 768], replicated, may hold values from -0.5 to 1.8, as said below
- layer_first: float32 [4, 768], replicated
- layer_second: float32 [4, 768], replicated, may hold values from 8320 to 133120
- inner_gains: float32 [2, 2048], P(None, 'tp'), may hold values from -0.5 to 1.8, as said below
- inner_first: float32 [2, 2048], P(None, 'tp')
- inner_second: float32 [2, 2048], P(None, 'tp'), may hold values from 2080 to 33280
- attend_weight: float32 [3, 768, 768], P(None, ('fsdp', 'ctx'), 'tp'), may hold values from -0.21875 to 0.21875
- attend_first: float32 [3, 768, 768], P(None, ('fsdp', 'ctx'), 'tp')
- attend_second: float32 [3, 768, 768], P(None, ('fsdp', 'ctx'), 'tp'), may hold values from 2080 to 33280
- merge_weight: float32 [768, 768], P('tp', ('fsdp', 'ctx')), may hold values from -0.875 to 0.875
- merge_first: float32 [768, 768], P('tp', ('fsdp', 'ctx'))
- merge_second: float32 [768, 768], P('tp', ('fsdp', 'ctx')), may hold values from 520 to 8320
- expand_weight: float32 [2, 768, 2048], P(None, ('fsdp', 'ctx'), 'tp'), may hold values from -0.21875 to 0.21875
- expand_first: float32 [2, 768, 2048], P(None, ('fsdp', 'ctx'), 'tp')
- expand_second: float32 [2, 768, 2048], P(None, ('fsdp', 'ctx'), 'tp'), may hold values from 2080 to 33280
- shrink_weight: float32 [2048, 768], P('tp', ('fsdp', 'ctx')), may hold values from -0.125 to 0.125
- shrink_first: float32 [2048, 768], P('tp', ('fsdp', 'ctx'))
- shrink_second: float32 [2048, 768], P('tp', ('fsdp', 'ctx')), may hold values from 8320 to 133120
Outputs:
- block_output: bfloat16 [16, 1040, 768], P('fsdp', ('ctx', 'tp'))
- token_gradient: float32 [16, 1040, 768], P('fsdp', ('ctx', 'tp'))
- attend_updated: float32 [3, 768, 768], P(None, ('fsdp', 'ctx'), 'tp')
- attend_moment: float32 [3, 768, 768], P(None, ('fsdp', 'ctx'), 'tp')
- attend_square: float32 [3, 768, 768], P(None, ('fsdp', 'ctx'), 'tp')
- merge_updated: float32 [768, 768], P('tp', ('fsdp', 'ctx'))
- merge_moment: float32 [768, 768], P('tp', ('fsdp', 'ctx'))
- merge_square: float32 [768, 768], P('tp', ('fsdp', 'ctx'))
- expand_updated: float32 [2, 768, 2048], P(None, ('fsdp', 'ctx'), 'tp')
- expand_moment: float32 [2, 768, 2048], P(None, ('fsdp', 'ctx'), 'tp')
- expand_square: float32 [2, 768, 2048], P(None, ('fsdp', 'ctx'), 'tp')
- shrink_updated: float32 [2048, 768], P('tp', ('fsdp', 'ctx'))
- shrink_moment: float32 [2048, 768], P('tp', ('fsdp', 'ctx'))
- shrink_square: float32 [2048, 768], P('tp', ('fsdp', 'ctx'))
- layer_updated: float32 [4, 768], replicated
- layer_moment: float32 [4, 768], replicated
- layer_square: float32 [4, 768], replicated
- inner_updated: float32 [2, 2048], P(None, 'tp')
- inner_moment: float32 [2, 2048], P(None, 'tp')
- inner_square: float32 [2, 2048], P(None, 'tp')
- trust_norms: float32 [4, 2], replicated
The draws below stay inside these ranges and needn't reach their ends.
Inputs may be any that keep to these rules, and one draw needn't show every extreme that they name: `layer_gains`: gains rise along the width; biases of order 0.3. `inner_gains`: gains rise along the width; biases of order 0.3.
All inputs are finite; a program needn't handle non-finite values.
Results may differ from the reference program's by a relative error of at most 0.012.
Values may be sent and summed in bfloat16 or wider, within the bound.
A program may use at most 192 MiB of HBM per device.

```python
import math
import jax
import jax.numpy as jnp
from jax import lax

D = 768
HEADS = 12
HD = 64
FF = 2048
GRID = 32
STEP = 5
VALID = 1025
SEQ = 1040
IMAGES = 16
TOKENS = 16640


def moment_draw(key, shape, factor):
    spread = factor * math.sqrt(TOKENS)
    return jax.random.uniform(key, shape, jnp.float32, -1.7, 1.7) * spread


def gains_draw(key, width):
    key_gain, key_shift = jax.random.split(key)
    ramp = 0.5 + jnp.arange(width, dtype=jnp.float32) / width
    gains = jax.random.uniform(key_gain, (2, width), jnp.float32, 0.8, 1.2) * ramp
    shifts = jax.random.uniform(key_shift, (2, width), jnp.float32, -0.5, 0.5)
    return (gains, shifts)


def draw_layer_gains(key, part):
    key = jax.random.fold_in(key, 11)
    gains, shifts = gains_draw(key, D)
    return jnp.stack([gains[0], shifts[0], gains[1], shifts[1]])


def draw_inner_gains(key, part):
    key = jax.random.fold_in(key, 12)
    gains, shifts = gains_draw(key, FF)
    return jnp.stack([gains[0], shifts[0]])


def draw_layer_first(key, part):
    key = jax.random.fold_in(key, 13)
    return moment_draw(key, (4, D), 1.0)


def draw_inner_first(key, part):
    key = jax.random.fold_in(key, 14)
    return moment_draw(key, (2, FF), 0.5)


def draw_attend_first(key, part):
    key = jax.random.fold_in(key, 15)
    return moment_draw(key, (3, D, D), 0.5)


def draw_merge_first(key, part):
    key = jax.random.fold_in(key, 16)
    return moment_draw(key, (D, D), 0.25)


def draw_expand_first(key, part):
    key = jax.random.fold_in(key, 17)
    return moment_draw(key, (2, D, FF), 0.5)


def draw_shrink_first(key, part):
    key = jax.random.fold_in(key, 18)
    return moment_draw(key, (FF, D), 1.0)


def steps_of(stream_key, extent, cuts, smallest, high):
    def one(position, blocks):
        heights = jax.random.uniform(jax.random.fold_in(jax.random.fold_in(stream_key, 6), position), (blocks,), jnp.float32, smallest / len(cuts), high / len(cuts))
        return jnp.repeat(jnp.exp(heights), extent[position] // blocks).reshape((-1,) + (1,) * (len(extent) - position - 1))

    level = one(*cuts[0])
    for cut in cuts[1:]:
        level = level * one(*cut)
    return level


def centred(key, shape, scale, reach, cuts=(), held_as=jnp.bfloat16):
    array = scale * jax.random.normal(key, shape, jnp.float32)
    if cuts:
        array = array * steps_of(key, shape, cuts, -0.22, 0.18)
    return jnp.clip(array, -reach, reach).astype(held_as)


def setup_inputs(seed: int = 0) -> dict:
    key_of = jax.random.split(jax.random.key(seed), 21)
    tokens = centred(key_of[0], (IMAGES, SEQ, D), 1.0, 6.0, ((0, 2), (1, 16)))
    cotangent = centred(key_of[1], (IMAGES, SEQ, D), 1.0, 6.0, ((0, 2), (1, 16)))
    layer_gains = draw_layer_gains(jax.random.fold_in(key_of[20], 71), 0)
    layer_first = draw_layer_first(jax.random.fold_in(key_of[20], 71), 0)
    layer_second = jnp.clip(jnp.exp(jax.random.uniform(key_of[4], (4, D), jnp.float32, math.log(8320.0), math.log(133120.0))), 8320.0, 133120.0)
    inner_gains = draw_inner_gains(jax.random.fold_in(key_of[20], 71), 0)
    inner_first = draw_inner_first(jax.random.fold_in(key_of[20], 71), 0)
    inner_second = jnp.clip(jnp.exp(math.log(33280.0) - 2.7725887 * jax.random.uniform(key_of[7], (2, FF), jnp.float32) ** steps_of(key_of[7], (2, FF), ((1, 4),), -0.2, 0.2)), 2080.0, 33280.0)
    attend_weight = centred(key_of[8], (3, D, D), D ** -0.5, 0.21875, ((1, 8), (2, 4)), jnp.float32)
    attend_first = draw_attend_first(jax.random.fold_in(key_of[20], 71), 0)
    attend_second = jnp.clip(jnp.exp(math.log(33280.0) - 2.7725887 * jax.random.uniform(key_of[10], (3, D, D), jnp.float32) ** steps_of(key_of[10], (3, D, D), ((1, 8), (2, 4)), -0.2, 0.2)), 2080.0, 33280.0)
    merge_weight = centred(key_of[11], (D, D), (D // 16) ** -0.5, 0.875, ((0, 4), (1, 8)), jnp.float32)
    merge_first = draw_merge_first(jax.random.fold_in(key_of[20], 71), 0)
    merge_second = jnp.clip(jnp.exp(math.log(8320.0) - 2.7725887 * jax.random.uniform(key_of[13], (D, D), jnp.float32) ** steps_of(key_of[13], (D, D), ((0, 4), (1, 8)), -0.2, 0.2)), 520.0, 8320.0)
    expand_weight = centred(key_of[14], (2, D, FF), D ** -0.5, 0.21875, ((1, 8), (2, 4)), jnp.float32)
    expand_first = draw_expand_first(jax.random.fold_in(key_of[20], 71), 0)
    expand_second = jnp.clip(jnp.exp(math.log(33280.0) - 2.7725887 * jax.random.uniform(key_of[16], (2, D, FF), jnp.float32) ** steps_of(key_of[16], (2, D, FF), ((1, 8), (2, 4)), -0.2, 0.2)), 2080.0, 33280.0)
    shrink_weight = centred(key_of[17], (FF, D), FF ** -0.5, 0.125, ((0, 4), (1, 8)), jnp.float32)
    shrink_first = draw_shrink_first(jax.random.fold_in(key_of[20], 71), 0)
    shrink_second = jnp.clip(jnp.exp(math.log(133120.0) - 2.7725887 * jax.random.uniform(key_of[19], (FF, D), jnp.float32) ** steps_of(key_of[19], (FF, D), ((0, 4), (1, 8)), -0.2, 0.2)), 8320.0, 133120.0)
    return {"tokens": tokens, "cotangent": cotangent, "layer_gains": layer_gains, "layer_first": layer_first, "layer_second": layer_second, "inner_gains": inner_gains, "inner_first": inner_first, "inner_second": inner_second, "attend_weight": attend_weight, "attend_first": attend_first, "attend_second": attend_second, "merge_weight": merge_weight, "merge_first": merge_first, "merge_second": merge_second, "expand_weight": expand_weight, "expand_first": expand_first, "expand_second": expand_second, "shrink_weight": shrink_weight, "shrink_first": shrink_first, "shrink_second": shrink_second}


EPS_NORM = 1e-06
BETA_ONE = 0.5
BETA_TWO = 0.5
EPS_ADAM = 1e-06
DECAY = 0.01
RATE = 0.5
RATE_GAINS = 0.3
HIGHEST = lax.Precision.HIGHEST

@jax.custom_vjp
def low(v):
    return lax.optimization_barrier(v.astype(jnp.bfloat16)).astype(jnp.float32)

@jax.custom_vjp
def low_back(v):
    return v

def low_keep(v):
    return (low(v), None)

def low_pass(kept, grad):
    return (grad,)

def back_keep(v):
    return (v, None)

def back_low(kept, grad):
    return (low(grad),)
low.defvjp(low_keep, low_pass)
low_back.defvjp(back_keep, back_low)

def layer_norm(values, gain, shift):
    average = lax.optimization_barrier(jnp.mean(values, axis=-1, keepdims=True))
    variance = lax.optimization_barrier(jnp.mean(values * values, axis=-1, keepdims=True)) - average * average
    return (values - average) * lax.rsqrt(variance + EPS_NORM) * gain + shift

def rotary_tables(positions):
    inside = (positions >= 1) & (positions <= GRID * GRID)
    patch_index = jnp.where(inside, positions - 1, 0)
    row_place = (patch_index // GRID).astype(jnp.float32)
    column_place = (patch_index % GRID).astype(jnp.float32)
    quarter = HD // 4
    frequency = 10000.0 ** (-jnp.arange(quarter, dtype=jnp.float32) / quarter)
    row_angle = row_place[:, None] * frequency
    column_angle = column_place[:, None] * frequency
    angles = jnp.concatenate([row_angle, row_angle, column_angle, column_angle], axis=-1)
    return (jnp.cos(angles), jnp.sin(angles))

def rotate(values):
    quarters = jnp.split(values, 4, axis=-1)
    return jnp.concatenate([-quarters[1], quarters[0], -quarters[3], quarters[2]], axis=-1)

def rotary(values, cosine, sine):
    return values * cosine + rotate(values) * sine

def attention(query, keys_all, values_all):
    score_scale = HD ** (-0.5)
    scores = low_back(jnp.einsum('bqhd,bkhd->bhqk', query, keys_all, precision=HIGHEST) * score_scale)
    key_valid = jnp.arange(SEQ, dtype=jnp.int32) < VALID
    scores = jnp.where(key_valid, scores, -1e+30)
    softmax_out = jax.nn.softmax(scores, axis=-1)
    return jnp.einsum('bhqk,bkhd->bqhd', low(softmax_out), values_all, precision=HIGHEST)

def forward(tokens, layer_gains, inner_gains, attend_weight, merge_weight, expand_weight, shrink_weight):
    images = tokens.shape[0]
    normed_one = low(layer_norm(tokens, layer_gains[0], layer_gains[1]))
    projected = low_back(jnp.einsum('bsd,tdc->tbsc', normed_one, low(attend_weight), precision=HIGHEST))
    projected = projected.reshape(3, images, SEQ, HEADS, HD)
    cosine, sine = rotary_tables(jnp.arange(SEQ, dtype=jnp.int32))
    cosine = cosine[:, None, :]
    sine = sine[:, None, :]
    query = low(rotary(projected[0], cosine, sine))
    keys_all = low(rotary(projected[1], cosine, sine))
    values_all = low(projected[2])
    attended = jax.checkpoint(attention)(query, keys_all, values_all)
    attended = low(low_back(attended)).reshape(images, SEQ, D)
    branch_one = low_back(jnp.einsum('bsc,cd->bsd', attended, low(merge_weight), precision=HIGHEST))
    middle = tokens + branch_one
    normed_two = low(layer_norm(middle, layer_gains[2], layer_gains[3]))
    gate_up = low_back(jnp.einsum('bsd,tdh->tbsh', normed_two, low(expand_weight), precision=HIGHEST))
    activated = jax.nn.silu(gate_up[0]) * gate_up[1]
    hidden = low(layer_norm(activated, inner_gains[0], inner_gains[1]))
    branch_two = low_back(jnp.einsum('bsh,hd->bsd', hidden, low(shrink_weight), precision=HIGHEST))
    return middle + branch_two

def moments(gradient, moment, square):
    moment = BETA_ONE * moment + (1.0 - BETA_ONE) * gradient
    square = BETA_TWO * square + (1.0 - BETA_TWO) * gradient * gradient
    update = moment / (1.0 - BETA_ONE ** STEP) / (jnp.sqrt(square / (1.0 - BETA_TWO ** STEP)) + EPS_ADAM)
    return (moment, square, update)

def reference(tokens, cotangent, layer_gains, layer_first, layer_second, inner_gains, inner_first, inner_second, attend_weight, attend_first, attend_second, merge_weight, merge_first, merge_second, expand_weight, expand_first, expand_second, shrink_weight, shrink_first, shrink_second):
    group = 4
    blocks = IMAGES // group
    params = (layer_gains, inner_gains, attend_weight, merge_weight, expand_weight, shrink_weight)
    token_blocks = tokens.astype(jnp.float32).reshape(blocks, group, SEQ, D)
    cotangent_blocks = cotangent.astype(jnp.float32).reshape(blocks, group, SEQ, D)

    def advance(running, pieces):
        block_tokens, block_cotangent = pieces
        result, pullback = jax.vjp(forward, block_tokens, *params)
        gradients = pullback(block_cotangent)
        running = tuple((total + gradient for total, gradient in zip(running, gradients[1:])))
        return (running, (result.astype(jnp.bfloat16), gradients[0]))
    initial = tuple((jnp.zeros_like(parameter) for parameter in params))
    summed, (outputs, token_grads) = lax.scan(advance, initial, (token_blocks, cotangent_blocks))
    block_output = outputs.reshape(IMAGES, SEQ, D)
    token_gradient = token_grads.reshape(IMAGES, SEQ, D)
    layer_grad, inner_grad, attend_grad, merge_grad, expand_grad, shrink_grad = summed
    matrices = ((attend_weight, attend_grad, attend_first, attend_second), (merge_weight, merge_grad, merge_first, merge_second), (expand_weight, expand_grad, expand_first, expand_second), (shrink_weight, shrink_grad, shrink_first, shrink_second))
    results = []
    norm_rows = []
    for weight, gradient, moment, square in matrices:
        moment_new, square_new, update = moments(gradient, moment, square)
        update = update + DECAY * weight
        weight_norm = jnp.sqrt(jnp.sum(weight * weight))
        update_norm = jnp.sqrt(jnp.sum(update * update))
        results.append((weight - RATE * (weight_norm / update_norm) * update, moment_new, square_new))
        norm_rows.append(jnp.stack([weight_norm, update_norm]))
    layer_moment, layer_square, layer_step = moments(layer_grad, layer_first, layer_second)
    inner_moment, inner_square, inner_step = moments(inner_grad, inner_first, inner_second)
    trust_norms = jnp.stack(norm_rows)
    return (block_output, token_gradient, results[0][0], results[0][1], results[0][2], results[1][0], results[1][1], results[1][2], results[2][0], results[2][1], results[2][2], results[3][0], results[3][1], results[3][2], layer_gains - RATE_GAINS * layer_step, layer_moment, layer_square, inner_gains - RATE_GAINS * inner_step, inner_moment, inner_square, trust_norms)
```

```python
import functools
import jax
import jax.numpy as jnp
from jax import lax
from jax.experimental import pallas as pl
from jax.experimental.pallas import tpu as pltpu
from jax.sharding import PartitionSpec as P

HD = 64
GRID = 32
STEP = 5
VALID = 1025
BETA_ONE = 0.5
BETA_TWO = 0.5
EPS_ADAM = 1e-06
DECAY = 0.01
RATE = 0.5
RATE_GAINS = 0.3
MESH = pl.DeviceIdType.MESH
f32 = jnp.float32
bf = jnp.bfloat16


class Place:
    def __init__(self, F, C, T):
        self.F, self.C, self.T = F, C, T
        self.f = lax.axis_index("fsdp"); self.c = lax.axis_index("ctx"); self.t = lax.axis_index("tp")
        self.low = lax.rem(self.t, 2)
        self.high = lax.div(self.t, 2)
        self.pair = self.c * (T // 2) + self.high
        self.pairs = C * (T // 2)
    def sibling(self):
        return {"tp": self.t + 1 - 2 * self.low}
    def x(self, k):
        return lax.rem(self.f + k, self.F)
    def z(self, k):
        return lax.rem(self.c + k, self.C)
    def y(self, k):
        return lax.rem(self.high + k, self.T // 2)
    def at_x(self, k): return {"fsdp": self.x(k)}
    def at_z(self, k): return {"ctx": self.z(k)}
    def at_y(self, k): return {"tp": self.y(k) * 2 + self.low}
    def pair_at(self, k):
        i = lax.rem(self.pair + k, self.pairs)
        return i, {"ctx": lax.div(i, self.T // 2), "tp": lax.rem(i, self.T // 2) * 2 + self.low}


def greet(pl_, partners):
    b = pltpu.get_barrier_semaphore()
    for p in partners:
        pl.semaphore_signal(b, inc=1, device_id=p, device_id_type=MESH)
    pl.semaphore_wait(b, len(partners))


class Sems:
    def __init__(self, send, recv):
        self.send, self.recv, self.n = send, recv, 0
    def remote(self, src, dst, dev):
        i = self.n; self.n += 1
        return pltpu.make_async_remote_copy(src, dst, self.send.at[i], self.recv.at[i], device_id=dev, device_id_type=MESH)
    def local(self, src, dst):
        i = self.n; self.n += 1
        return pltpu.make_async_copy(src, dst, self.send.at[i])


def send_chunks(P, S, src, dst):
    own = S.local(src.at[P.pair], dst.at[P.pair]); own.start()
    out = []
    for k in range(1, P.pairs):
        i, dev = P.pair_at(k)
        cp = S.remote(src.at[i], dst.at[P.pair], dev); cp.start()
        out.append(cp)
    return own, out


class Gather:
    def __init__(self, P, S, w_ref, W, cols, first):
        self.P, self.S, self.W, self.first = P, S, W, first
        self.cols = pl.ds(*cols)
        self.R = w_ref.shape[0]
        self.w = w_ref
        self.open = []
    def blk(self, t, row0, rows):
        return self.W.at[t, pl.ds(pl.multiple_of(row0, 16), rows), self.cols]
    def push(self, t, row0, rows, dev):
        b = self.blk(t, row0, rows)
        cp = self.S.remote(b, b, dev); cp.start(); self.open.append(cp)
        return cp
    def own(self):
        P, R = self.P, self.R
        self.row = (P.f * P.C + P.c) * R
        cp = self.S.local(self.w.at[:, self.cols], self.blk(P.t, self.row, R)); cp.start()
        self.mine = cp
    def stage_z(self):
        P, R = self.P, self.R
        self.mine.wait()
        self.zs = [self.push(P.t, self.row, R, P.at_z(k)) for k in range(1, P.C)]
    def stage_2(self):
        P, R = self.P, self.R
        for cp in self.zs: cp.wait_recv()
        n = P.C * R
        row = P.f * n
        if self.first == "y":
            self.s2 = [self.push(P.t, row, n, P.at_y(k)) for k in range(1, P.T // 2)]
        else:
            self.s2 = [self.push(P.t, row, n, P.at_x(k)) for k in range(1, P.F)]
        self.sib = [self.push(P.t, row, n, P.sibling())]
    def stage_3(self):
        P, R = self.P, self.R
        for cp in self.s2: cp.wait_recv()
        n = P.C * R
        self.s3 = []
        if self.first == "y":
            row = P.f * n
            for k in range(1, P.F):
                for a in range(P.T // 2):
                    self.s3.append(self.push(P.y(a) * 2 + P.low, row, n, P.at_x(k)))
            for a in range(1, P.T // 2):
                self.sib.append(self.push(P.y(a) * 2 + P.low, row, n, P.sibling()))
        else:
            for k in range(1, P.T // 2):
                self.s3.append(self.push(P.t, 0, n * P.F, P.at_y(k)))
            for k in range(1, P.F):
                self.sib.append(self.push(P.t, P.x(k) * n, n, P.sibling()))
    def stage_4(self):
        P, R = self.P, self.R
        for cp in self.s3: cp.wait_recv()
        n = P.C * R
        if self.first == "y":
            for k in range(1, P.F):
                for a in range(P.T // 2):
                    self.sib.append(self.push(P.y(a) * 2 + P.low, P.x(k) * n, n, P.sibling()))
        else:
            for k in range(1, P.T // 2):
                self.sib.append(self.push(P.y(k) * 2 + P.low, 0, n * P.F, P.sibling()))
    def finish(self):
        for cp in self.sib: cp.wait_recv()
        for cp in self.open: cp.wait_send()


def rows_loop(rows, step, body):
    if rows <= step:
        body(0, rows); return
    assert rows % step == 0
    def it(i, _):
        body(pl.multiple_of(i * step, step), step)
        return 0
    lax.fori_loop(0, rows // step, it, 0)


class Reduce:
    def __init__(self, P, S, G, cols, first, RC, W1, R1, W2, R2, R3, out, out_col, R):
        self.P, self.S, self.G, self.first = P, S, G, first
        self.cols = pl.ds(*cols); self.n = cols[1]
        self.RC, self.W1, self.R1, self.W2, self.R2, self.R3, self.out = RC, W1, R1, W2, R2, R3, out
        self.oc = pl.ds(out_col, self.n); self.R = R
        self.open = []
    def remote(self, src, dst, dev):
        cp = self.S.remote(src, dst, dev); cp.start(); self.open.append(cp); return cp
    def stage_c(self):
        P = self.P; H = P.T // 2
        self.c = [self.remote(self.G.at[2 * a + 1 - P.low, :, self.cols], self.RC.at[a], P.sibling()) for a in range(H)]
    def stage_1(self):
        P = self.P; H = P.T // 2; rows = self.RC.shape[1]; n = P.C * self.R
        for a in range(H):
            self.c[a].wait_recv()
            def add(r, k, a=a):
                s = pl.ds(r, k)
                self.W1[a, s, :] = (self.G[2 * a + P.low, s, self.cols].astype(jnp.float32) + self.RC[a, s, :].astype(jnp.float32)).astype(jnp.bfloat16)
            rows_loop(rows, 96, add)
        self.s1 = []
        if self.first == "x":
            for k in range(1, P.F):
                for a in range(H):
                    self.s1.append(self.remote(self.W1.at[a, pl.ds(pl.multiple_of(P.x(k) * n, 16), n)], self.R1.at[k - 1, a], P.at_x(k)))
        else:
            for k in range(1, H):
                self.s1.append(self.remote(self.W1.at[P.y(k)], self.R1.at[k - 1], P.at_y(k)))
    def stage_2(self):
        P = self.P; H = P.T // 2; rows = self.RC.shape[1]; n = P.C * self.R
        for cp in self.s1: cp.wait_recv()
        self.s2 = []
        if self.first == "x":
            base = P.f * n
            for a in range(H):
                def add(r, k, a=a):
                    s = pl.ds(r, k)
                    v = self.W1[a, pl.ds(pl.multiple_of(base + r, 16), k), :].astype(jnp.float32)
                    for j in range(P.F - 1): v = v + self.R1[j, a, s, :].astype(jnp.float32)
                    self.W2[a, s, :] = v.astype(jnp.bfloat16)
                rows_loop(n, 96, add)
            for k in range(1, H):
                self.s2.append(self.remote(self.W2.at[P.y(k)], self.R2.at[k - 1], P.at_y(k)))
        else:
            def add(r, k):
                s = pl.ds(r, k)
                v = self.W1[P.high, s, :].astype(jnp.float32)
                for j in range(H - 1): v = v + self.R1[j, s, :].astype(jnp.float32)
                self.W2[s, :] = v.astype(jnp.bfloat16)
            rows_loop(rows, 96, add)
            for k in range(1, P.F):
                self.s2.append(self.remote(self.W2.at[pl.ds(pl.multiple_of(P.x(k) * n, 16), n)], self.R2.at[k - 1], P.at_x(k)))
    def stage_3(self):
        P = self.P; H = P.T // 2; R = self.R; n = P.C * R
        for cp in self.s2: cp.wait_recv()
        count = (H if self.first == "x" else P.F) - 1
        def add(r, k):
            s = pl.ds(r, k)
            if self.first == "x":
                v = self.W2[P.high, s, :].astype(jnp.float32)
            else:
                v = self.W2[pl.ds(pl.multiple_of(P.f * n + r, 16), k), :].astype(jnp.float32)
            for j in range(count): v = v + self.R2[j, s, :].astype(jnp.float32)
            self.W1[0, s, :] = v.astype(jnp.bfloat16)
        if self.first == "x":
            for cp in self.s1: cp.wait_send()
        else:
            for cp in self.s1: cp.wait_send()
        rows_loop(n, 96, add)
        self.s3 = []
        for k in range(1, P.C):
            self.s3.append(self.remote(self.W1.at[0, pl.ds(pl.multiple_of(P.z(k) * R, 16), R)], self.R3.at[k - 1], P.at_z(k)))
    def stage_4(self):
        P = self.P; R = self.R
        for cp in self.s3: cp.wait_recv()
        v = self.W1[0, pl.ds(pl.multiple_of(P.c * R, 16), R), :].astype(jnp.float32)
        for j in range(P.C - 1): v = v + self.R3[j].astype(jnp.float32)
        self.out[:, self.oc] = v
    def finish(self):
        for cp in self.open:
            if not any(cp is s for s in self.s1): cp.wait_send()
EPS=1e-6
def dot(a,b): return jnp.dot(a,b,preferred_element_type=f32)
def dot_t(a,b): return lax.dot_general(a,b,(((1,),(1,)),((),())),preferred_element_type=f32)
def dot_l(a,b): return lax.dot_general(a,b,(((0,),(0,)),((),())),preferred_element_type=f32)

def chunks(rows, step, body):
    def it(i,_):
        body(pl.ds(pl.multiple_of(i*step,step),step)); return 0
    lax.fori_loop(0,rows//step,it,0)

def norm(v):
    mean=jnp.mean(v,axis=-1,keepdims=True)
    var=jnp.mean(v*v,axis=-1,keepdims=True)-mean*mean
    inv=lax.rsqrt(var+EPS)
    return (v-mean)*inv, inv

def spread(src3, dst):
    J,r,D=src3.shape
    n=dst.shape[0]
    pad=n-J*r
    if pad: dst[n-16:n,:]=jnp.zeros((16,D),f32)
    for j in range(J):
        dst[j*r:(j+1)*r,:]=src3[j].astype(f32)

def join(WA, g, dst, T):
    w=WA.shape[2]//4
    def it(i,_):
        s=pl.ds(pl.multiple_of(i*96,96),96)
        row=jnp.concatenate([WA[t,s,g*w:(g+1)*w] for t in range(T)],axis=1)
        dst[s,:]=row
        return 0
    lax.fori_loop(0,WA.shape[1]//96,it,0)

def part(src, GA, g, T):
    w=GA.shape[2]//4
    def it(i,_):
        s=pl.ds(pl.multiple_of(i*96,96),96)
        v=src[s,:]
        for t in range(T):
            GA[t,s,g*w:(g+1)*w]=v[:,t*w:(t+1)*w].astype(bf)
        return 0
    lax.fori_loop(0,GA.shape[1]//96,it,0)

def turn(v, cos, sa, sb):
    n=v.shape[1]
    out=[]
    for i in range(n//128):
        a=v[:,i*128:(i+1)*128]
        out.append(a*cos+pltpu.roll(a,128-16,1)*sa+pltpu.roll(a,16,1)*sb)
    return jnp.concatenate(out,axis=1)

def qkv(x, gains, Wq, Wk, Wv, cos, sa, sb, ln1, q, K, V):
    n=x.shape[0]
    def ln(s):
        v,_=norm(x[s,:])
        ln1[s,:]=(v*gains[0:1,:]+gains[1:2,:]).astype(bf)
    chunks(n,48,ln)
    for W,dst,kind in ((Wq,q,0),(Wk,K,1),(Wv,V,2)):
        y=dot(ln1[...],W[...])
        if kind==0: y=turn(y,cos[...],sa[...],sb[...])*0.125
        if kind==1: y=turn(y,cos[...],sa[...],sb[...])
        dst[0:n,:]=y.astype(bf)

def lanes(n, a):
    return (lax.broadcasted_iota(jnp.int32,(n,128),1)//64==a)

def attention(q,K,V,bias,E,linv,att, step=176):
    n=q.shape[0]; m=K.shape[0]
    def pair(p,_):
        c=pl.ds(pl.multiple_of(p*128,128),128)
        k2=K[:,c]; v2=V[:,c]
        ks=[jnp.where(lanes(m,a),k2,jnp.zeros_like(k2)) for a in (0,1)]
        vs=[jnp.where(lanes(m,a),v2,jnp.zeros_like(v2)) for a in (0,1)]
        def rows(i,_):
            s=pl.ds(pl.multiple_of(i*step,step),step)
            q2=q[s,c]
            o=None; li=[]
            for a in (0,1):
                S=dot_t(q2,ks[a])+bias[0:1,:]
                mx=jnp.max(S,axis=1,keepdims=True)
                e=jnp.exp(S-mx)
                l=1.0/jnp.sum(e,axis=1,keepdims=True)
                eb=e.astype(bf)
                E[2*p+a,s,:]=eb
                oa=dot(eb,vs[a])*l
                o=oa if o is None else o+oa
                li.append(l)
            att[s,c]=o.astype(bf)
            linv[s,c]=jnp.where(lanes(step,0),li[0],li[1])
            return 0
        lax.fori_loop(0,n//step,rows,0)
        return 0
    lax.fori_loop(0,q.shape[1]//128,pair,0)

def merge(att,Wm,x,mid,gains,ln2):
    mid[...]=x[...]+dot_t(att[...],Wm[...])
    def ln(s):
        v,_=norm(mid[s,:])
        ln2[s,:]=(v*gains[2:3,:]+gains[3:4,:]).astype(bf)
    chunks(x.shape[0],48,ln)

def silu_parts(g):
    s=jax.nn.sigmoid(g)
    return s, g*s

def ffn(ln2,ln2T,cot,cotT,WF,mid,ig,gate,up,act,gh,stat,GF,inner,out,gln2,T):
    n=ln2.shape[0]; Hd=WF.shape[2]//3; FFN=T*Hd
    def one(t,c):
        s0,s1=c
        gu=dot(ln2[...],WF[t,:,0:2*Hd])
        g=gu[:,:Hd]; u=gu[:,Hd:]
        _,si=silu_parts(g)
        a=si*u
        gate[t]=g; up[t]=u; act[t]=a
        return s0+jnp.sum(a,axis=1,keepdims=True), s1+jnp.sum(a*a,axis=1,keepdims=True)
    z=jnp.zeros((n,1),f32)
    s0,s1=lax.fori_loop(0,T,one,(z,z))
    mean=s0/FFN; inv=lax.rsqrt(s1/FFN-mean*mean+EPS)
    out[...]=mid[...]
    def two(t,c):
        r0,r1=c
        n3=(act[t]-mean)*inv
        act[t]=n3
        gt=ig[t,0:1,:]
        hid=(n3*gt+ig[t,1:2,:]).astype(bf)
        out[...]+=dot_t(hid,WF[t,:,2*Hd:3*Hd])
        h=dot(cot[...],WF[t,:,2*Hd:3*Hd])
        GF[t,:,2*Hd:3*Hd]=dot(cotT[...],hid).astype(bf)
        inner[t,0:1,:]=jnp.sum(h*n3,axis=0,keepdims=True)
        inner[t,1:2,:]=jnp.sum(h,axis=0,keepdims=True)
        e=h*gt
        gh[t]=e
        return r0+jnp.sum(e,axis=1,keepdims=True), r1+jnp.sum(e*n3,axis=1,keepdims=True)
    r0,r1=lax.fori_loop(0,T,two,(z,z))
    r0=r0/FFN; r1=r1/FFN
    gln2[...]=jnp.zeros_like(gln2)
    def three(t,_):
        ga=inv*(gh[t]-r0-act[t]*r1)
        g=gate[t]; u=up[t]
        s,si=silu_parts(g)
        gg=(ga*u*s*(1.0+g*(1.0-s))).astype(bf)
        gu=(ga*si).astype(bf)
        both=jnp.concatenate([gg,gu],axis=1)
        GF[t,:,0:2*Hd]=dot(ln2T[...],both).astype(bf)
        gln2[...]+=dot_t(both,WF[t,:,0:2*Hd])
        return 0
    lax.fori_loop(0,T,three,0)

def norm_back(src, e_src, gain, add, dst, lay, row, dst16=None):
    n=src.shape[0]
    lay[row:row+2,:]=jnp.zeros((2,src.shape[1]),f32)
    def it(s):
        a,inv=norm(src[s,:]); e=e_src[s,:]
        lay[row:row+1,:]+=jnp.sum(e*a,axis=0,keepdims=True)
        lay[row+1:row+2,:]+=jnp.sum(e,axis=0,keepdims=True)
        eg=e*gain
        d=add[s,:]+inv*(eg-jnp.mean(eg,axis=1,keepdims=True)-a*jnp.mean(eg*a,axis=1,keepdims=True))
        dst[s,:]=d
        if dst16 is not None: dst16[s,:]=d.astype(bf)
    chunks(n,48,it)

def attention_back(q,K,V,E,linv,att,gatt,dq,dK,dV,step=528):
    n=q.shape[0]; m=K.shape[0]
    def pair(p,_):
        c=pl.ds(pl.multiple_of(p*128,128),128)
        k2=K[:,c]; v2=V[:,c]
        R=linv[:,c]
        do=gatt[:,c].astype(f32)*R
        dob=do.astype(bf)
        dl=dob.astype(f32)*att[:,c].astype(f32)
        q2=q[:,c]
        dqv=None; dkv=None; dvv=None
        for a in (0,1):
            ka=jnp.where(lanes(m,a),k2,jnp.zeros_like(k2))
            va=jnp.where(lanes(m,a),v2,jnp.zeros_like(v2))
            qa=jnp.where(lanes(n,a),q2,jnp.zeros_like(q2))
            da=jnp.where(lanes(n,a),dob,jnp.zeros_like(dob))
            delta=jnp.sum(jnp.where(lanes(n,a),dl,0.0),axis=1,keepdims=True)
            dP=dot_t(dob,va)
            e=E[2*p+a]
            dS=(e.astype(f32)*(dP-delta)).astype(bf)
            x=dot(dS,ka); y=dot_l(dS,qa); z=dot_l(e,da)
            dqv=x if dqv is None else dqv+x
            dkv=y if dkv is None else dkv+y
            dvv=z if dvv is None else dvv+z
        dq[:,c]=dqv*0.125
        dK[:,c]=dkv
        dV[:,c]=dvv
        return 0
    lax.fori_loop(0,q.shape[1]//128,pair,0)

VMEM = pl.BlockSpec(memory_space=pltpu.VMEM)
HBM = pl.BlockSpec(memory_space=pl.ANY)
LIMIT = 60 * 2**20


def local_call(body, ins, outs, scratch=(), flops=0):
    return pl.pallas_call(
        body,
        out_shape=[jax.ShapeDtypeStruct(s, d) for s, d in outs],
        in_specs=[VMEM] * len(ins),
        out_specs=[VMEM] * len(outs),
        scratch_shapes=[pltpu.VMEM(s, d) for s, d in scratch],
        compiler_params=pltpu.CompilerParams(vmem_limit_bytes=LIMIT),
    )(*ins)


def rotary_tables(slots, rows, total):
    quarter = HD // 4
    positions = (slots[:, None] * rows + jnp.arange(rows, dtype=jnp.int32)).reshape(-1)
    inside = (positions >= 1) & (positions <= GRID * GRID)
    patch = jnp.where(inside, positions - 1, 0)
    frequency = 10000.0 ** (-jnp.arange(quarter, dtype=jnp.float32) / quarter)
    row_angle = (patch // GRID).astype(jnp.float32)[:, None] * frequency
    column_angle = (patch % GRID).astype(jnp.float32)[:, None] * frequency
    angles = jnp.concatenate([row_angle, row_angle, column_angle, column_angle], axis=-1)
    angles = jnp.pad(angles, ((0, total - angles.shape[0]), (0, 0)))
    angles = jnp.concatenate([angles, angles], axis=-1)
    sine = jnp.sin(angles)
    first = (jnp.arange(2 * HD) // quarter) % 2 == 0
    return jnp.cos(angles), jnp.where(first, -sine, 0.0), jnp.where(first, 0.0, sine)


def key_bias(slots, rows, total):
    positions = (slots[:, None] * rows + jnp.arange(rows, dtype=jnp.int32)).reshape(-1)
    bias = jnp.where(positions < VALID, 0.0, -1e30).astype(jnp.float32)
    return jnp.pad(bias, (0, total - bias.shape[0]), constant_values=-1e30)


GATHER_PARTS = ((0, (0, 384), "y"), (0, (384, 384), "x"), (1, (0, 384), "y"), (1, (384, 384), "x"), (1, (768, 384), "y"), (1, (1152, 384), "x"))
REDUCE_PARTS = ((1, (0, 384), "x"), (1, (384, 384), "y"), (1, (768, 384), "x"), (1, (1152, 384), "y"), (0, (0, 384), "x"), (0, (384, 384), "y"))


def gather_kernel(F, C, T, weights, tok, cot, *refs):
    if weights:
        wa, wf, tin, cin, WA, WF, send, recv = refs
    else:
        tin, cin, send, recv = refs
    place = Place(F, C, T)
    S = Sems(send, recv)
    partners = [place.sibling()] + [place.pair_at(k)[1] for k in range(1, place.pairs)]
    if weights:
        partners += [place.at_x(k) for k in range(1, F)]
    greet(place, partners)
    waits = [send_chunks(place, S, tok, tin)]
    gathers = []
    if weights:
        for which, cols, first in GATHER_PARTS:
            gathers.append(Gather(place, S, (wa, wf)[which], (WA, WF)[which], cols, first))
            gathers[-1].own()
    for name in ("stage_z", "stage_2", "stage_3", "stage_4"):
        for g in gathers:
            getattr(g, name)()
    waits.append(send_chunks(place, S, cot, cin))
    for g in gathers:
        g.finish()
    for own, copies in waits:
        own.wait()
        for copy in copies:
            copy.wait()


def gather_call(F, C, T, tokens, cotangent, packs):
    weights = bool(packs)
    D = tokens.shape[-1]
    J = C * T // 2
    chunk = jax.ShapeDtypeStruct((J,) + tokens.shape[1:], jnp.bfloat16)
    outs = [chunk, chunk]
    if weights:
        outs += [jax.ShapeDtypeStruct((T, D, p.shape[1]), jnp.bfloat16) for p in packs]
    return pl.pallas_call(
        functools.partial(gather_kernel, F, C, T, weights),
        out_shape=outs,
        in_specs=[HBM] * (2 + len(packs)),
        out_specs=[HBM] * len(outs),
        scratch_shapes=[pltpu.SemaphoreType.DMA((128,)), pltpu.SemaphoreType.DMA((128,))],
        compiler_params=pltpu.CompilerParams(collective_id=1, has_side_effects=True),
    )(tokens, cotangent, *packs)


def reduce_kernel(F, C, T, R, weights, *refs):
    if weights:
        GA, GF, bo, tg, out, bo_out, tg_out, send, recv = refs[:9]
        scr = iter(refs[9:])
    else:
        bo, tg, bo_out, tg_out, send, recv = refs
    place = Place(F, C, T)
    S = Sems(send, recv)
    partners = [place.sibling()] + [place.pair_at(k)[1] for k in range(1, place.pairs)]
    if weights:
        partners += [place.at_x(k) for k in range(1, F)]
    greet(place, partners)
    parts = []
    if weights:
        for which, cols, first in REDUCE_PARTS:
            parts.append(
                Reduce(
                    place, S, (GA, GF)[which], cols, first, next(scr), next(scr), next(scr), next(scr), next(scr), next(scr),
                    out, cols[0] + which * GA.shape[2], R,
                )
            )
    names = ("stage_c", "stage_1", "stage_2", "stage_3", "stage_4", "finish")
    steps = sorted((2 * s + i // 2, i, s) for i in range(len(parts)) for s in range(6))
    for _, i, s in steps:
        getattr(parts[i], names[s])()
    waits = [send_chunks(place, S, bo, bo_out), send_chunks(place, S, tg, tg_out)]
    for own, copies in waits:
        own.wait()
        for copy in copies:
            copy.wait()


def reduce_call(F, C, T, R, grads, bo, tg):
    weights = bool(grads)
    H = T // 2
    scratch = [pltpu.SemaphoreType.DMA((128,)), pltpu.SemaphoreType.DMA((128,))]
    outs = []
    bufs = lambda *s: scratch.append(pltpu.VMEM(s, jnp.bfloat16))
    if weights:
        D = grads[0].shape[1]
        outs.append(jax.ShapeDtypeStruct((R, sum(g.shape[2] for g in grads)), jnp.float32))
        for _, (_, n), first in REDUCE_PARTS:
            bufs(H, D, n)
            bufs(H, D, n)
            if first == "x":
                bufs(F - 1, H, C * R, n)
                bufs(H, C * R, n)
                bufs(H - 1, C * R, n)
            else:
                bufs(H - 1, D, n)
                bufs(D, n)
                bufs(F - 1, C * R, n)
            bufs(C - 1, R, n)
    outs += [jax.ShapeDtypeStruct(bo.shape, bo.dtype)] * 2
    return pl.pallas_call(
        functools.partial(reduce_kernel, F, C, T, R, weights),
        out_shape=outs,
        in_specs=[VMEM] * len(grads) + [HBM] * 2,
        out_specs=[VMEM] * (1 if weights else 0) + [HBM] * 2,
        scratch_shapes=scratch,
        compiler_params=pltpu.CompilerParams(collective_id=2, has_side_effects=True, vmem_limit_bytes=LIMIT),
    )(*grads, bo, tg)


def project_kernel(T, tin, gains, WA, cos, sa, sb, x, ln1, q, K, V, Wq, Wk, Wv, Wm):
    spread(tin, x)
    for g, W in enumerate((Wq, Wk, Wv, Wm)):
        join(WA, g, W, T)
    qkv(x, gains, Wq, Wk, Wv, cos, sa, sb, ln1, q, K, V)


def attend_kernel(x, gains, q, K, V, bias, Wm, E, linv, att, mid, ln2):
    attention(q, K, V, bias, E, linv, att, q.shape[0])
    merge(att, Wm, x, mid, gains, ln2)


def ffn_kernel(T, cin, ln2, WF, mid, ig, gains, GF, inner, bo, gmid, gb, lay, cot, cotb, ln2T, cotT, gate, up, act, gh, out, gln2):
    spread(cin, cot)
    cotb[...] = cot[...].astype(jnp.bfloat16)
    cotT[...] = cot[...].T.astype(jnp.bfloat16)
    ln2T[...] = ln2[...].astype(jnp.float32).T.astype(jnp.bfloat16)
    ffn(ln2, ln2T, cotb, cotT, WF, mid, ig, gate, up, act, gh, None, GF, inner, out, gln2, T)
    J, r, _ = bo.shape
    for j in range(J):
        bo[j] = out[j * r : (j + 1) * r, :].astype(jnp.bfloat16)
    norm_back(mid, gln2, gains[2:3, :], cot, gmid, lay, 0, gb)


def attend_back_kernel(q, K, V, E, linv, att, gb, Wm, dq, dK, dV, Gm, gatt):
    gatt[...] = dot(gb[...], Wm[...]).astype(jnp.bfloat16)
    Gm[...] = dot_l(gb[...], att[...])
    attention_back(q, K, V, E, linv, att, gatt, dq, dK, dV)


def final_kernel(T, x, ln1, gains, gmid, dq, dK, dV, oK, oV, Gm, Wq, Wk, Wv, cos, sa, sb, GA, tg, lay, G, gln1, tok):
    n = x.shape[0]
    c, a, b = cos[...], -sa[...], -sb[...]
    for g, W in enumerate((Wq, Wk, Wv)):
        if g == 0:
            v = turn(dq[...], c, a, b)
        elif g == 1:
            v = turn(dK[...] + oK[...].astype(jnp.float32), c, a, b)
        else:
            v = dV[...] + oV[...].astype(jnp.float32)
        v = v.astype(jnp.bfloat16)
        G[...] = dot_l(ln1[...], v)
        part(G, GA, g, T)
        d = dot_t(v, W[...])
        gln1[...] = d if g == 0 else gln1[...] + d
    part(Gm, GA, 3, T)
    norm_back(x, gln1, gains[0:1, :], gmid, tok, lay, 0)
    J, r, _ = tg.shape
    for j in range(J):
        tg[j] = tok[j * r : (j + 1) * r, :].astype(jnp.bfloat16)


def moments(gradient, moment, square):
    moment = BETA_ONE * moment + (1.0 - BETA_ONE) * gradient
    square = BETA_TWO * square + (1.0 - BETA_TWO) * gradient * gradient
    update = (
        moment / (1.0 - BETA_ONE**STEP) / (jnp.sqrt(square / (1.0 - BETA_TWO**STEP)) + EPS_ADAM)
    )
    return (moment, square, update)


def body(
    F, C, T,
    tokens, cotangent, layer_gains, layer_first, layer_second, inner_gains, inner_first, inner_second,
    attend_weight, attend_first, attend_second, merge_weight, merge_first, merge_second,
    expand_weight, expand_first, expand_second, shrink_weight, shrink_first, shrink_second,
):
    bf, f32 = jnp.bfloat16, jnp.float32
    D = tokens.shape[-1]
    R = attend_weight.shape[1]
    rows = tokens.shape[1]
    J = C * T // 2
    assert J == tokens.shape[0]
    n = -(-J * rows // 48) * 48
    heads = attend_weight.shape[2]
    hidden = expand_weight.shape[2]
    fast = R % 16 == 0
    low = lax.axis_index("tp") % 2
    slots = jnp.arange(J, dtype=jnp.int32) * 2
    cos, sa, sb = rotary_tables(slots + low, rows, n)
    bias = jnp.concatenate([key_bias(slots + low, rows, n), key_bias(slots + 1 - low, rows, n)])[None]
    pack_a = jnp.concatenate([attend_weight[0], attend_weight[1], attend_weight[2], merge_weight.T], axis=1).astype(bf)
    pack_f = jnp.concatenate([expand_weight[0], expand_weight[1], shrink_weight.T], axis=1).astype(bf)
    if fast:
        tin, cin, WA, WF = gather_call(F, C, T, tokens, cotangent, [pack_a, pack_f])
    else:
        tin, cin = gather_call(F, C, T, tokens, cotangent, [])
        WA, WF = (
            lax.all_gather(lax.all_gather(p, ("fsdp", "ctx"), axis=0, tiled=True), "tp", axis=0)
            for p in (pack_a, pack_f)
        )
    inner_all = lax.all_gather(inner_gains, "tp", axis=0)
    x, ln1, q, K, V, Wq, Wk, Wv, Wm = local_call(
        functools.partial(project_kernel, T),
        [tin, layer_gains, WA, cos, sa, sb],
        [((n, D), f32)] + [((n, D), bf)] * 4 + [((D, D), bf)] * 4,
    )
    swap = [(t, t + 1 - 2 * (t % 2)) for t in range(T)]
    oK, oV = lax.ppermute((K, V), "tp", swap)
    K = jnp.concatenate([K, oK])
    V = jnp.concatenate([V, oV])
    nh = D // HD
    E, linv, att, mid, ln2 = local_call(
        attend_kernel,
        [x, layer_gains, q, K, V, bias, Wm],
        [((nh, n, 2 * n), bf), ((n, D), f32), ((n, D), bf), ((n, D), f32), ((n, D), bf)],
    )
    GF, inner, bo, gmid, gb, lay2 = local_call(
        functools.partial(ffn_kernel, T),
        [cin, ln2, WF, mid, inner_all, layer_gains],
        [((T, D, 3 * hidden), bf), ((T, 2, hidden), f32), (tokens.shape, bf), ((n, D), f32), ((n, D), bf), ((2, D), f32)],
        [((n, D), f32), ((n, D), bf), ((D, n), bf), ((D, n), bf)] + [((T, n, hidden), f32)] * 4 + [((n, D), f32)] * 2,
    )
    dq, dK, dV, Gm = local_call(
        attend_back_kernel,
        [q, K, V, E, linv, att, gb, Wm],
        [((n, D), f32), ((2 * n, D), f32), ((2 * n, D), f32), ((D, D), f32)],
        [((n, D), bf)],
    )
    oK, oV = lax.ppermute((dK[n:].astype(bf), dV[n:].astype(bf)), "tp", swap)
    GA, tg, lay1 = local_call(
        functools.partial(final_kernel, T),
        [x, ln1, layer_gains, gmid, dq, dK[:n], dV[:n], oK, oV, Gm, Wq, Wk, Wv, cos, sa, sb],
        [((T, D, 4 * heads), bf), (tokens.shape, bf), ((2, D), f32)],
        [((D, D), f32), ((n, D), f32), ((n, D), f32)],
    )
    if fast:
        sums, block_output, token_gradient = reduce_call(F, C, T, R, [GA, GF], bo, tg)
    else:
        block_output, token_gradient = reduce_call(F, C, T, R, [], bo, tg)
        sums = jnp.concatenate([GA, GF], axis=2).astype(f32)
        sums = lax.psum_scatter(sums, "tp", scatter_dimension=0, tiled=False)
        sums = lax.psum_scatter(sums, ("fsdp", "ctx"), scatter_dimension=0, tiled=True)
    token_gradient = token_gradient.astype(f32)
    a = sums[:, : 4 * heads]
    attend_sum = jnp.stack([a[:, i * heads : (i + 1) * heads] for i in range(3)])
    merge_sum = a[:, 3 * heads :].T
    b = sums[:, 4 * heads :]
    expand_sum = jnp.stack([b[:, i * hidden : (i + 1) * hidden] for i in range(2)])
    shrink_sum = b[:, 2 * hidden :].T
    layer_grad, inner_total = lax.psum((jnp.concatenate([lay1, lay2]), inner), ("fsdp", "ctx", "tp"))
    inner_grad = lax.dynamic_index_in_dim(inner_total, lax.axis_index("tp"), 0, keepdims=False)
    matrices = (
        (attend_weight, attend_sum, attend_first, attend_second),
        (merge_weight, merge_sum, merge_first, merge_second),
        (expand_weight, expand_sum, expand_first, expand_second),
        (shrink_weight, shrink_sum, shrink_first, shrink_second),
    )
    states = []
    weight_terms = []
    update_terms = []
    for weight, gradient, moment, square in matrices:
        moment_new, square_new, update = moments(gradient, moment, square)
        update = update + DECAY * weight
        states.append((moment_new, square_new, update))
        weight_terms.append(jnp.sum(weight * weight))
        update_terms.append(jnp.sum(update * update))
    weight_sums, update_sums = lax.psum(
        (jnp.stack(weight_terms), jnp.stack(update_terms)), ("fsdp", "ctx", "tp")
    )
    weight_norms = jnp.sqrt(weight_sums)
    update_norms = jnp.sqrt(update_sums)
    updated = []
    for number in range(4):
        ratio = weight_norms[number] / update_norms[number]
        updated.append(matrices[number][0] - RATE * ratio * states[number][2])
    layer_moment, layer_square, layer_step = moments(layer_grad, layer_first, layer_second)
    inner_moment, inner_square, inner_step = moments(inner_grad, inner_first, inner_second)
    trust_norms = jnp.stack([weight_norms, update_norms], axis=1)
    return (
        block_output, token_gradient,
        updated[0], states[0][0], states[0][1],
        updated[1], states[1][0], states[1][1],
        updated[2], states[2][0], states[2][1],
        updated[3], states[3][0], states[3][1],
        layer_gains - RATE_GAINS * layer_step, layer_moment, layer_square,
        inner_gains - RATE_GAINS * inner_step, inner_moment, inner_square,
        trust_norms,
    )


def solution(mesh):
    tok = P("fsdp", ("ctx", "tp"), None)
    wide = P(None, ("fsdp", "ctx"), "tp")
    tall = P("tp", ("fsdp", "ctx"))
    split = P(None, "tp")
    sizes = (mesh.shape["fsdp"], mesh.shape["ctx"], mesh.shape["tp"])
    return jax.shard_map(
        functools.partial(body, *sizes),
        mesh=mesh,
        in_specs=(tok, tok, P(), P(), P(), split, split, split)
        + (wide,) * 3 + (tall,) * 3 + (wide,) * 3 + (tall,) * 3,
        out_specs=(tok, tok) + (wide,) * 3 + (tall,) * 3 + (wide,) * 3 + (tall,) * 3
        + (P(),) * 3 + (split,) * 3 + (P(),),
        check_vma=False,
    )
```

```python
import functools
import jax
import jax.numpy as jnp
from jax import lax
from jax.experimental import pallas as pl
from jax.experimental.pallas import tpu as pltpu
from jax.sharding import PartitionSpec as P

HD = 64
GRID = 32
STEP = 5
VALID = 1025
BETA_ONE = 0.5
BETA_TWO = 0.5
EPS_ADAM = 1e-06
DECAY = 0.01
RATE = 0.5
RATE_GAINS = 0.3
MESH = pl.DeviceIdType.MESH
f32 = jnp.float32
bf = jnp.bfloat16


class Place:
    def __init__(self, F, C, T):
        self.F, self.C, self.T, self.H = F, C, T, T // 2
        self.f = lax.axis_index("fsdp")
        self.c = lax.axis_index("ctx")
        self.t = lax.axis_index("tp")
        self.low = lax.rem(self.t, 2)
        self.high = lax.div(self.t, 2)
        self.pair = self.c * self.H + self.high
        self.pairs = C * self.H
        self.sibling = {"tp": self.t + 1 - 2 * self.low}
        self.xs = [lax.rem(self.f + k, F) for k in range(F)]
        self.ys = [lax.rem(self.high + k, self.H) for k in range(self.H)]
        self.zs = [lax.rem(self.c + k, C) for k in range(C)]

    def at_x(self, k):
        return {"fsdp": self.xs[k]}

    def at_y(self, k):
        return {"tp": self.ys[k] * 2 + self.low}

    def at_z(self, k):
        return {"ctx": self.zs[k]}

    def pair_at(self, k):
        i = lax.rem(self.pair + k, self.pairs)
        return i, {"ctx": lax.div(i, self.H), "tp": lax.rem(i, self.H) * 2 + self.low}

    def partners(self, with_x):
        out = [self.sibling] + [self.pair_at(k)[1] for k in range(1, self.pairs)]
        if with_x:
            out += [self.at_x(k) for k in range(1, self.F)]
        return out


def hail(partners):
    barrier = pltpu.get_barrier_semaphore()
    for partner in partners:
        pl.semaphore_signal(barrier, inc=1, device_id=partner, device_id_type=MESH)


def heard(partners):
    pl.semaphore_wait(pltpu.get_barrier_semaphore(), len(partners))


class Sems:
    def __init__(self, send, recv):
        self.send, self.recv, self.n = send, recv, 0

    def remote(self, src, dst, device):
        i = self.n
        self.n += 1
        return pltpu.make_async_remote_copy(
            src, dst, self.send.at[i], self.recv.at[i], device_id=device, device_id_type=MESH
        )

    def local(self, src, dst):
        i = self.n
        self.n += 1
        return pltpu.make_async_copy(src, dst, self.send.at[i])


class Exchange:
    def __init__(self, place, sems, src, dst):
        self.own = sems.local(src.at[place.pair], dst.at[place.pair])
        self.copies = []
        for k in range(1, place.pairs):
            i, device = place.pair_at(k)
            self.copies.append(sems.remote(src.at[i], dst.at[place.pair], device))

    def start(self):
        self.own.start()
        for copy in self.copies:
            copy.start()

    def wait(self):
        self.own.wait()
        for copy in self.copies:
            copy.wait_recv()

    def finish(self):
        for copy in self.copies:
            copy.wait_send()


class Gather:
    def __init__(self, place, sems, pack, whole, cols, first):
        P, R = place, pack.shape[0]
        C, F, H = P.C, P.F, P.H
        n = C * R
        window = pl.ds(*cols)

        def push(t, row, rows, device):
            block = whole.at[t, pl.ds(pl.multiple_of(row, 16), rows), window]
            return sems.remote(block, block, device)

        row = (P.f * C + P.c) * R
        base = P.f * n
        self.own = sems.local(
            pack.at[:, window], whole.at[P.t, pl.ds(pl.multiple_of(row, 16), R), window]
        )
        along_z = [push(P.t, row, R, P.at_z(k)) for k in range(1, C)]
        tees = [y * 2 + P.low for y in P.ys]
        if first == "y":
            second = [push(P.t, base, n, P.at_y(k)) for k in range(1, H)]
            third = [push(t, base, n, P.at_x(k)) for k in range(1, F) for t in tees]
            over_3 = [push(t, base, n, P.sibling) for t in tees[1:]]
            over_4 = [push(t, P.xs[k] * n, n, P.sibling) for k in range(1, F) for t in tees]
        else:
            second = [push(P.t, base, n, P.at_x(k)) for k in range(1, F)]
            third = [push(P.t, 0, n * F, P.at_y(k)) for k in range(1, H)]
            over_3 = [push(P.t, P.xs[k] * n, n, P.sibling) for k in range(1, F)]
            over_4 = [push(t, 0, n * F, P.sibling) for t in tees[1:]]
        over_2 = [push(P.t, base, n, P.sibling)]
        self.waits = [[], along_z, second, third]
        self.starts = [along_z, second + over_2, third + over_3, over_4]
        self.sent_over = over_2 + over_3 + over_4

    def stage(self, s):
        if s == 0:
            self.own.wait()
        for copy in self.waits[s]:
            copy.wait_recv()
        for copy in self.starts[s]:
            copy.start()

    def finish(self):
        for copy in self.sent_over:
            copy.wait_recv()

    def settle(self):
        for group in self.starts:
            for copy in group:
                copy.wait_send()


def rows_loop(rows, step, body):
    if rows <= step:
        body(0, rows); return
    assert rows % step == 0
    def it(i, _):
        body(pl.multiple_of(i * step, step), step)
        return 0
    lax.fori_loop(0, rows // step, it, 0)


class Reduce:
    def __init__(self, P, S, G, cols, first, RC, W1, R1, W2, R2, R3, out, out_col, R):
        self.P, self.S, self.G, self.first = P, S, G, first
        self.cols = pl.ds(*cols); self.n = cols[1]
        self.RC, self.W1, self.R1, self.W2, self.R2, self.R3, self.out = RC, W1, R1, W2, R2, R3, out
        self.oc = pl.ds(out_col, self.n); self.R = R
        self.open = []
    def remote(self, src, dst, dev):
        cp = self.S.remote(src, dst, dev); cp.start(); self.open.append(cp); return cp
    def stage_c(self):
        P = self.P; H = P.T // 2
        self.c = [self.remote(self.G.at[2 * a + 1 - P.low, :, self.cols], self.RC.at[a], P.sibling) for a in range(H)]
    def stage_1(self):
        P = self.P; H = P.T // 2; rows = self.RC.shape[1]; n = P.C * self.R
        for a in range(H):
            self.c[a].wait_recv()
            def add(r, k, a=a):
                s = pl.ds(r, k)
                self.W1[a, s, :] = (self.G[2 * a + P.low, s, self.cols].astype(jnp.float32) + self.RC[a, s, :].astype(jnp.float32)).astype(jnp.bfloat16)
            rows_loop(rows, 96, add)
        self.s1 = []
        if self.first == "x":
            for k in range(1, P.F):
                for a in range(H):
                    self.s1.append(self.remote(self.W1.at[a, pl.ds(pl.multiple_of(P.xs[k] * n, 16), n)], self.R1.at[k - 1, a], P.at_x(k)))
        else:
            for k in range(1, H):
                self.s1.append(self.remote(self.W1.at[P.ys[k]], self.R1.at[k - 1], P.at_y(k)))
    def stage_2(self):
        P = self.P; H = P.T // 2; rows = self.RC.shape[1]; n = P.C * self.R
        for cp in self.s1: cp.wait_recv()
        self.s2 = []
        if self.first == "x":
            base = P.f * n
            for a in range(H):
                def add(r, k, a=a):
                    s = pl.ds(r, k)
                    v = self.W1[a, pl.ds(pl.multiple_of(base + r, 16), k), :].astype(jnp.float32)
                    for j in range(P.F - 1): v = v + self.R1[j, a, s, :].astype(jnp.float32)
                    self.W2[a, s, :] = v.astype(jnp.bfloat16)
                rows_loop(n, 96, add)
            for k in range(1, H):
                self.s2.append(self.remote(self.W2.at[P.ys[k]], self.R2.at[k - 1], P.at_y(k)))
        else:
            def add(r, k):
                s = pl.ds(r, k)
                v = self.W1[P.high, s, :].astype(jnp.float32)
                for j in range(H - 1): v = v + self.R1[j, s, :].astype(jnp.float32)
                self.W2[s, :] = v.astype(jnp.bfloat16)
            rows_loop(rows, 96, add)
            for k in range(1, P.F):
                self.s2.append(self.remote(self.W2.at[pl.ds(pl.multiple_of(P.xs[k] * n, 16), n)], self.R2.at[k - 1], P.at_x(k)))
    def stage_3(self):
        P = self.P; H = P.T // 2; R = self.R; n = P.C * R
        for cp in self.s2: cp.wait_recv()
        count = (H if self.first == "x" else P.F) - 1
        def add(r, k):
            s = pl.ds(r, k)
            if self.first == "x":
                v = self.W2[P.high, s, :].astype(jnp.float32)
            else:
                v = self.W2[pl.ds(pl.multiple_of(P.f * n + r, 16), k), :].astype(jnp.float32)
            for j in range(count): v = v + self.R2[j, s, :].astype(jnp.float32)
            self.W1[0, s, :] = v.astype(jnp.bfloat16)
        if self.first == "x":
            for cp in self.s1: cp.wait_send()
        else:
            for cp in self.s1: cp.wait_send()
        rows_loop(n, 96, add)
        self.s3 = []
        for k in range(1, P.C):
            self.s3.append(self.remote(self.W1.at[0, pl.ds(pl.multiple_of(P.zs[k] * R, 16), R)], self.R3.at[k - 1], P.at_z(k)))
    def stage_4(self):
        P = self.P; R = self.R
        for cp in self.s3: cp.wait_recv()
        v = self.W1[0, pl.ds(pl.multiple_of(P.c * R, 16), R), :].astype(jnp.float32)
        for j in range(P.C - 1): v = v + self.R3[j].astype(jnp.float32)
        self.out[:, self.oc] = v
    def finish(self):
        for cp in self.open:
            if not any(cp is s for s in self.s1): cp.wait_send()
EPS=1e-6
def dot(a,b): return jnp.dot(a,b,preferred_element_type=f32)
def dot_t(a,b): return lax.dot_general(a,b,(((1,),(1,)),((),())),preferred_element_type=f32)
def dot_l(a,b): return lax.dot_general(a,b,(((0,),(0,)),((),())),preferred_element_type=f32)

def chunks(rows, step, body):
    def it(i,_):
        body(pl.ds(pl.multiple_of(i*step,step),step)); return 0
    lax.fori_loop(0,rows//step,it,0)

def norm(v):
    mean=jnp.mean(v,axis=-1,keepdims=True)
    var=jnp.mean(v*v,axis=-1,keepdims=True)-mean*mean
    inv=lax.rsqrt(var+EPS)
    return (v-mean)*inv, inv

def spread(src3, dst):
    J,r,D=src3.shape
    n=dst.shape[0]
    pad=n-J*r
    if pad: dst[n-16:n,:]=jnp.zeros((16,D),f32)
    for j in range(J):
        dst[j*r:(j+1)*r,:]=src3[j].astype(f32)

def join(WA, g, dst, T):
    w=WA.shape[2]//4
    def it(i,_):
        s=pl.ds(pl.multiple_of(i*96,96),96)
        row=jnp.concatenate([WA[t,s,g*w:(g+1)*w] for t in range(T)],axis=1)
        dst[s,:]=row
        return 0
    lax.fori_loop(0,WA.shape[1]//96,it,0)

def part(src, GA, g, T):
    w=GA.shape[2]//4
    def it(i,_):
        s=pl.ds(pl.multiple_of(i*96,96),96)
        v=src[s,:]
        for t in range(T):
            GA[t,s,g*w:(g+1)*w]=v[:,t*w:(t+1)*w].astype(bf)
        return 0
    lax.fori_loop(0,GA.shape[1]//96,it,0)

def turn(v, cos, sa, sb):
    n=v.shape[1]
    out=[]
    for i in range(n//128):
        a=v[:,i*128:(i+1)*128]
        out.append(a*cos+pltpu.roll(a,128-16,1)*sa+pltpu.roll(a,16,1)*sb)
    return jnp.concatenate(out,axis=1)

def normal(x, gains, ln1):
    def ln(s):
        v,_=norm(x[s,:])
        ln1[s,:]=(v*gains[0:1,:]+gains[1:2,:]).astype(bf)
    chunks(x.shape[0],48,ln)


def project(ln1, W, cos, sa, sb, dst, scale=None):
    y=dot(ln1[...],W[...])
    if cos is not None: y=turn(y,cos[...],sa[...],sb[...])
    if scale is not None: y=y*scale
    dst[0:ln1.shape[0],:]=y.astype(bf)


def lanes(n, a):
    return (lax.broadcasted_iota(jnp.int32,(n,128),1)//64==a)

def attention(q,K,V,bias,E,linv,att,service):
    n=q.shape[0]; m=K.shape[0]
    def pair(p,_):
        service(p)
        c=pl.ds(pl.multiple_of(p*128,128),128)
        k2=K[:,c]; v2=V[:,c]
        q2=q[:,c]
        o=None; li=[]
        for a in (0,1):
            ka=jnp.where(lanes(m,a),k2,jnp.zeros_like(k2))
            va=jnp.where(lanes(m,a),v2,jnp.zeros_like(v2))
            S=dot_t(q2,ka)+bias[0:1,:]
            mx=jnp.max(S,axis=1,keepdims=True)
            e=jnp.exp(S-mx)
            l=1.0/jnp.sum(e,axis=1,keepdims=True)
            eb=e.astype(bf)
            E[2*p+a]=eb
            oa=dot(eb,va)*l
            o=oa if o is None else o+oa
            li.append(l)
        att[:,c]=o.astype(bf)
        linv[:,c]=jnp.where(lanes(n,0),li[0],li[1])
        return 0
    lax.fori_loop(0,q.shape[1]//128,pair,0)

def merge(att,Wm,x,mid,gains,ln2):
    mid[...]=x[...]+dot_t(att[...],Wm[...])
    def ln(s):
        v,_=norm(mid[s,:])
        ln2[s,:]=(v*gains[2:3,:]+gains[3:4,:]).astype(bf)
    chunks(x.shape[0],48,ln)

def silu_parts(g):
    s=jax.nn.sigmoid(g)
    return s, g*s

def ffn(ln2,ln2T,cot,cotT,WF,mid,ig,gate,up,act,gh,stat,GF,inner,out,gln2,T):
    n=ln2.shape[0]; Hd=WF.shape[2]//3; FFN=T*Hd
    def one(t,c):
        s0,s1=c
        gu=dot(ln2[...],WF[t,:,0:2*Hd])
        g=gu[:,:Hd]; u=gu[:,Hd:]
        _,si=silu_parts(g)
        a=si*u
        gate[t]=g; up[t]=u; act[t]=a
        return s0+jnp.sum(a,axis=1,keepdims=True), s1+jnp.sum(a*a,axis=1,keepdims=True)
    z=jnp.zeros((n,1),f32)
    s0,s1=lax.fori_loop(0,T,one,(z,z))
    mean=s0/FFN; inv=lax.rsqrt(s1/FFN-mean*mean+EPS)
    out[...]=mid[...]
    def two(t,c):
        r0,r1=c
        n3=(act[t]-mean)*inv
        act[t]=n3
        gt=ig[t,0:1,:]
        hid=(n3*gt+ig[t,1:2,:]).astype(bf)
        out[...]+=dot_t(hid,WF[t,:,2*Hd:3*Hd])
        h=dot(cot[...],WF[t,:,2*Hd:3*Hd])
        GF[t,:,2*Hd:3*Hd]=dot(cotT[...],hid).astype(bf)
        inner[t,0:1,:]=jnp.sum(h*n3,axis=0,keepdims=True)
        inner[t,1:2,:]=jnp.sum(h,axis=0,keepdims=True)
        e=h*gt
        gh[t]=e
        return r0+jnp.sum(e,axis=1,keepdims=True), r1+jnp.sum(e*n3,axis=1,keepdims=True)
    r0,r1=lax.fori_loop(0,T,two,(z,z))
    r0=r0/FFN; r1=r1/FFN
    gln2[...]=jnp.zeros_like(gln2)
    def three(t,_):
        ga=inv*(gh[t]-r0-act[t]*r1)
        g=gate[t]; u=up[t]
        s,si=silu_parts(g)
        gg=(ga*u*s*(1.0+g*(1.0-s))).astype(bf)
        gu=(ga*si).astype(bf)
        both=jnp.concatenate([gg,gu],axis=1)
        GF[t,:,0:2*Hd]=dot(ln2T[...],both).astype(bf)
        gln2[...]+=dot_t(both,WF[t,:,0:2*Hd])
        return 0
    lax.fori_loop(0,T,three,0)

def norm_back(src, e_src, gain, add, dst, lay, row, dst16=None):
    n=src.shape[0]
    lay[row:row+2,:]=jnp.zeros((2,src.shape[1]),f32)
    def it(s):
        a,inv=norm(src[s,:]); e=e_src[s,:]
        lay[row:row+1,:]+=jnp.sum(e*a,axis=0,keepdims=True)
        lay[row+1:row+2,:]+=jnp.sum(e,axis=0,keepdims=True)
        eg=e*gain
        d=add[s,:]+inv*(eg-jnp.mean(eg,axis=1,keepdims=True)-a*jnp.mean(eg*a,axis=1,keepdims=True))
        dst[s,:]=d
        if dst16 is not None: dst16[s,:]=d.astype(bf)
    chunks(n,48,it)

def attention_back(q,K,V,E,linv,att,gatt,dq,dK,dV,step=528):
    n=q.shape[0]; m=K.shape[0]
    def pair(p,_):
        c=pl.ds(pl.multiple_of(p*128,128),128)
        k2=K[:,c]; v2=V[:,c]
        R=linv[:,c]
        do=gatt[:,c].astype(f32)*R
        dob=do.astype(bf)
        dl=dob.astype(f32)*att[:,c].astype(f32)
        q2=q[:,c]
        dqv=None; dkv=None; dvv=None
        for a in (0,1):
            ka=jnp.where(lanes(m,a),k2,jnp.zeros_like(k2))
            va=jnp.where(lanes(m,a),v2,jnp.zeros_like(v2))
            qa=jnp.where(lanes(n,a),q2,jnp.zeros_like(q2))
            da=jnp.where(lanes(n,a),dob,jnp.zeros_like(dob))
            delta=jnp.sum(jnp.where(lanes(n,a),dl,0.0),axis=1,keepdims=True)
            dP=dot_t(dob,va)
            e=E[2*p+a]
            dS=(e.astype(f32)*(dP-delta)).astype(bf)
            x=dot(dS,ka); y=dot_l(dS,qa); z=dot_l(e,da)
            dqv=x if dqv is None else dqv+x
            dkv=y if dkv is None else dkv+y
            dvv=z if dvv is None else dvv+z
        dq[:,c]=dqv*0.125
        dK[:,c]=dkv
        dV[:,c]=dvv
        return 0
    lax.fori_loop(0,q.shape[1]//128,pair,0)

VMEM = pl.BlockSpec(memory_space=pltpu.VMEM)
HBM = pl.BlockSpec(memory_space=pl.ANY)
LIMIT = 60 * 2**20


def local_call(body, ins, outs, scratch=(), flops=0):
    return pl.pallas_call(
        body,
        out_shape=[jax.ShapeDtypeStruct(s, d) for s, d in outs],
        in_specs=[VMEM] * len(ins),
        out_specs=[VMEM] * len(outs),
        scratch_shapes=[pltpu.VMEM(s, d) for s, d in scratch],
        compiler_params=pltpu.CompilerParams(vmem_limit_bytes=LIMIT),
    )(*ins)


def rotary_tables(slots, rows, total):
    quarter = HD // 4
    positions = (slots[:, None] * rows + jnp.arange(rows, dtype=jnp.int32)).reshape(-1)
    inside = (positions >= 1) & (positions <= GRID * GRID)
    patch = jnp.where(inside, positions - 1, 0)
    frequency = 10000.0 ** (-jnp.arange(quarter, dtype=jnp.float32) / quarter)
    row_angle = (patch // GRID).astype(jnp.float32)[:, None] * frequency
    column_angle = (patch % GRID).astype(jnp.float32)[:, None] * frequency
    angles = jnp.concatenate([row_angle, row_angle, column_angle, column_angle], axis=-1)
    angles = jnp.pad(angles, ((0, total - angles.shape[0]), (0, 0)))
    angles = jnp.concatenate([angles, angles], axis=-1)
    sine = jnp.sin(angles)
    first = (jnp.arange(2 * HD) // quarter) % 2 == 0
    return jnp.cos(angles), jnp.where(first, -sine, 0.0), jnp.where(first, 0.0, sine)


def key_bias(slots, rows, total):
    positions = (slots[:, None] * rows + jnp.arange(rows, dtype=jnp.int32)).reshape(-1)
    bias = jnp.where(positions < VALID, 0.0, -1e30).astype(jnp.float32)
    return jnp.pad(bias, (0, total - bias.shape[0]), constant_values=-1e30)


GATHER_A = (((0, 384), "y"), ((384, 384), "x"))
GATHER_F = (((0, 384), "y"), ((384, 384), "x"), ((768, 384), "y"), ((1152, 384), "x"))


def forward_kernel(
    F, C, T, weights,
    tok, cot, wa, wf, gains, cos, sa, sb, bias,
    cin, WF, x, ln1, q, K, V, Wq, Wk, Wv, Wm, E, linv, att, mid, ln2,
    tin, WA, send, recv, local,
):
    place = Place(F, C, T)
    sems = Sems(send, recv)
    partners = place.partners(weights)
    hail(partners)
    n = x.shape[0]
    tokens = Exchange(place, sems, tok, tin)
    cots = Exchange(place, sems, cot, cin)
    swap = [sems.remote(X.at[pl.ds(0, n)], X.at[pl.ds(n, n)], place.sibling) for X in (K, V)]
    if weights:
        ga = [Gather(place, sems, wa, WA, cols, first) for cols, first in GATHER_A]
        gf = [Gather(place, sems, wf, WF, cols, first) for cols, first in GATHER_F]
    else:
        ga, gf = [], []
        copy = pltpu.make_async_copy(wa, WA, local.at[0])
        copy.start()
        copy.wait()
    for g in ga + gf:
        g.own.start()
    heard(partners)
    for s in range(3):
        for g in ga:
            g.stage(s)
        if s == 1:
            tokens.start()
    tokens.wait()
    for g in gf[:2]:
        g.stage(0)
    spread(tin, x)
    normal(x, gains, ln1)
    for g in ga:
        g.stage(3)
    for g in ga:
        g.finish()
    for i, W in enumerate((Wq, Wk, Wv, Wm)):
        join(WA, i, W, T)
    for g in gf[:2]:
        g.stage(1)
    for g in gf[2:]:
        g.stage(0)
    project(ln1, Wk, cos, sa, sb, K)
    swap[0].start()
    project(ln1, Wv, None, None, None, V)
    swap[1].start()
    for g in gf[:2]:
        g.stage(2)
    project(ln1, Wq, cos, sa, sb, q, 0.125)
    for copy in swap:
        copy.wait_recv()

    def service(p):
        if weights:

            @pl.when(p == 1)
            def _():
                for g in gf[2:]:
                    g.stage(1)
                cots.start()

            @pl.when(p == 2)
            def _():
                for g in gf[:2]:
                    g.stage(3)

            @pl.when(p == 3)
            def _():
                for g in gf[2:]:
                    g.stage(2)

            @pl.when(p == 5)
            def _():
                for g in gf[2:]:
                    g.stage(3)

        else:

            @pl.when(p == 1)
            def _():
                cots.start()

    attention(q, K, V, bias, E, linv, att, service)
    merge(att, Wm, x, mid, gains, ln2)
    cots.wait()
    for g in gf:
        g.finish()
    for g in ga + gf:
        g.settle()
    for copy in swap:
        copy.wait_send()
    tokens.finish()
    cots.finish()


def forward_call(F, C, T, n, tokens, cotangent, a, f, gains, cos, sa, sb, bias):
    weights = a.ndim == 2
    D = tokens.shape[-1]
    J = C * T // 2
    nh = D // HD
    chunk = (J,) + tokens.shape[1:]
    whole_a = (T, D, a.shape[-1])
    whole_f = (T, D, f.shape[-1])
    outs = [(chunk, bf), (whole_f if weights else (8, 128), bf)]
    outs += [((n, D), f32), ((n, D), bf), ((n, D), bf), ((2 * n, D), bf), ((2 * n, D), bf)]
    outs += [((D, D), bf)] * 4
    outs += [((nh, n, 2 * n), bf), ((n, D), f32), ((n, D), bf), ((n, D), f32), ((n, D), bf)]
    return pl.pallas_call(
        functools.partial(forward_kernel, F, C, T, weights),
        out_shape=[jax.ShapeDtypeStruct(s, d) for s, d in outs],
        in_specs=[HBM] * 4 + [VMEM] * 5,
        out_specs=[HBM] * 2 + [VMEM] * (len(outs) - 2),
        scratch_shapes=[
            pltpu.VMEM(chunk, bf),
            pltpu.VMEM(whole_a, bf),
            pltpu.SemaphoreType.DMA((128,)),
            pltpu.SemaphoreType.DMA((128,)),
            pltpu.SemaphoreType.DMA((1,)),
        ],
        compiler_params=pltpu.CompilerParams(collective_id=1, has_side_effects=True, vmem_limit_bytes=LIMIT),
    )(tokens, cotangent, a, f, gains, cos, sa, sb, bias)


REDUCE_PARTS = ((1, (0, 384), "x"), (1, (384, 384), "y"), (1, (768, 384), "x"), (1, (1152, 384), "y"), (0, (0, 384), "x"), (0, (384, 384), "y"))


def reduce_kernel(F, C, T, R, weights, *refs):
    if weights:
        GA, GF, bo, tg, out, bo_out, tg_out, send, recv = refs[:9]
        scr = iter(refs[9:])
    else:
        bo, tg, bo_out, tg_out, send, recv = refs
    place = Place(F, C, T)
    S = Sems(send, recv)
    partners = place.partners(weights)
    hail(partners)
    heard(partners)
    parts = []
    if weights:
        for which, cols, first in REDUCE_PARTS:
            parts.append(
                Reduce(
                    place, S, (GA, GF)[which], cols, first, next(scr), next(scr), next(scr), next(scr), next(scr), next(scr),
                    out, cols[0] + which * GA.shape[2], R,
                )
            )
    names = ("stage_c", "stage_1", "stage_2", "stage_3", "stage_4", "finish")
    steps = sorted((2 * s + i // 2, i, s) for i in range(len(parts)) for s in range(6))
    for _, i, s in steps:
        getattr(parts[i], names[s])()
    back = [Exchange(place, S, bo, bo_out), Exchange(place, S, tg, tg_out)]
    for b in back:
        b.start()
    for b in back:
        b.wait()
        b.finish()


def reduce_call(F, C, T, R, grads, bo, tg):
    weights = bool(grads)
    H = T // 2
    scratch = [pltpu.SemaphoreType.DMA((128,)), pltpu.SemaphoreType.DMA((128,))]
    outs = []
    bufs = lambda *s: scratch.append(pltpu.VMEM(s, jnp.bfloat16))
    if weights:
        D = grads[0].shape[1]
        outs.append(jax.ShapeDtypeStruct((R, sum(g.shape[2] for g in grads)), jnp.float32))
        for _, (_, n), first in REDUCE_PARTS:
            bufs(H, D, n)
            bufs(H, D, n)
            if first == "x":
                bufs(F - 1, H, C * R, n)
                bufs(H, C * R, n)
                bufs(H - 1, C * R, n)
            else:
                bufs(H - 1, D, n)
                bufs(D, n)
                bufs(F - 1, C * R, n)
            bufs(C - 1, R, n)
    outs += [jax.ShapeDtypeStruct(bo.shape, bo.dtype)] * 2
    return pl.pallas_call(
        functools.partial(reduce_kernel, F, C, T, R, weights),
        out_shape=outs,
        in_specs=[VMEM] * len(grads) + [HBM] * 2,
        out_specs=[VMEM] * (1 if weights else 0) + [HBM] * 2,
        scratch_shapes=scratch,
        compiler_params=pltpu.CompilerParams(collective_id=2, has_side_effects=True, vmem_limit_bytes=LIMIT),
    )(*grads, bo, tg)


def ffn_kernel(T, cin, ln2, WF, mid, ig, gains, GF, inner, bo, gmid, gb, lay, cot, cotb, ln2T, cotT, gate, up, act, gh, out, gln2):
    spread(cin, cot)
    cotb[...] = cot[...].astype(jnp.bfloat16)
    cotT[...] = cot[...].T.astype(jnp.bfloat16)
    ln2T[...] = ln2[...].astype(jnp.float32).T.astype(jnp.bfloat16)
    ffn(ln2, ln2T, cotb, cotT, WF, mid, ig, gate, up, act, gh, None, GF, inner, out, gln2, T)
    J, r, _ = bo.shape
    for j in range(J):
        bo[j] = out[j * r : (j + 1) * r, :].astype(jnp.bfloat16)
    norm_back(mid, gln2, gains[2:3, :], cot, gmid, lay, 0, gb)


def attend_back_kernel(q, K, V, E, linv, att, gb, Wm, dq, dK, dV, Gm, gatt):
    gatt[...] = dot(gb[...], Wm[...]).astype(jnp.bfloat16)
    Gm[...] = dot_l(gb[...], att[...])
    attention_back(q, K, V, E, linv, att, gatt, dq, dK, dV)


def final_kernel(T, x, ln1, gains, gmid, dq, dK, dV, oK, oV, Gm, Wq, Wk, Wv, cos, sa, sb, GA, tg, lay, G, gln1, tok):
    n = x.shape[0]
    c, a, b = cos[...], -sa[...], -sb[...]
    for g, W in enumerate((Wq, Wk, Wv)):
        if g == 0:
            v = turn(dq[...], c, a, b)
        elif g == 1:
            v = turn(dK[...] + oK[...].astype(jnp.float32), c, a, b)
        else:
            v = dV[...] + oV[...].astype(jnp.float32)
        v = v.astype(jnp.bfloat16)
        G[...] = dot_l(ln1[...], v)
        part(G, GA, g, T)
        d = dot_t(v, W[...])
        gln1[...] = d if g == 0 else gln1[...] + d
    part(Gm, GA, 3, T)
    norm_back(x, gln1, gains[0:1, :], gmid, tok, lay, 0)
    J, r, _ = tg.shape
    for j in range(J):
        tg[j] = tok[j * r : (j + 1) * r, :].astype(jnp.bfloat16)


def moments(gradient, moment, square):
    moment = BETA_ONE * moment + (1.0 - BETA_ONE) * gradient
    square = BETA_TWO * square + (1.0 - BETA_TWO) * gradient * gradient
    update = (
        moment / (1.0 - BETA_ONE**STEP) / (jnp.sqrt(square / (1.0 - BETA_TWO**STEP)) + EPS_ADAM)
    )
    return (moment, square, update)


def body(
    F, C, T,
    tokens, cotangent, layer_gains, layer_first, layer_second, inner_gains, inner_first, inner_second,
    attend_weight, attend_first, attend_second, merge_weight, merge_first, merge_second,
    expand_weight, expand_first, expand_second, shrink_weight, shrink_first, shrink_second,
):
    bf, f32 = jnp.bfloat16, jnp.float32
    D = tokens.shape[-1]
    R = attend_weight.shape[1]
    rows = tokens.shape[1]
    J = C * T // 2
    assert J == tokens.shape[0]
    n = -(-J * rows // 48) * 48
    heads = attend_weight.shape[2]
    hidden = expand_weight.shape[2]
    fast = R % 16 == 0
    low = lax.axis_index("tp") % 2
    slots = jnp.arange(J, dtype=jnp.int32) * 2
    cos, sa, sb = rotary_tables(slots + low, rows, n)
    bias = jnp.concatenate([key_bias(slots + low, rows, n), key_bias(slots + 1 - low, rows, n)])[None]
    pack_a = jnp.concatenate([attend_weight[0], attend_weight[1], attend_weight[2], merge_weight.T], axis=1).astype(bf)
    pack_f = jnp.concatenate([expand_weight[0], expand_weight[1], shrink_weight.T], axis=1).astype(bf)
    if not fast:
        pack_a, pack_f = (
            lax.all_gather(lax.all_gather(p, ("fsdp", "ctx"), axis=0, tiled=True), "tp", axis=0)
            for p in (pack_a, pack_f)
        )
    inner_all = lax.all_gather(inner_gains, "tp", axis=0)
    cin, WF, x, ln1, q, K, V, Wq, Wk, Wv, Wm, E, linv, att, mid, ln2 = forward_call(
        F, C, T, n, tokens, cotangent, pack_a, pack_f, layer_gains, cos, sa, sb, bias
    )
    if not fast:
        WF = pack_f
    swap = [(t, t + 1 - 2 * (t % 2)) for t in range(T)]
    GF, inner, bo, gmid, gb, lay2 = local_call(
        functools.partial(ffn_kernel, T),
        [cin, ln2, WF, mid, inner_all, layer_gains],
        [((T, D, 3 * hidden), bf), ((T, 2, hidden), f32), (tokens.shape, bf), ((n, D), f32), ((n, D), bf), ((2, D), f32)],
        [((n, D), f32), ((n, D), bf), ((D, n), bf), ((D, n), bf)] + [((T, n, hidden), f32)] * 4 + [((n, D), f32)] * 2,
    )
    dq, dK, dV, Gm = local_call(
        attend_back_kernel,
        [q, K, V, E, linv, att, gb, Wm],
        [((n, D), f32), ((2 * n, D), f32), ((2 * n, D), f32), ((D, D), f32)],
        [((n, D), bf)],
    )
    oK, oV = lax.ppermute((dK[n:].astype(bf), dV[n:].astype(bf)), "tp", swap)
    GA, tg, lay1 = local_call(
        functools.partial(final_kernel, T),
        [x, ln1, layer_gains, gmid, dq, dK[:n], dV[:n], oK, oV, Gm, Wq, Wk, Wv, cos, sa, sb],
        [((T, D, 4 * heads), bf), (tokens.shape, bf), ((2, D), f32)],
        [((D, D), f32), ((n, D), f32), ((n, D), f32)],
    )
    if fast:
        sums, block_output, token_gradient = reduce_call(F, C, T, R, [GA, GF], bo, tg)
    else:
        block_output, token_gradient = reduce_call(F, C, T, R, [], bo, tg)
        sums = jnp.concatenate([GA, GF], axis=2).astype(f32)
        sums = lax.psum_scatter(sums, "tp", scatter_dimension=0, tiled=False)
        sums = lax.psum_scatter(sums, ("fsdp", "ctx"), scatter_dimension=0, tiled=True)
    token_gradient = token_gradient.astype(f32)
    a = sums[:, : 4 * heads]
    attend_sum = jnp.stack([a[:, i * heads : (i + 1) * heads] for i in range(3)])
    merge_sum = a[:, 3 * heads :].T
    b = sums[:, 4 * heads :]
    expand_sum = jnp.stack([b[:, i * hidden : (i + 1) * hidden] for i in range(2)])
    shrink_sum = b[:, 2 * hidden :].T
    layer_grad, inner_total = lax.psum((jnp.concatenate([lay1, lay2]), inner), ("fsdp", "ctx", "tp"))
    inner_grad = lax.dynamic_index_in_dim(inner_total, lax.axis_index("tp"), 0, keepdims=False)
    matrices = (
        (attend_weight, attend_sum, attend_first, attend_second),
        (merge_weight, merge_sum, merge_first, merge_second),
        (expand_weight, expand_sum, expand_first, expand_second),
        (shrink_weight, shrink_sum, shrink_first, shrink_second),
    )
    states = []
    weight_terms = []
    update_terms = []
    for weight, gradient, moment, square in matrices:
        moment_new, square_new, update = moments(gradient, moment, square)
        update = update + DECAY * weight
        states.append((moment_new, square_new, update))
        weight_terms.append(jnp.sum(weight * weight))
        update_terms.append(jnp.sum(update * update))
    weight_sums, update_sums = lax.psum(
        (jnp.stack(weight_terms), jnp.stack(update_terms)), ("fsdp", "ctx", "tp")
    )
    weight_norms = jnp.sqrt(weight_sums)
    update_norms = jnp.sqrt(update_sums)
    updated = []
    for number in range(4):
        ratio = weight_norms[number] / update_norms[number]
        updated.append(matrices[number][0] - RATE * ratio * states[number][2])
    layer_moment, layer_square, layer_step = moments(layer_grad, layer_first, layer_second)
    inner_moment, inner_square, inner_step = moments(inner_grad, inner_first, inner_second)
    trust_norms = jnp.stack([weight_norms, update_norms], axis=1)
    return (
        block_output, token_gradient,
        updated[0], states[0][0], states[0][1],
        updated[1], states[1][0], states[1][1],
        updated[2], states[2][0], states[2][1],
        updated[3], states[3][0], states[3][1],
        layer_gains - RATE_GAINS * layer_step, layer_moment, layer_square,
        inner_gains - RATE_GAINS * inner_step, inner_moment, inner_square,
        trust_norms,
    )


def solution(mesh):
    tok = P("fsdp", ("ctx", "tp"), None)
    wide = P(None, ("fsdp", "ctx"), "tp")
    tall = P("tp", ("fsdp", "ctx"))
    split = P(None, "tp")
    sizes = (mesh.shape["fsdp"], mesh.shape["ctx"], mesh.shape["tp"])
    return jax.shard_map(
        functools.partial(body, *sizes),
        mesh=mesh,
        in_specs=(tok, tok, P(), P(), P(), split, split, split)
        + (wide,) * 3 + (tall,) * 3 + (wide,) * 3 + (tall,) * 3,
        out_specs=(tok, tok) + (wide,) * 3 + (tall,) * 3 + (wide,) * 3 + (tall,) * 3
        + (P(),) * 3 + (split,) * 3 + (P(),),
        check_vma=False,
    )
```

```python
import functools
import jax
import jax.numpy as jnp
from jax import lax
from jax.experimental import pallas as pl
from jax.experimental.pallas import tpu as pltpu
from jax.sharding import PartitionSpec as P

HD = 64
GRID = 32
STEP = 5
VALID = 1025
BETA_ONE = 0.5
BETA_TWO = 0.5
EPS_ADAM = 1e-06
DECAY = 0.01
RATE = 0.5
RATE_GAINS = 0.3
MESH = pl.DeviceIdType.MESH
f32 = jnp.float32
bf = jnp.bfloat16


class Place:
    def __init__(self, F, C, T):
        self.F, self.C, self.T, self.H = F, C, T, T // 2
        self.f = lax.axis_index("fsdp")
        self.c = lax.axis_index("ctx")
        self.t = lax.axis_index("tp")
        self.low = lax.rem(self.t, 2)
        self.high = lax.div(self.t, 2)
        self.pair = self.c * self.H + self.high
        self.pairs = C * self.H
        self.sibling = {"tp": self.t + 1 - 2 * self.low}
        self.xs = [lax.rem(self.f + k, F) for k in range(F)]
        self.ys = [lax.rem(self.high + k, self.H) for k in range(self.H)]
        self.zs = [lax.rem(self.c + k, C) for k in range(C)]

    def at_x(self, k):
        return {"fsdp": self.xs[k]}

    def at_y(self, k):
        return {"tp": self.ys[k] * 2 + self.low}

    def at_z(self, k):
        return {"ctx": self.zs[k]}

    def pair_at(self, k):
        i = lax.rem(self.pair + k, self.pairs)
        return i, {"ctx": lax.div(i, self.H), "tp": lax.rem(i, self.H) * 2 + self.low}

    def partners(self, with_x):
        out = [self.sibling] + [self.pair_at(k)[1] for k in range(1, self.pairs)]
        if with_x:
            out += [self.at_x(k) for k in range(1, self.F)]
        return out


def hail(partners):
    barrier = pltpu.get_barrier_semaphore()
    for partner in partners:
        pl.semaphore_signal(barrier, inc=1, device_id=partner, device_id_type=MESH)


def heard(partners):
    pl.semaphore_wait(pltpu.get_barrier_semaphore(), len(partners))


class Sems:
    def __init__(self, send, recv):
        self.send, self.recv, self.n = send, recv, 0

    def remote(self, src, dst, device):
        i = self.n
        self.n += 1
        return pltpu.make_async_remote_copy(
            src, dst, self.send.at[i], self.recv.at[i], device_id=device, device_id_type=MESH
        )

    def local(self, src, dst):
        i = self.n
        self.n += 1
        return pltpu.make_async_copy(src, dst, self.send.at[i])


class Exchange:
    def __init__(self, place, sems, src, dst):
        self.own = sems.local(src.at[place.pair], dst.at[place.pair])
        self.copies = []
        for k in range(1, place.pairs):
            i, device = place.pair_at(k)
            self.copies.append(sems.remote(src.at[i], dst.at[place.pair], device))

    def start(self):
        self.own.start()
        for copy in self.copies:
            copy.start()

    def wait(self):
        self.own.wait()
        for copy in self.copies:
            copy.wait_recv()

    def finish(self):
        for copy in self.copies:
            copy.wait_send()


class Gather:
    def __init__(self, place, sems, pack, whole, cols, first):
        P, R = place, pack.shape[0]
        C, F, H = P.C, P.F, P.H
        n = C * R
        window = pl.ds(*cols)

        def push(t, row, rows, device):
            block = whole.at[t, pl.ds(pl.multiple_of(row, 16), rows), window]
            return sems.remote(block, block, device)

        row = (P.f * C + P.c) * R
        base = P.f * n
        self.own = sems.local(
            pack.at[:, window], whole.at[P.t, pl.ds(pl.multiple_of(row, 16), R), window]
        )
        along_z = [push(P.t, row, R, P.at_z(k)) for k in range(1, C)]
        tees = [y * 2 + P.low for y in P.ys]
        if first == "y":
            second = [push(P.t, base, n, P.at_y(k)) for k in range(1, H)]
            third = [push(t, base, n, P.at_x(k)) for k in range(1, F) for t in tees]
            over_3 = [push(t, base, n, P.sibling) for t in tees[1:]]
            over_4 = [push(t, P.xs[k] * n, n, P.sibling) for k in range(1, F) for t in tees]
        else:
            second = [push(P.t, base, n, P.at_x(k)) for k in range(1, F)]
            third = [push(P.t, 0, n * F, P.at_y(k)) for k in range(1, H)]
            over_3 = [push(P.t, P.xs[k] * n, n, P.sibling) for k in range(1, F)]
            over_4 = [push(t, 0, n * F, P.sibling) for t in tees[1:]]
        over_2 = [push(P.t, base, n, P.sibling)]
        self.waits = [[], along_z, second, third]
        self.starts = [along_z, second + over_2, third + over_3, over_4]
        self.sent_over = over_2 + over_3 + over_4

    def stage(self, s):
        if s == 0:
            self.own.wait()
        for copy in self.waits[s]:
            copy.wait_recv()
        for copy in self.starts[s]:
            copy.start()

    def finish(self):
        for copy in self.sent_over:
            copy.wait_recv()

    def settle(self):
        for group in self.starts:
            for copy in group:
                copy.wait_send()


def by_rows(rows, step, body):
    def it(i, _):
        body(pl.multiple_of(i * step, step), step)
        return 0

    lax.fori_loop(0, rows // step, it, 0)


class Reduce:
    def __init__(self, place, sems, G, cols, first, lands, out, out_col, R):
        P, n = place, place.C * R
        C, F, H, D = P.C, P.F, P.H, G.shape[1]
        window = pl.ds(*cols)
        L1, L2, L3 = lands
        self.out, self.to, self.R = out, pl.ds(out_col, cols[1]), R
        base = pl.multiple_of(P.f * n, 16)
        mine = pl.multiple_of(base + P.c * R, 16)
        self.copies = [[], [], []]

        def rows(u, start, count):
            return G.at[u, pl.ds(start, count), window]

        def send(stage, src, dst, device):
            self.copies[stage].append(sems.remote(src, dst, device))

        if first == "x":
            for k in range(1, F):
                for u in range(H):
                    send(0, rows(u, pl.multiple_of(P.xs[k] * n, 16), n), L1.at[k - 1, u], P.at_x(k))
            for k in range(1, H):
                send(1, rows(P.ys[k], base, n), L2.at[k - 1], P.at_y(k))
            self.adds = [
                [(rows(u, base, n), [L1.at[k - 1, u] for k in range(1, F)]) for u in range(H)],
                [(rows(P.high, base, n), [L2.at[k - 1] for k in range(1, H)])],
            ]
        else:
            for k in range(1, H):
                send(0, rows(P.ys[k], 0, D), L1.at[k - 1], P.at_y(k))
            for k in range(1, F):
                send(1, rows(P.high, pl.multiple_of(P.xs[k] * n, 16), n), L2.at[k - 1], P.at_x(k))
            self.adds = [
                [(rows(P.high, 0, D), [L1.at[k - 1] for k in range(1, H)])],
                [(rows(P.high, base, n), [L2.at[k - 1] for k in range(1, F)])],
            ]
        for k in range(1, C):
            send(2, rows(P.high, pl.multiple_of(base + P.zs[k] * R, 16), R), L3.at[k - 1], P.at_z(k))
        self.last = (rows(P.high, mine, R), [L3.at[k - 1] for k in range(1, C)])

    def stage(self, s):
        if s > 0:
            for copy in self.copies[s - 1]:
                copy.wait_recv()
        if s in (1, 2):
            for dst, lands in self.adds[s - 1]:

                def add(r, k, dst=dst, lands=lands):
                    v = dst[pl.ds(r, k), :].astype(f32)
                    for land in lands:
                        v = v + land[pl.ds(r, k), :].astype(f32)
                    dst[pl.ds(r, k), :] = v.astype(bf)

                by_rows(dst.shape[0], 96, add)
        if s == 3:
            dst, lands = self.last
            v = dst[...].astype(f32)
            for land in lands:
                v = v + land[...].astype(f32)
            self.out[:, self.to] = v
        else:
            for copy in self.copies[s]:
                copy.start()

    def settle(self):
        for group in self.copies:
            for copy in group:
                copy.wait_send()


def reduce_lands(parts, F, C, H, D, R):
    out = []
    for (_, n), first in parts:
        if first == "x":
            out += [(F - 1, H, C * R, n), (H - 1, C * R, n)]
        else:
            out += [(H - 1, D, n), (F - 1, C * R, n)]
        out.append((C - 1, R, n))
    return [pltpu.VMEM(s, bf) for s in out]
EPS=1e-6
def dot(a,b): return jnp.dot(a,b,preferred_element_type=f32)
def dot_t(a,b): return lax.dot_general(a,b,(((1,),(1,)),((),())),preferred_element_type=f32)
def dot_l(a,b): return lax.dot_general(a,b,(((0,),(0,)),((),())),preferred_element_type=f32)

def chunks(rows, step, body):
    def it(i,_):
        body(pl.ds(pl.multiple_of(i*step,step),step)); return 0
    lax.fori_loop(0,rows//step,it,0)

def norm(v):
    mean=jnp.mean(v,axis=-1,keepdims=True)
    var=jnp.mean(v*v,axis=-1,keepdims=True)-mean*mean
    inv=lax.rsqrt(var+EPS)
    return (v-mean)*inv, inv

def spread(src3, dst):
    J,r,D=src3.shape
    n=dst.shape[0]
    pad=n-J*r
    if pad: dst[n-16:n,:]=jnp.zeros((16,D),f32)
    for j in range(J):
        dst[j*r:(j+1)*r,:]=src3[j].astype(f32)

def join(WA, g, dst, T):
    w=WA.shape[2]//4
    def it(i,_):
        s=pl.ds(pl.multiple_of(i*96,96),96)
        row=jnp.concatenate([WA[t,s,g*w:(g+1)*w] for t in range(T)],axis=1)
        dst[s,:]=row
        return 0
    lax.fori_loop(0,WA.shape[1]//96,it,0)

def part(src, GA, g, T):
    w=GA.shape[2]//4
    def it(i,_):
        s=pl.ds(pl.multiple_of(i*96,96),96)
        v=src[s,:]
        for t in range(T):
            GA[t,s,g*w:(g+1)*w]=v[:,t*w:(t+1)*w].astype(bf)
        return 0
    lax.fori_loop(0,GA.shape[1]//96,it,0)

def turn(v, cos, sa, sb):
    n=v.shape[1]
    out=[]
    for i in range(n//128):
        a=v[:,i*128:(i+1)*128]
        out.append(a*cos+pltpu.roll(a,128-16,1)*sa+pltpu.roll(a,16,1)*sb)
    return jnp.concatenate(out,axis=1)

def normal(x, gains, ln1):
    def ln(s):
        v,_=norm(x[s,:])
        ln1[s,:]=(v*gains[0:1,:]+gains[1:2,:]).astype(bf)
    chunks(x.shape[0],48,ln)


def project(ln1, W, cos, sa, sb, dst, scale=None):
    n=ln1.shape[0]//2
    y=dot(ln1[0:n,:],W[...])
    if cos is not None: y=turn(y,cos[...],sa[...],sb[...])
    if scale is not None: y=y*scale
    dst[0:n,:]=y.astype(bf)


def lanes(n, a):
    return (lax.broadcasted_iota(jnp.int32,(n,128),1)//64==a)

def attention(q,K,V,bias,E,linv,att,service):
    n=q.shape[0]; m=K.shape[0]
    def pair(p,_):
        service(p)
        c=pl.ds(pl.multiple_of(p*128,128),128)
        k2=K[:,c]; v2=V[:,c]
        q2=q[:,c]
        o=None; li=[]
        for a in (0,1):
            ka=jnp.where(lanes(m,a),k2,jnp.zeros_like(k2))
            va=jnp.where(lanes(m,a),v2,jnp.zeros_like(v2))
            S=dot_t(q2,ka)+bias[0:1,:]
            mx=jnp.max(S,axis=1,keepdims=True)
            e=jnp.exp(S-mx)
            l=1.0/jnp.sum(e,axis=1,keepdims=True)
            eb=e.astype(bf)
            E[2*p+a]=eb
            oa=dot(eb,va)*l
            o=oa if o is None else o+oa
            li.append(l)
        att[:,c]=o.astype(bf)
        linv[:,c]=jnp.where(lanes(n,0),li[0],li[1])
        return 0
    lax.fori_loop(0,q.shape[1]//128,pair,0)

def merge(att,Wm,x,mid,gains,ln2):
    mid[...]=x[...]+dot_t(att[...],Wm[...])
    def ln(s):
        v,_=norm(mid[s,:])
        ln2[s,:]=(v*gains[2:3,:]+gains[3:4,:]).astype(bf)
    chunks(x.shape[0],48,ln)

def silu_parts(g):
    s=jax.nn.sigmoid(g)
    return s, g*s

def ffn(ln2,ln2T,cot,cotT,WF,mid,ig,gate,up,act,gh,stat,GF,inner,out,gln2,T):
    n=ln2.shape[0]; Hd=WF.shape[2]//3; FFN=T*Hd
    def one(t,c):
        s0,s1=c
        gu=dot(ln2[...],WF[t,:,0:2*Hd])
        g=gu[:,:Hd]; u=gu[:,Hd:]
        _,si=silu_parts(g)
        a=si*u
        gate[t]=g; up[t]=u; act[t]=a
        return s0+jnp.sum(a,axis=1,keepdims=True), s1+jnp.sum(a*a,axis=1,keepdims=True)
    z=jnp.zeros((n,1),f32)
    s0,s1=lax.fori_loop(0,T,one,(z,z))
    mean=s0/FFN; inv=lax.rsqrt(s1/FFN-mean*mean+EPS)
    out[...]=mid[...]
    def two(t,c):
        r0,r1=c
        n3=(act[t]-mean)*inv
        act[t]=n3
        gt=ig[t,0:1,:]
        hid=(n3*gt+ig[t,1:2,:]).astype(bf)
        out[...]+=dot_t(hid,WF[t,:,2*Hd:3*Hd])
        h=dot(cot[...],WF[t,:,2*Hd:3*Hd])
        GF[t,:,2*Hd:3*Hd]=dot(cotT[...],hid).astype(bf)
        inner[t,0:1,:]=jnp.sum(h*n3,axis=0,keepdims=True)
        inner[t,1:2,:]=jnp.sum(h,axis=0,keepdims=True)
        e=h*gt
        gh[t]=e
        return r0+jnp.sum(e,axis=1,keepdims=True), r1+jnp.sum(e*n3,axis=1,keepdims=True)
    r0,r1=lax.fori_loop(0,T,two,(z,z))
    r0=r0/FFN; r1=r1/FFN
    gln2[...]=jnp.zeros_like(gln2)
    def three(t,_):
        ga=inv*(gh[t]-r0-act[t]*r1)
        g=gate[t]; u=up[t]
        s,si=silu_parts(g)
        gg=(ga*u*s*(1.0+g*(1.0-s))).astype(bf)
        gu=(ga*si).astype(bf)
        both=jnp.concatenate([gg,gu],axis=1)
        GF[t,:,0:2*Hd]=dot(ln2T[...],both).astype(bf)
        gln2[...]+=dot_t(both,WF[t,:,0:2*Hd])
        return 0
    lax.fori_loop(0,T,three,0)

def norm_back(src, e_src, gain, add, dst, lay, row, dst16=None):
    n=src.shape[0]
    lay[row:row+2,:]=jnp.zeros((2,src.shape[1]),f32)
    def it(s):
        a,inv=norm(src[s,:]); e=e_src[s,:]
        lay[row:row+1,:]+=jnp.sum(e*a,axis=0,keepdims=True)
        lay[row+1:row+2,:]+=jnp.sum(e,axis=0,keepdims=True)
        eg=e*gain
        d=add[s,:].astype(f32)+inv*(eg-jnp.mean(eg,axis=1,keepdims=True)-a*jnp.mean(eg*a,axis=1,keepdims=True))
        dst[s,:]=d
        if dst16 is not None: dst16[s,:]=d.astype(bf)
    chunks(n,48,it)

def attention_back(q,K,V,E,linv,att,gatt,dq,dK,dV,step=528):
    n=q.shape[0]; m=K.shape[0]
    def pair(p,_):
        c=pl.ds(pl.multiple_of(p*128,128),128)
        k2=K[:,c]; v2=V[:,c]
        R=linv[:,c]
        do=gatt[:,c].astype(f32)*R
        dob=do.astype(bf)
        dl=dob.astype(f32)*att[:,c].astype(f32)
        q2=q[:,c]
        dqv=None; dkv=None; dvv=None
        for a in (0,1):
            ka=jnp.where(lanes(m,a),k2,jnp.zeros_like(k2))
            va=jnp.where(lanes(m,a),v2,jnp.zeros_like(v2))
            qa=jnp.where(lanes(n,a),q2,jnp.zeros_like(q2))
            da=jnp.where(lanes(n,a),dob,jnp.zeros_like(dob))
            delta=jnp.sum(jnp.where(lanes(n,a),dl,0.0),axis=1,keepdims=True)
            dP=dot_t(dob,va)
            e=E[2*p+a]
            dS=(e.astype(f32)*(dP-delta)).astype(bf)
            x=dot(dS,ka); y=dot_l(dS,qa); z=dot_l(e,da)
            dqv=x if dqv is None else dqv+x
            dkv=y if dkv is None else dkv+y
            dvv=z if dvv is None else dvv+z
        dq[:,c]=dqv*0.125
        dK[:,c]=dkv
        dV[:,c]=dvv
        return 0
    lax.fori_loop(0,q.shape[1]//128,pair,0)

VMEM = pl.BlockSpec(memory_space=pltpu.VMEM)
HBM = pl.BlockSpec(memory_space=pl.ANY)
LIMIT = 60 * 2**20


def local_call(body, ins, outs, scratch=(), flops=0):
    return pl.pallas_call(
        body,
        out_shape=[jax.ShapeDtypeStruct(s, d) for s, d in outs],
        in_specs=[VMEM] * len(ins),
        out_specs=[VMEM] * len(outs),
        scratch_shapes=[pltpu.VMEM(s, d) for s, d in scratch],
        compiler_params=pltpu.CompilerParams(vmem_limit_bytes=LIMIT),
    )(*ins)


def rotary_tables(slots, rows, total):
    quarter = HD // 4
    positions = (slots[:, None] * rows + jnp.arange(rows, dtype=jnp.int32)).reshape(-1)
    inside = (positions >= 1) & (positions <= GRID * GRID)
    patch = jnp.where(inside, positions - 1, 0)
    frequency = 10000.0 ** (-jnp.arange(quarter, dtype=jnp.float32) / quarter)
    row_angle = (patch // GRID).astype(jnp.float32)[:, None] * frequency
    column_angle = (patch % GRID).astype(jnp.float32)[:, None] * frequency
    angles = jnp.concatenate([row_angle, row_angle, column_angle, column_angle], axis=-1)
    angles = jnp.pad(angles, ((0, total - angles.shape[0]), (0, 0)))
    angles = jnp.concatenate([angles, angles], axis=-1)
    sine = jnp.sin(angles)
    first = (jnp.arange(2 * HD) // quarter) % 2 == 0
    return jnp.cos(angles), jnp.where(first, -sine, 0.0), jnp.where(first, 0.0, sine)


def key_bias(slots, rows, total):
    positions = (slots[:, None] * rows + jnp.arange(rows, dtype=jnp.int32)).reshape(-1)
    bias = jnp.where(positions < VALID, 0.0, -1e30).astype(jnp.float32)
    return jnp.pad(bias, (0, total - bias.shape[0]), constant_values=-1e30)


GATHER_A = (((0, 384), "y"), ((384, 384), "x"))
GATHER_F = (((0, 384), "y"), ((384, 384), "x"), ((768, 384), "y"), ((1152, 384), "x"))


def forward_kernel(
    F, C, T, weights,
    tok, cot, wa, wf, gains, cos, sa, sb, bias,
    cin, WF, x, ln1, q, K, V, Wq, Wk, Wv, Wm, E, linv, att, mid, ln2,
    tin, WA, send, recv, local,
):
    place = Place(F, C, T)
    sems = Sems(send, recv)
    partners = place.partners(weights)
    hail(partners)
    n = x.shape[0]
    tokens = Exchange(place, sems, tok, tin)
    cots = Exchange(place, sems, cot, cin)
    swap = [sems.remote(X.at[pl.ds(0, n)], X.at[pl.ds(n, n)], place.sibling) for X in (K, V, ln1)]
    if weights:
        ga = [Gather(place, sems, wa, WA, cols, first) for cols, first in GATHER_A]
        gf = [Gather(place, sems, wf, WF, cols, first) for cols, first in GATHER_F]
    else:
        ga, gf = [], []
        copy = pltpu.make_async_copy(wa, WA, local.at[0])
        copy.start()
        copy.wait()
    for g in ga + gf:
        g.own.start()
    heard(partners)
    for s in range(3):
        for g in ga:
            g.stage(s)
        if s == 1:
            tokens.start()
    tokens.wait()
    for g in gf[:2]:
        g.stage(0)
    spread(tin, x)
    normal(x, gains, ln1)
    swap[2].start()
    for g in ga:
        g.stage(3)
    for g in ga:
        g.finish()
    for i, W in enumerate((Wq, Wk, Wv, Wm)):
        join(WA, i, W, T)
    for g in gf[:2]:
        g.stage(1)
    for g in gf[2:]:
        g.stage(0)
    project(ln1, Wk, cos, sa, sb, K)
    swap[0].start()
    project(ln1, Wv, None, None, None, V)
    swap[1].start()
    for g in gf[:2]:
        g.stage(2)
    project(ln1, Wq, cos, sa, sb, q, 0.125)
    for copy in swap:
        copy.wait_recv()

    def service(p):
        if weights:

            @pl.when(p == 1)
            def _():
                for g in gf[2:]:
                    g.stage(1)
                cots.start()

            @pl.when(p == 2)
            def _():
                for g in gf[:2]:
                    g.stage(3)

            @pl.when(p == 3)
            def _():
                for g in gf[2:]:
                    g.stage(2)

            @pl.when(p == 5)
            def _():
                for g in gf[2:]:
                    g.stage(3)

        else:

            @pl.when(p == 1)
            def _():
                cots.start()

    attention(q, K, V, bias, E, linv, att, service)
    merge(att, Wm, x, mid, gains, ln2)
    cots.wait()
    for g in gf:
        g.finish()
    for g in ga + gf:
        g.settle()
    for copy in swap:
        copy.wait_send()
    tokens.finish()
    cots.finish()


def forward_call(F, C, T, n, tokens, cotangent, a, f, gains, cos, sa, sb, bias):
    weights = a.ndim == 2
    D = tokens.shape[-1]
    J = C * T // 2
    nh = D // HD
    chunk = (J,) + tokens.shape[1:]
    whole_a = (T, D, a.shape[-1])
    whole_f = (T, D, f.shape[-1])
    outs = [(chunk, bf), (whole_f if weights else (8, 128), bf)]
    outs += [((n, D), f32), ((2 * n, D), bf), ((n, D), bf), ((2 * n, D), bf), ((2 * n, D), bf)]
    outs += [((D, D), bf)] * 4
    outs += [((nh, n, 2 * n), bf), ((n, D), f32), ((n, D), bf), ((n, D), f32), ((n, D), bf)]
    return pl.pallas_call(
        functools.partial(forward_kernel, F, C, T, weights),
        out_shape=[jax.ShapeDtypeStruct(s, d) for s, d in outs],
        in_specs=[HBM] * 4 + [VMEM] * 5,
        out_specs=[HBM] * 2 + [VMEM] * (len(outs) - 2),
        scratch_shapes=[
            pltpu.VMEM(chunk, bf),
            pltpu.VMEM(whole_a, bf),
            pltpu.SemaphoreType.DMA((128,)),
            pltpu.SemaphoreType.DMA((128,)),
            pltpu.SemaphoreType.DMA((1,)),
        ],
        compiler_params=pltpu.CompilerParams(collective_id=1, has_side_effects=True, vmem_limit_bytes=LIMIT),
    )(tokens, cotangent, a, f, gains, cos, sa, sb, bias)


REDUCE_F = (
    ((1024, 256), "x"), ((1280, 256), "y"),
    ((0, 256), "x"), ((256, 256), "y"), ((512, 256), "x"), ((768, 256), "y"),
)
REDUCE_A = (((0, 256), "x"), ((256, 256), "y"), ((512, 128), "x"), ((640, 128), "y"))


def own_and_other(v, low, H):
    w = v.shape[1] // (2 * H)
    mine, theirs = [], []
    for u in range(H):
        a, b = v[:, 2 * u * w : (2 * u + 1) * w], v[:, (2 * u + 1) * w : (2 * u + 2) * w]
        mine.append(jnp.where(low == 0, a, b))
        theirs.append(jnp.where(low == 0, b, a))
    return mine, theirs


def backward_kernel(
    F, C, T, R, weights,
    cin, WF, ln2, mid, x, ln1, q, K, V, Wq, Wk, Wv, Wm, E, linv, att, ig, gains, cos, sa, sb,
    bo_out, tg_out, sums, small, *rest,
):
    if weights:
        GF, GA = None, None
    else:
        GF, GA = rest[:2]
        rest = rest[2:]
    (LN2, CT, GB, XO, gmid, bo, tg, SM, SML, GF_s, GA_s, send, recv, local, free) = rest[:15]
    if weights:
        GF, GA = GF_s, GA_s
    lands = rest[15:]
    place = Place(F, C, T)
    H, low, sib = place.H, place.low, place.sibling
    sems = Sems(send, recv)
    partners = place.partners(True)
    hail(partners)
    J, r, D = bo.shape
    n = gmid.shape[0]
    Hd = ig.shape[2]
    top, bottom = pl.ds(0, n), pl.ds(n, n)
    nlocal = [0]

    def fetch(src, dst):
        copy = pltpu.make_async_copy(src, dst, local.at[nlocal[0]])
        nlocal[0] += 1
        copy.start()
        return copy

    swap_ln2 = sems.remote(LN2.at[top], LN2.at[bottom], sib)
    swap_ct = sems.remote(CT.at[top], CT.at[bottom], sib)
    swap_gb = sems.remote(GB.at[top], GB.at[bottom], sib)
    back_bo = Exchange(place, sems, bo, bo_out)
    back_tg = Exchange(place, sems, tg, tg_out)
    rf, ra = [], []
    if weights:
        for i, (cols, first) in enumerate(REDUCE_F):
            rf.append(Reduce(place, sems, GF, cols, first, lands[3 * i : 3 * i + 3], sums, D + cols[0], R))
        for i, (cols, first) in enumerate(REDUCE_A, len(REDUCE_F)):
            ra.append(Reduce(place, sems, GA, cols, first, lands[3 * i : 3 * i + 3], sums, cols[0], R))

    def serve(parts, s):
        for part in parts:
            part.stage(s)

    get_ln2 = fetch(ln2, LN2.at[top])

    def feed(WFv, cinv, midv, gate, up, act, gh, out, XT):
        w0 = nlocal[0]
        nlocal[0] += 2

        def get_w(t, start, size):
            slot = lax.rem(t, 2)
            return pltpu.make_async_copy(
                WF.at[t, :, pl.ds(start, size)], WFv.at[slot, :, pl.ds(0, size)], local.at[w0 + slot]
            )

        def through(body, start, size, init):
            def step(t, c):
                get_w(t, start, size).wait()
                c = body(t, lax.rem(t, 2), c)

                @pl.when(t + 2 < T)
                def _():
                    get_w(t + 2, start, size).start()

                return c

            return lax.fori_loop(0, T, step, init)

        def ahead(start, size):
            for t in range(2):
                get_w(t, start, size).start()

        ahead(0, 2 * Hd)
        get_c = fetch(cin, cinv)
        get_mid = fetch(mid, midv)
        get_ln2.wait()

        def one(t, slot, c):
            s0, s1 = c
            gu = dot(LN2[top, :], WFv[slot])
            g, u = gu[:, :Hd], gu[:, Hd:]
            a = g * jax.nn.sigmoid(g) * u
            gate[t] = g.astype(gate.dtype)
            up[t] = u.astype(up.dtype)
            act[t] = a
            return s0 + jnp.sum(a, axis=1, keepdims=True), s1 + jnp.sum(a * a, axis=1, keepdims=True)

        z = jnp.zeros((n, 1), f32)
        s0, s1 = through(one, 0, 2 * Hd, (z, z))
        ahead(2 * Hd, Hd)
        width = T * Hd
        mean = s0 / width
        inv = lax.rsqrt(s1 / width - mean * mean + EPS)
        get_c.wait()
        spread(cinv, out)
        CT[top, :] = out[...].astype(bf)
        heard(partners)
        swap_ct.start()
        swap_ln2.start()
        get_mid.wait()
        out[...] = midv[...]

        def two(t, slot, c):
            r0, r1 = c
            n3 = (act[t] - mean) * inv
            act[t] = n3
            gt = ig[t, 0:1, :]
            hid = (n3 * gt + ig[t, 1:2, :]).astype(bf)
            XT[t, :, 2 * Hd : 3 * Hd] = hid
            out[...] += dot_t(hid, WFv[slot, :, 0:Hd])
            h = dot(CT[top, :], WFv[slot, :, 0:Hd])
            SM[0, pl.ds(8 + 2 * t, 1), 0:Hd] = jnp.sum(h * n3, axis=0, keepdims=True)
            SM[0, pl.ds(9 + 2 * t, 1), 0:Hd] = jnp.sum(h, axis=0, keepdims=True)
            e = h * gt
            gh[t] = e
            return r0 + jnp.sum(e, axis=1, keepdims=True), r1 + jnp.sum(e * n3, axis=1, keepdims=True)

        SM[0] = jnp.zeros(SM.shape[1:], f32)
        r0, r1 = through(two, 2 * Hd, Hd, (z, z))
        ahead(0, 2 * Hd)
        r0, r1 = r0 / width, r1 / width
        hidden_cols = pl.ds(2 * Hd, Hd)
        swap_h = [
            sems.remote(XT.at[2 * u + 1 - low, :, hidden_cols], XO.at[u, :, hidden_cols], sib) for u in range(H)
        ]
        for copy in swap_h:
            copy.start()
        for j in range(J):
            bo[j] = out[j * r : (j + 1) * r, :].astype(bf)
        back_bo.start()
        swap_ct.wait_recv()
        swap_ln2.wait_recv()

        def shrink_grad(u, _):
            t = 2 * u + low
            d = dot_l(CT[top, :], XT[t, :, 2 * Hd : 3 * Hd]) + dot_l(CT[bottom, :], XO[u, :, 2 * Hd : 3 * Hd])
            GF[u, :, 2 * Hd : 3 * Hd] = d.astype(bf)
            return 0

        for copy in swap_h:
            copy.wait_recv()
        lax.fori_loop(0, H, shrink_grad, 0)
        serve(rf[:2], 0)
        gln2 = out
        gln2[...] = jnp.zeros(gln2.shape, f32)

        def three(t, slot, _):
            ga = inv * (gh[t] - r0 - act[t] * r1)
            g, u = gate[t].astype(f32), up[t].astype(f32)
            s = jax.nn.sigmoid(g)
            gg = (ga * u * s * (1.0 + g * (1.0 - s))).astype(bf)
            gu = (ga * g * s).astype(bf)
            XT[t, :, 0:Hd] = gg
            XT[t, :, Hd : 2 * Hd] = gu
            gln2[...] += dot_t(XT[t, :, 0 : 2 * Hd], WFv[slot])
            return 0

        through(three, 0, 2 * Hd, 0)
        both_cols = pl.ds(0, 2 * Hd)
        swap_g = [
            sems.remote(XT.at[2 * u + 1 - low, :, both_cols], XO.at[u, :, both_cols], sib) for u in range(H)
        ]
        for copy in swap_g:
            copy.start()
        norm_back(midv, gln2, gains[2:3, :], CT, gmid, SM.at[0], 2, GB)
        swap_gb.start()
        serve(rf[:2], 1)
        for copy in swap_g:
            copy.wait_recv()

        def expand_grad(i, _):
            u = lax.div(i, 2)
            t = 2 * u + low
            c = pl.ds(pl.multiple_of(lax.rem(i, 2) * Hd, Hd), Hd)
            d = dot_l(LN2[top, :], XT[t, :, c]) + dot_l(LN2[bottom, :], XO[u, :, c])
            GF[u, :, c] = d.astype(bf)
            return 0

        lax.fori_loop(0, 2 * H, expand_grad, 0)
        serve(rf[2:], 0)
        for copy in swap_h + swap_g:
            copy.wait_send()
        pl.semaphore_signal(free, inc=1, device_id=sib, device_id_type=MESH)

    pl.run_scoped(
        feed,
        pltpu.VMEM((2, D, 2 * Hd), bf),
        pltpu.VMEM((J, r, D), bf),
        pltpu.VMEM((n, D), f32),
        pltpu.VMEM((T, n, Hd), bf),
        pltpu.VMEM((T, n, Hd), bf),
        pltpu.VMEM((T, n, Hd), f32),
        pltpu.VMEM((T, n, Hd), f32),
        pltpu.VMEM((n, D), f32),
        pltpu.VMEM((T, n, 3 * Hd), bf),
    )
    serve(rf[:2], 2)

    def attend(qv, Kv, Vv, lv, av, Wmv, gatt, dq, dK, dV, sK, sV):
        gets = [fetch(a, b) for a, b in ((Wm, Wmv), (att, av), (linv, lv), (q, qv), (K, Kv), (V, Vv))]
        half = (D // 256) * 128
        cuts = [pl.ds(0, half), pl.ds(half, D - half)]
        give = [
            [sems.remote(S.at[:, cut], XO.at[0, :, pl.ds(off + cut.start, cut.size)], sib) for off, S in ((0, sK), (D, sV))]
            for cut in cuts
        ]
        e0 = nlocal[0]
        nlocal[0] += 2

        def pairs(Es):
            def get_e(p, slot):
                return pltpu.make_async_copy(E.at[pl.ds(2 * p, 2)], Es.at[slot], local.at[e0 + slot])

            for p in range(2):
                get_e(p, p).start()
            for copy in gets:
                copy.wait()
            gatt[...] = dot(GB[top, :], Wmv[...]).astype(bf)

            def pair(p, _):
                for k, (parts, s) in {
                    0: (rf[:2], 3), 2: (rf[2:4], 1), 3: (rf[4:], 1), 4: (rf[2:4], 2), 5: (rf[4:], 2)
                }.items():
                    if parts:

                        @pl.when(p == k)
                        def _(parts=parts, s=s):
                            serve(parts, s)

                slot = lax.rem(p, 2)
                get_e(p, slot).wait()
                c = pl.ds(pl.multiple_of(p * 128, 128), 128)
                k2, v2, q2 = Kv[:, c], Vv[:, c], qv[:, c]
                dob = (gatt[:, c].astype(f32) * lv[:, c]).astype(bf)
                dl = dob.astype(f32) * av[:, c].astype(f32)
                m = 2 * n
                dqv = dkv = dvv = None
                for a in (0, 1):
                    ka = jnp.where(lanes(m, a), k2, jnp.zeros_like(k2))
                    va = jnp.where(lanes(m, a), v2, jnp.zeros_like(v2))
                    qa = jnp.where(lanes(n, a), q2, jnp.zeros_like(q2))
                    da = jnp.where(lanes(n, a), dob, jnp.zeros_like(dob))
                    delta = jnp.sum(jnp.where(lanes(n, a), dl, 0.0), axis=1, keepdims=True)
                    e = Es[slot, a]
                    dS = (e.astype(f32) * (dot_t(dob, va) - delta)).astype(bf)
                    x1, x2, x3 = dot(dS, ka), dot_l(dS, qa), dot_l(e, da)
                    dqv = x1 if a == 0 else dqv + x1
                    dkv = x2 if a == 0 else dkv + x2
                    dvv = x3 if a == 0 else dvv + x3
                dq[:, c] = dqv * 0.125
                dK[:, c] = dkv[:n]
                dV[:, c] = dvv[:n]
                sK[:, c] = dkv[n:].astype(bf)
                sV[:, c] = dvv[n:].astype(bf)

                @pl.when(p + 2 < D // 128)
                def _():
                    get_e(p + 2, slot).start()

                @pl.when(p == half // 128 - 1)
                def _():
                    pl.semaphore_wait(free, 1)
                    for copy in give[0]:
                        copy.start()

                return 0

            lax.fori_loop(0, D // 128, pair, 0)

        pl.run_scoped(pairs, pltpu.VMEM((2, 2, n, 2 * n), bf))
        for copy in give[1]:
            copy.start()

        def final(XT, LN1, Wqv, Wkv, Wvv, xv):
            gln1, tok = dK, dq
            late = [fetch(a, b) for a, b in ((Wq, Wqv), (Wk, Wkv), (Wv, Wvv), (ln1, LN1), (x, xv))]
            for group in give:
                for copy in group:
                    copy.wait_recv()
            Gq, Gk, Gv = gatt, qv, Kv

            def rows(i, _):
                p = pl.ds(pl.multiple_of(i * 48, 48), 48)
                co, si, sj = cos[p, :], -sa[p, :], -sb[p, :]
                g_q = turn(dq[p, :], co, si, sj)
                g_k = turn(dK[p, :] + XO[0, p, 0:D].astype(f32), co, si, sj)
                g_v = dV[p, :] + XO[0, p, D : 2 * D].astype(f32)
                Gq[p, :] = g_q.astype(bf)
                Gk[p, :] = g_k.astype(bf)
                Gv[p, :] = g_v.astype(bf)
                split = [own_and_other(v, low, H) for v in (g_q, g_k, g_v, av[p, :].astype(f32))]
                for u in range(H):
                    for side in (0, 1):
                        XT[side, u, p, :] = jnp.concatenate([z[side][u] for z in split], axis=1).astype(bf)
                return 0

            lax.fori_loop(0, n // 48, rows, 0)
            swap_a = [sems.remote(XT.at[1, u], XO.at[1, :, pl.ds(u * D, D)], sib) for u in range(H)]
            for copy in swap_a:
                copy.start()
            for copy in late:
                copy.wait()
            gln1[...] = dot_t(Gq[...], Wqv[...])
            gln1[...] += dot_t(Gk[...], Wkv[...])
            gln1[...] += dot_t(Gv[top, :], Wvv[...])
            for copy in swap_a + [swap_gb]:
                copy.wait_recv()
            w = D // T
            for u in range(H):
                o = XO[1, :, u * D : (u + 1) * D]
                m = XT[0, u]
                d = dot_l(LN1[top, :], m[:, : 3 * w]) + dot_l(LN1[bottom, :], o[:, : 3 * w])
                e = dot_l(GB[top, :], m[:, 3 * w :]) + dot_l(GB[bottom, :], o[:, 3 * w :])
                GA[u] = jnp.concatenate([d, e], axis=1).astype(bf)
            serve(ra, 0)
            serve(rf[2:], 3)
            norm_back(xv, gln1, gains[0:1, :], gmid, tok, SM.at[0], 0)
            for j in range(J):
                tg[j] = tok[j * r : (j + 1) * r, :].astype(bf)
            back_tg.start()
            at = 0
            hops = [[sib], [place.at_y(k) for k in range(1, H)], [place.at_x(k) for k in range(1, F)], [place.at_z(k) for k in range(1, C)]]
            for s, devices in enumerate(hops):
                copies = []
                for device in devices:
                    copies.append(sems.remote(SM.at[s], SML.at[at], device))
                    copies[-1].start()
                    at += 1
                if s > 0:
                    serve(ra, s)
                total = SM[s]
                for i, copy in enumerate(copies):
                    copy.wait_recv()
                    total = total + SML[at - len(copies) + i]
                for copy in copies:
                    copy.wait_send()
                if s + 1 < len(hops):
                    SM[s + 1] = total
                else:
                    small[...] = total
            for copy in swap_a:
                copy.wait_send()

        pl.run_scoped(
            final, pltpu.VMEM((2, H, n, D), bf), pltpu.VMEM((2 * n, D), bf), *[pltpu.VMEM((D, D), bf)] * 3, pltpu.VMEM((n, D), f32)
        )
        for group in give:
            for copy in group:
                copy.wait_send()

    pl.run_scoped(
        attend,
        pltpu.VMEM((n, D), bf),
        pltpu.VMEM((2 * n, D), bf),
        pltpu.VMEM((2 * n, D), bf),
        pltpu.VMEM((n, D), f32),
        pltpu.VMEM((n, D), bf),
        pltpu.VMEM((D, D), bf),
        pltpu.VMEM((n, D), bf),
        *[pltpu.VMEM((n, D), f32)] * 3,
        *[pltpu.VMEM((n, D), bf)] * 2,
    )
    for part in rf + ra:
        part.settle()
    for back in (back_bo, back_tg):
        back.wait()
        back.finish()
    for copy in (swap_ln2, swap_ct, swap_gb):
        copy.wait_send()


def backward_call(F, C, T, R, weights, shape, saved, ig, gains, cos, sa, sb):
    J, r, D = shape
    H, Hd = T // 2, ig.shape[2]
    n = cos.shape[0]
    heads = D // T
    outs = [(shape, bf), (shape, bf), ((R, 4 * heads + 3 * Hd), f32), ((16, D), f32)]
    grads = [((H, D, 3 * Hd), bf), ((H, D, D), bf)]
    out_specs = [HBM, HBM, VMEM, VMEM]
    if not weights:
        outs += grads
        out_specs += [VMEM, VMEM]
    small = (8, 128)
    scratch = [((2 * n, D), bf)] * 3 + [((H, n, 3 * Hd), bf), ((n, D), f32), (shape, bf), (shape, bf)]
    scratch += [((4, 16, D), f32), ((H + F + C - 2, 16, D), f32)]
    scratch += grads if weights else [(small, bf)] * 2
    scratch = [pltpu.VMEM(s, d) for s, d in scratch]
    scratch += [
        pltpu.SemaphoreType.DMA((128,)),
        pltpu.SemaphoreType.DMA((128,)),
        pltpu.SemaphoreType.DMA((32,)),
        pltpu.SemaphoreType.REGULAR,
    ]
    if weights:
        scratch += reduce_lands(REDUCE_F + REDUCE_A, F, C, H, D, R)
    return pl.pallas_call(
        functools.partial(backward_kernel, F, C, T, R, weights),
        out_shape=[jax.ShapeDtypeStruct(s, d) for s, d in outs],
        in_specs=[HBM] * len(saved) + [VMEM] * 5,
        out_specs=out_specs,
        scratch_shapes=scratch,
        compiler_params=pltpu.CompilerParams(collective_id=2, has_side_effects=True, vmem_limit_bytes=LIMIT),
    )(*saved, ig, gains, cos, sa, sb)

def moments(gradient, moment, square):
    moment = BETA_ONE * moment + (1.0 - BETA_ONE) * gradient
    square = BETA_TWO * square + (1.0 - BETA_TWO) * gradient * gradient
    update = (
        moment / (1.0 - BETA_ONE**STEP) / (jnp.sqrt(square / (1.0 - BETA_TWO**STEP)) + EPS_ADAM)
    )
    return (moment, square, update)


def body(
    F, C, T,
    tokens, cotangent, layer_gains, layer_first, layer_second, inner_gains, inner_first, inner_second,
    attend_weight, attend_first, attend_second, merge_weight, merge_first, merge_second,
    expand_weight, expand_first, expand_second, shrink_weight, shrink_first, shrink_second,
):
    bf, f32 = jnp.bfloat16, jnp.float32
    D = tokens.shape[-1]
    R = attend_weight.shape[1]
    rows = tokens.shape[1]
    J = C * T // 2
    assert J == tokens.shape[0]
    n = -(-J * rows // 48) * 48
    heads = attend_weight.shape[2]
    hidden = expand_weight.shape[2]
    fast = R % 16 == 0
    low = lax.axis_index("tp") % 2
    slots = jnp.arange(J, dtype=jnp.int32) * 2
    cos, sa, sb = rotary_tables(slots + low, rows, n)
    bias = jnp.concatenate([key_bias(slots + low, rows, n), key_bias(slots + 1 - low, rows, n)])[None]
    pack_a = jnp.concatenate([attend_weight[0], attend_weight[1], attend_weight[2], merge_weight.T], axis=1).astype(bf)
    pack_f = jnp.concatenate([expand_weight[0], expand_weight[1], shrink_weight.T], axis=1).astype(bf)
    if not fast:
        pack_a, pack_f = (
            lax.all_gather(lax.all_gather(p, ("fsdp", "ctx"), axis=0, tiled=True), "tp", axis=0)
            for p in (pack_a, pack_f)
        )
    inner_all = lax.all_gather(inner_gains, "tp", axis=0)
    cin, WF, x, ln1, q, K, V, Wq, Wk, Wv, Wm, E, linv, att, mid, ln2 = forward_call(
        F, C, T, n, tokens, cotangent, pack_a, pack_f, layer_gains, cos, sa, sb, bias
    )
    if not fast:
        WF = pack_f
    saved = (cin, WF, ln2, mid, x, ln1, q, K, V, Wq, Wk, Wv, Wm, E, linv, att)
    out = backward_call(F, C, T, R, fast, tokens.shape, saved, inner_all, layer_gains, cos, sa, sb)
    block_output, token_gradient, sums, small = out[:4]
    if not fast:
        sums = jnp.concatenate([out[5], out[4]], axis=2).astype(f32)
        same = [[t for t in range(T) if t % 2 == k] for k in range(2)]
        sums = lax.psum_scatter(sums, "tp", scatter_dimension=0, axis_index_groups=same, tiled=False)
        sums = lax.psum_scatter(sums, ("fsdp", "ctx"), scatter_dimension=0, tiled=True)
    token_gradient = token_gradient.astype(f32)
    a = sums[:, : 4 * heads]
    attend_sum = jnp.stack([a[:, i * heads : (i + 1) * heads] for i in range(3)])
    merge_sum = a[:, 3 * heads :].T
    b = sums[:, 4 * heads :]
    expand_sum = jnp.stack([b[:, i * hidden : (i + 1) * hidden] for i in range(2)])
    shrink_sum = b[:, 2 * hidden :].T
    layer_grad = small[:4]
    inner_grad = lax.dynamic_slice(small, (8 + 2 * lax.axis_index("tp"), 0), (2, hidden))
    matrices = (
        (attend_weight, attend_sum, attend_first, attend_second),
        (merge_weight, merge_sum, merge_first, merge_second),
        (expand_weight, expand_sum, expand_first, expand_second),
        (shrink_weight, shrink_sum, shrink_first, shrink_second),
    )
    states = []
    weight_terms = []
    update_terms = []
    for weight, gradient, moment, square in matrices:
        moment_new, square_new, update = moments(gradient, moment, square)
        update = update + DECAY * weight
        states.append((moment_new, square_new, update))
        weight_terms.append(jnp.sum(weight * weight))
        update_terms.append(jnp.sum(update * update))
    weight_sums, update_sums = lax.psum(
        (jnp.stack(weight_terms), jnp.stack(update_terms)), ("fsdp", "ctx", "tp")
    )
    weight_norms = jnp.sqrt(weight_sums)
    update_norms = jnp.sqrt(update_sums)
    updated = []
    for number in range(4):
        ratio = weight_norms[number] / update_norms[number]
        updated.append(matrices[number][0] - RATE * ratio * states[number][2])
    layer_moment, layer_square, layer_step = moments(layer_grad, layer_first, layer_second)
    inner_moment, inner_square, inner_step = moments(inner_grad, inner_first, inner_second)
    trust_norms = jnp.stack([weight_norms, update_norms], axis=1)
    return (
        block_output, token_gradient,
        updated[0], states[0][0], states[0][1],
        updated[1], states[1][0], states[1][1],
        updated[2], states[2][0], states[2][1],
        updated[3], states[3][0], states[3][1],
        layer_gains - RATE_GAINS * layer_step, layer_moment, layer_square,
        inner_gains - RATE_GAINS * inner_step, inner_moment, inner_square,
        trust_norms,
    )


def solution(mesh):
    tok = P("fsdp", ("ctx", "tp"), None)
    wide = P(None, ("fsdp", "ctx"), "tp")
    tall = P("tp", ("fsdp", "ctx"))
    split = P(None, "tp")
    sizes = (mesh.shape["fsdp"], mesh.shape["ctx"], mesh.shape["tp"])
    return jax.shard_map(
        functools.partial(body, *sizes),
        mesh=mesh,
        in_specs=(tok, tok, P(), P(), P(), split, split, split)
        + (wide,) * 3 + (tall,) * 3 + (wide,) * 3 + (tall,) * 3,
        out_specs=(tok, tok) + (wide,) * 3 + (tall,) * 3 + (wide,) * 3 + (tall,) * 3
        + (P(),) * 3 + (split,) * 3 + (P(),),
        check_vma=False,
    )
```

```python
import functools
import jax
import jax.numpy as jnp
from jax import lax
from jax.experimental import pallas as pl
from jax.experimental.pallas import tpu as pltpu
from jax.sharding import PartitionSpec as P

HD = 64
GRID = 32
STEP = 5
VALID = 1025
BETA_ONE = 0.5
BETA_TWO = 0.5
EPS_ADAM = 1e-06
DECAY = 0.01
RATE = 0.5
RATE_GAINS = 0.3
MESH = pl.DeviceIdType.MESH
f32 = jnp.float32
bf = jnp.bfloat16


class Place:
    def __init__(self, F, C, T):
        self.F, self.C, self.T, self.H = F, C, T, T // 2
        self.f = lax.axis_index("fsdp")
        self.c = lax.axis_index("ctx")
        self.t = lax.axis_index("tp")
        self.low = lax.rem(self.t, 2)
        self.high = lax.div(self.t, 2)
        self.pair = self.c * self.H + self.high
        self.pairs = C * self.H
        self.sibling = {"tp": self.t + 1 - 2 * self.low}
        self.xs = [lax.rem(self.f + k, F) for k in range(F)]
        self.ys = [lax.rem(self.high + k, self.H) for k in range(self.H)]
        self.zs = [lax.rem(self.c + k, C) for k in range(C)]

    def at_x(self, k):
        return {"fsdp": self.xs[k]}

    def at_y(self, k):
        return {"tp": self.ys[k] * 2 + self.low}

    def at_z(self, k):
        return {"ctx": self.zs[k]}

    def pair_at(self, k):
        i = lax.rem(self.pair + k, self.pairs)
        return i, {"ctx": lax.div(i, self.H), "tp": lax.rem(i, self.H) * 2 + self.low}

    def tees(self):
        return [{"tp": lax.rem(self.t + k, self.T)} for k in range(1, self.T)]

    def partners(self, with_x):
        out = self.tees() + [
            {"ctx": self.zs[c], "tp": self.ys[y] * 2 + self.low} for c in range(1, self.C) for y in range(self.H)
        ]
        if with_x:
            out += [self.at_x(k) for k in range(1, self.F)]
        return out


def hail(partners):
    barrier = pltpu.get_barrier_semaphore()
    for partner in partners:
        pl.semaphore_signal(barrier, inc=1, device_id=partner, device_id_type=MESH)


def heard(partners):
    pl.semaphore_wait(pltpu.get_barrier_semaphore(), len(partners))


class Sems:
    def __init__(self, send, recv):
        self.send, self.recv, self.n = send, recv, 0

    def remote(self, src, dst, device):
        i = self.n
        self.n += 1
        return pltpu.make_async_remote_copy(
            src, dst, self.send.at[i], self.recv.at[i], device_id=device, device_id_type=MESH
        )

    def local(self, src, dst):
        i = self.n
        self.n += 1
        return pltpu.make_async_copy(src, dst, self.send.at[i])


class Exchange:
    def __init__(self, place, sems, src, dst):
        self.own = sems.local(src.at[place.pair], dst.at[place.pair])
        self.copies = []
        for k in range(1, place.pairs):
            i, device = place.pair_at(k)
            self.copies.append(sems.remote(src.at[i], dst.at[place.pair], device))

    def start(self):
        self.own.start()
        for copy in self.copies:
            copy.start()

    def wait(self):
        self.own.wait()
        for copy in self.copies:
            copy.wait_recv()

    def finish(self):
        for copy in self.copies:
            copy.wait_send()


class Gather:
    def __init__(self, place, sems, pack, whole, cols, first):
        P, R = place, pack.shape[0]
        C, F, H = P.C, P.F, P.H
        n = C * R
        window = pl.ds(*cols)

        def push(t, row, rows, device):
            block = whole.at[t, pl.ds(pl.multiple_of(row, 16), rows), window]
            return sems.remote(block, block, device)

        row = (P.f * C + P.c) * R
        base = P.f * n
        self.own = sems.local(
            pack.at[:, window], whole.at[P.t, pl.ds(pl.multiple_of(row, 16), R), window]
        )
        along_z = [push(P.t, row, R, P.at_z(k)) for k in range(1, C)]
        tees = [y * 2 + P.low for y in P.ys]
        if first == "y":
            second = [push(P.t, base, n, P.at_y(k)) for k in range(1, H)]
            third = [push(t, base, n, P.at_x(k)) for k in range(1, F) for t in tees]
            over_3 = [push(t, base, n, P.sibling) for t in tees[1:]]
            over_4 = [push(t, P.xs[k] * n, n, P.sibling) for k in range(1, F) for t in tees]
        else:
            second = [push(P.t, base, n, P.at_x(k)) for k in range(1, F)]
            third = [push(P.t, 0, n * F, P.at_y(k)) for k in range(1, H)]
            over_3 = [push(P.t, P.xs[k] * n, n, P.sibling) for k in range(1, F)]
            over_4 = [push(t, 0, n * F, P.sibling) for t in tees[1:]]
        over_2 = [push(P.t, base, n, P.sibling)]
        self.waits = [[], along_z, second, third]
        self.starts = [along_z, second + over_2, third + over_3, over_4]
        self.sent_over = over_2 + over_3 + over_4

    def stage(self, s):
        if s == 0:
            self.own.wait()
        for copy in self.waits[s]:
            copy.wait_recv()
        for copy in self.starts[s]:
            copy.start()

    def finish(self):
        for copy in self.sent_over:
            copy.wait_recv()

    def settle(self):
        for group in self.starts:
            for copy in group:
                copy.wait_send()


def by_rows(rows, step, body):
    def it(i, _):
        body(pl.multiple_of(i * step, step), step)
        return 0

    lax.fori_loop(0, rows // step, it, 0)


class Reduce:
    def __init__(self, place, sems, G, cols, first, lands, out, out_col, R):
        P, n = place, place.C * R
        C, F, H, D = P.C, P.F, P.H, G.shape[1]
        window = pl.ds(*cols)
        L1, L2, L3 = lands
        self.out, self.to, self.R = out, pl.ds(out_col, cols[1]), R
        base = pl.multiple_of(P.f * n, 16)
        mine = pl.multiple_of(base + P.c * R, 16)
        self.copies = [[], [], []]

        def rows(u, start, count):
            return G.at[u, pl.ds(start, count), window]

        def send(stage, src, dst, device):
            self.copies[stage].append(sems.remote(src, dst, device))

        if first == "x":
            for k in range(1, F):
                for u in range(H):
                    send(0, rows(u, pl.multiple_of(P.xs[k] * n, 16), n), L1.at[k - 1, u], P.at_x(k))
            for k in range(1, H):
                send(1, rows(P.ys[k], base, n), L2.at[k - 1], P.at_y(k))
            self.adds = [
                [(rows(u, base, n), [L1.at[k - 1, u] for k in range(1, F)]) for u in range(H)],
                [(rows(P.high, base, n), [L2.at[k - 1] for k in range(1, H)])],
            ]
        else:
            for k in range(1, H):
                send(0, rows(P.ys[k], 0, D), L1.at[k - 1], P.at_y(k))
            for k in range(1, F):
                send(1, rows(P.high, pl.multiple_of(P.xs[k] * n, 16), n), L2.at[k - 1], P.at_x(k))
            self.adds = [
                [(rows(P.high, 0, D), [L1.at[k - 1] for k in range(1, H)])],
                [(rows(P.high, base, n), [L2.at[k - 1] for k in range(1, F)])],
            ]
        for k in range(1, C):
            send(2, rows(P.high, pl.multiple_of(base + P.zs[k] * R, 16), R), L3.at[k - 1], P.at_z(k))
        self.last = (rows(P.high, mine, R), [L3.at[k - 1] for k in range(1, C)])

    def stage(self, s):
        if s > 0:
            for copy in self.copies[s - 1]:
                copy.wait_recv()
        if s in (1, 2):
            for dst, lands in self.adds[s - 1]:

                def add(r, k, dst=dst, lands=lands):
                    v = dst[pl.ds(r, k), :].astype(f32)
                    for land in lands:
                        v = v + land[pl.ds(r, k), :].astype(f32)
                    dst[pl.ds(r, k), :] = v.astype(bf)

                by_rows(dst.shape[0], 96, add)
        if s == 3:
            dst, lands = self.last
            v = dst[...].astype(f32)
            for land in lands:
                v = v + land[...].astype(f32)
            self.out[:, self.to] = v
        else:
            for copy in self.copies[s]:
                copy.start()

    def settle(self):
        for group in self.copies:
            for copy in group:
                copy.wait_send()


def reduce_lands(parts, F, C, H, D, R):
    out = []
    for (_, n), first in parts:
        if first == "x":
            out += [(F - 1, H, C * R, n), (H - 1, C * R, n)]
        else:
            out += [(H - 1, D, n), (F - 1, C * R, n)]
        out.append((C - 1, R, n))
    return [pltpu.VMEM(s, bf) for s in out]
EPS=1e-6
def dot(a,b): return jnp.dot(a,b,preferred_element_type=f32)
def dot_t(a,b): return lax.dot_general(a,b,(((1,),(1,)),((),())),preferred_element_type=f32)
def dot_l(a,b): return lax.dot_general(a,b,(((0,),(0,)),((),())),preferred_element_type=f32)

def chunks(rows, step, body):
    def it(i,_):
        body(pl.ds(pl.multiple_of(i*step,step),step)); return 0
    lax.fori_loop(0,rows//step,it,0)

def norm(v):
    mean=jnp.mean(v,axis=-1,keepdims=True)
    var=jnp.mean(v*v,axis=-1,keepdims=True)-mean*mean
    inv=lax.rsqrt(var+EPS)
    return (v-mean)*inv, inv

def spread(src3, dst):
    J,r,D=src3.shape
    n=dst.shape[0]
    pad=n-J*r
    if pad: dst[n-16:n,:]=jnp.zeros((16,D),f32)
    for j in range(J):
        dst[j*r:(j+1)*r,:]=src3[j].astype(f32)

def join(WA, g, dst, T):
    w=WA.shape[2]//4
    def it(i,_):
        s=pl.ds(pl.multiple_of(i*96,96),96)
        row=jnp.concatenate([WA[t,s,g*w:(g+1)*w] for t in range(T)],axis=1)
        dst[s,:]=row
        return 0
    lax.fori_loop(0,WA.shape[1]//96,it,0)

def part(src, GA, g, T):
    w=GA.shape[2]//4
    def it(i,_):
        s=pl.ds(pl.multiple_of(i*96,96),96)
        v=src[s,:]
        for t in range(T):
            GA[t,s,g*w:(g+1)*w]=v[:,t*w:(t+1)*w].astype(bf)
        return 0
    lax.fori_loop(0,GA.shape[1]//96,it,0)

def turn(v, cos, sa, sb):
    n=v.shape[1]
    out=[]
    for i in range(n//128):
        a=v[:,i*128:(i+1)*128]
        out.append(a*cos+pltpu.roll(a,128-16,1)*sa+pltpu.roll(a,16,1)*sb)
    return jnp.concatenate(out,axis=1)

def normal(x, gains, ln1):
    def ln(s):
        v,_=norm(x[s,:])
        ln1[s,:]=(v*gains[0:1,:]+gains[1:2,:]).astype(bf)
    chunks(x.shape[0],48,ln)


def project(ln1, W, cos, sa, sb, dst, scale=None):
    n=ln1.shape[0]//2
    y=dot(ln1[0:n,:],W[...])
    if cos is not None: y=turn(y,cos[...],sa[...],sb[...])
    if scale is not None: y=y*scale
    dst[0:n,:]=y.astype(bf)


def lanes(n, a):
    return (lax.broadcasted_iota(jnp.int32,(n,128),1)//64==a)

def attention(q,K,V,bias,E,linv,att,service):
    n=q.shape[0]; m=K.shape[0]
    def pair(p,_):
        service(p)
        c=pl.ds(pl.multiple_of(p*128,128),128)
        k2=K[:,c]; v2=V[:,c]
        q2=q[:,c]
        o=None; li=[]
        for a in (0,1):
            ka=jnp.where(lanes(m,a),k2,jnp.zeros_like(k2))
            va=jnp.where(lanes(m,a),v2,jnp.zeros_like(v2))
            S=dot_t(q2,ka)+bias[0:1,:]
            mx=jnp.max(S,axis=1,keepdims=True)
            e=jnp.exp(S-mx)
            l=1.0/jnp.sum(e,axis=1,keepdims=True)
            eb=e.astype(bf)
            E[2*p+a]=eb
            oa=dot(eb,va)*l
            o=oa if o is None else o+oa
            li.append(l)
        att[:,c]=o.astype(bf)
        linv[:,c]=jnp.where(lanes(n,0),li[0],li[1])
        return 0
    lax.fori_loop(0,q.shape[1]//128,pair,0)

def merge(att,Wm,x,mid,gains,ln2):
    mid[...]=x[...]+dot_t(att[...],Wm[...])
    def ln(s):
        v,_=norm(mid[s,:])
        ln2[s,:]=(v*gains[2:3,:]+gains[3:4,:]).astype(bf)
    chunks(x.shape[0],48,ln)

def silu_parts(g):
    s=jax.nn.sigmoid(g)
    return s, g*s

def ffn(ln2,ln2T,cot,cotT,WF,mid,ig,gate,up,act,gh,stat,GF,inner,out,gln2,T):
    n=ln2.shape[0]; Hd=WF.shape[2]//3; FFN=T*Hd
    def one(t,c):
        s0,s1=c
        gu=dot(ln2[...],WF[t,:,0:2*Hd])
        g=gu[:,:Hd]; u=gu[:,Hd:]
        _,si=silu_parts(g)
        a=si*u
        gate[t]=g; up[t]=u; act[t]=a
        return s0+jnp.sum(a,axis=1,keepdims=True), s1+jnp.sum(a*a,axis=1,keepdims=True)
    z=jnp.zeros((n,1),f32)
    s0,s1=lax.fori_loop(0,T,one,(z,z))
    mean=s0/FFN; inv=lax.rsqrt(s1/FFN-mean*mean+EPS)
    out[...]=mid[...]
    def two(t,c):
        r0,r1=c
        n3=(act[t]-mean)*inv
        act[t]=n3
        gt=ig[t,0:1,:]
        hid=(n3*gt+ig[t,1:2,:]).astype(bf)
        out[...]+=dot_t(hid,WF[t,:,2*Hd:3*Hd])
        h=dot(cot[...],WF[t,:,2*Hd:3*Hd])
        GF[t,:,2*Hd:3*Hd]=dot(cotT[...],hid).astype(bf)
        inner[t,0:1,:]=jnp.sum(h*n3,axis=0,keepdims=True)
        inner[t,1:2,:]=jnp.sum(h,axis=0,keepdims=True)
        e=h*gt
        gh[t]=e
        return r0+jnp.sum(e,axis=1,keepdims=True), r1+jnp.sum(e*n3,axis=1,keepdims=True)
    r0,r1=lax.fori_loop(0,T,two,(z,z))
    r0=r0/FFN; r1=r1/FFN
    gln2[...]=jnp.zeros_like(gln2)
    def three(t,_):
        ga=inv*(gh[t]-r0-act[t]*r1)
        g=gate[t]; u=up[t]
        s,si=silu_parts(g)
        gg=(ga*u*s*(1.0+g*(1.0-s))).astype(bf)
        gu=(ga*si).astype(bf)
        both=jnp.concatenate([gg,gu],axis=1)
        GF[t,:,0:2*Hd]=dot(ln2T[...],both).astype(bf)
        gln2[...]+=dot_t(both,WF[t,:,0:2*Hd])
        return 0
    lax.fori_loop(0,T,three,0)

def norm_back(src, e_src, gain, add, dst, lay, row, dst16=None):
    n=src.shape[0]
    lay[row:row+2,:]=jnp.zeros((2,src.shape[1]),f32)
    def it(s):
        a,inv=norm(src[s,:]); e=e_src[s,:]
        lay[row:row+1,:]+=jnp.sum(e*a,axis=0,keepdims=True)
        lay[row+1:row+2,:]+=jnp.sum(e,axis=0,keepdims=True)
        eg=e*gain
        d=add[s,:].astype(f32)+inv*(eg-jnp.mean(eg,axis=1,keepdims=True)-a*jnp.mean(eg*a,axis=1,keepdims=True))
        dst[s,:]=d
        if dst16 is not None: dst16[s,:]=d.astype(bf)
    chunks(n,48,it)

def attention_back(q,K,V,E,linv,att,gatt,dq,dK,dV,step=528):
    n=q.shape[0]; m=K.shape[0]
    def pair(p,_):
        c=pl.ds(pl.multiple_of(p*128,128),128)
        k2=K[:,c]; v2=V[:,c]
        R=linv[:,c]
        do=gatt[:,c].astype(f32)*R
        dob=do.astype(bf)
        dl=dob.astype(f32)*att[:,c].astype(f32)
        q2=q[:,c]
        dqv=None; dkv=None; dvv=None
        for a in (0,1):
            ka=jnp.where(lanes(m,a),k2,jnp.zeros_like(k2))
            va=jnp.where(lanes(m,a),v2,jnp.zeros_like(v2))
            qa=jnp.where(lanes(n,a),q2,jnp.zeros_like(q2))
            da=jnp.where(lanes(n,a),dob,jnp.zeros_like(dob))
            delta=jnp.sum(jnp.where(lanes(n,a),dl,0.0),axis=1,keepdims=True)
            dP=dot_t(dob,va)
            e=E[2*p+a]
            dS=(e.astype(f32)*(dP-delta)).astype(bf)
            x=dot(dS,ka); y=dot_l(dS,qa); z=dot_l(e,da)
            dqv=x if dqv is None else dqv+x
            dkv=y if dkv is None else dkv+y
            dvv=z if dvv is None else dvv+z
        dq[:,c]=dqv*0.125
        dK[:,c]=dkv
        dV[:,c]=dvv
        return 0
    lax.fori_loop(0,q.shape[1]//128,pair,0)

VMEM = pl.BlockSpec(memory_space=pltpu.VMEM)
HBM = pl.BlockSpec(memory_space=pl.ANY)
LIMIT = 60 * 2**20


def local_call(body, ins, outs, scratch=(), flops=0):
    return pl.pallas_call(
        body,
        out_shape=[jax.ShapeDtypeStruct(s, d) for s, d in outs],
        in_specs=[VMEM] * len(ins),
        out_specs=[VMEM] * len(outs),
        scratch_shapes=[pltpu.VMEM(s, d) for s, d in scratch],
        compiler_params=pltpu.CompilerParams(vmem_limit_bytes=LIMIT),
    )(*ins)


def rotary_tables(slots, rows, total):
    quarter = HD // 4
    positions = (slots[:, None] * rows + jnp.arange(rows, dtype=jnp.int32)).reshape(-1)
    inside = (positions >= 1) & (positions <= GRID * GRID)
    patch = jnp.where(inside, positions - 1, 0)
    frequency = 10000.0 ** (-jnp.arange(quarter, dtype=jnp.float32) / quarter)
    row_angle = (patch // GRID).astype(jnp.float32)[:, None] * frequency
    column_angle = (patch % GRID).astype(jnp.float32)[:, None] * frequency
    angles = jnp.concatenate([row_angle, row_angle, column_angle, column_angle], axis=-1)
    angles = jnp.pad(angles, ((0, total - angles.shape[0]), (0, 0)))
    angles = jnp.concatenate([angles, angles], axis=-1)
    sine = jnp.sin(angles)
    first = (jnp.arange(2 * HD) // quarter) % 2 == 0
    return jnp.cos(angles), jnp.where(first, -sine, 0.0), jnp.where(first, 0.0, sine)


def key_bias(slots, rows, total):
    positions = (slots[:, None] * rows + jnp.arange(rows, dtype=jnp.int32)).reshape(-1)
    bias = jnp.where(positions < VALID, 0.0, -1e30).astype(jnp.float32)
    return jnp.pad(bias, (0, total - bias.shape[0]), constant_values=-1e30)


GATHER_A = (((0, 384), "y"), ((384, 384), "x"))
GATHER_F = (((0, 384), "y"), ((384, 384), "x"), ((768, 384), "y"), ((1152, 384), "x"))


def forward_kernel(
    F, C, T, weights,
    tok, cot, wa, wf, gains, cos, sa, sb, bias, inner,
    IG, cin, WF, x, ln1, q, K, V, Wq, Wk, Wv, Wm, E, linv, att, mid, ln2,
    tin, WA, send, recv, local,
):
    place = Place(F, C, T)
    sems = Sems(send, recv)
    partners = place.partners(weights)
    hail(partners)
    n = x.shape[0]
    tokens = Exchange(place, sems, tok, tin)
    cots = Exchange(place, sems, cot, cin)
    swap = [sems.remote(X.at[pl.ds(0, n)], X.at[pl.ds(n, n)], place.sibling) for X in (K, V, ln1)]
    share = [sems.remote(inner, IG.at[place.t], device) for device in place.tees()]
    if weights:
        ga = [Gather(place, sems, wa, WA, cols, first) for cols, first in GATHER_A]
        gf = [Gather(place, sems, wf, WF, cols, first) for cols, first in GATHER_F]
    else:
        ga, gf = [], []
        copy = pltpu.make_async_copy(wa, WA, local.at[0])
        copy.start()
        copy.wait()
    for g in ga + gf:
        g.own.start()
    heard(partners)
    IG[place.t] = inner[...]
    for s in range(3):
        for g in ga:
            g.stage(s)
        if s == 1:
            tokens.start()
    for copy in share:
        copy.start()
    tokens.wait()
    for g in gf[:2]:
        g.stage(0)
    spread(tin, x)
    normal(x, gains, ln1)
    swap[2].start()
    for g in ga:
        g.stage(3)
    for g in ga:
        g.finish()
    for i, W in enumerate((Wq, Wk, Wv, Wm)):
        join(WA, i, W, T)
    for g in gf[:2]:
        g.stage(1)
    for g in gf[2:]:
        g.stage(0)
    project(ln1, Wk, cos, sa, sb, K)
    swap[0].start()
    project(ln1, Wv, None, None, None, V)
    swap[1].start()
    for g in gf[:2]:
        g.stage(2)
    project(ln1, Wq, cos, sa, sb, q, 0.125)
    for copy in swap:
        copy.wait_recv()

    def service(p):
        if weights:

            @pl.when(p == 1)
            def _():
                for g in gf[2:]:
                    g.stage(1)
                cots.start()

            @pl.when(p == 2)
            def _():
                for g in gf[:2]:
                    g.stage(3)

            @pl.when(p == 3)
            def _():
                for g in gf[2:]:
                    g.stage(2)

            @pl.when(p == 5)
            def _():
                for g in gf[2:]:
                    g.stage(3)

        else:

            @pl.when(p == 1)
            def _():
                cots.start()

    attention(q, K, V, bias, E, linv, att, service)
    merge(att, Wm, x, mid, gains, ln2)
    cots.wait()
    for g in gf:
        g.finish()
    for g in ga + gf:
        g.settle()
    for copy in swap:
        copy.wait_send()
    for copy in share:
        copy.wait()
    tokens.finish()
    cots.finish()


def forward_call(F, C, T, n, tokens, cotangent, a, f, gains, cos, sa, sb, bias, inner):
    weights = a.ndim == 2
    D = tokens.shape[-1]
    J = C * T // 2
    nh = D // HD
    chunk = (J,) + tokens.shape[1:]
    whole_a = (T, D, a.shape[-1])
    whole_f = (T, D, f.shape[-1])
    outs = [((T,) + inner.shape, f32), (chunk, bf), (whole_f if weights else (8, 128), bf)]
    outs += [((n, D), f32), ((2 * n, D), bf), ((n, D), bf), ((2 * n, D), bf), ((2 * n, D), bf)]
    outs += [((D, D), bf)] * 4
    outs += [((nh, n, 2 * n), bf), ((n, D), f32), ((n, D), bf), ((n, D), f32), ((n, D), bf)]
    return pl.pallas_call(
        functools.partial(forward_kernel, F, C, T, weights),
        out_shape=[jax.ShapeDtypeStruct(s, d) for s, d in outs],
        in_specs=[HBM] * 4 + [VMEM] * 6,
        out_specs=[VMEM] + [HBM] * 2 + [VMEM] * (len(outs) - 3),
        scratch_shapes=[
            pltpu.VMEM(chunk, bf),
            pltpu.VMEM(whole_a, bf),
            pltpu.SemaphoreType.DMA((128,)),
            pltpu.SemaphoreType.DMA((128,)),
            pltpu.SemaphoreType.DMA((1,)),
        ],
        compiler_params=pltpu.CompilerParams(collective_id=1, has_side_effects=True, vmem_limit_bytes=LIMIT),
    )(tokens, cotangent, a, f, gains, cos, sa, sb, bias, inner)


REDUCE_F = (
    ((1024, 256), "x"), ((1280, 256), "y"),
    ((0, 256), "x"), ((256, 256), "y"), ((512, 256), "x"), ((768, 256), "y"),
)
REDUCE_A = (((0, 256), "x"), ((256, 256), "y"), ((512, 128), "x"), ((640, 128), "y"))


def own_and_other(v, low, H):
    w = v.shape[1] // (2 * H)
    mine, theirs = [], []
    for u in range(H):
        a, b = v[:, 2 * u * w : (2 * u + 1) * w], v[:, (2 * u + 1) * w : (2 * u + 2) * w]
        mine.append(jnp.where(low == 0, a, b))
        theirs.append(jnp.where(low == 0, b, a))
    return mine, theirs


def backward_kernel(
    F, C, T, R, weights,
    cin, WF, ln2, mid, x, ln1, q, K, V, Wq, Wk, Wv, Wm, E, linv, att, *rest,
):
    raw, rest = rest[:12], rest[12:]
    ig, gains, cos, sa, sb, bo_out, tg_out, sums, small, norms = rest[:10]
    rest = rest[10:]
    if weights:
        GF, GA = None, None
    else:
        GF, GA = rest[:2]
        rest = rest[2:]
    (LN2, CT, GB, XO, gmid, bo, tg, SM, SML, NV, NVL, GF_s, GA_s, send, recv, local, free) = rest[:17]
    if weights:
        GF, GA = GF_s, GA_s
    lands = rest[17:]
    place = Place(F, C, T)
    H, low, sib = place.H, place.low, place.sibling
    sems = Sems(send, recv)
    partners = place.partners(True)
    hail(partners)
    J, r, D = bo.shape
    n = gmid.shape[0]
    Hd = ig.shape[2]
    top, bottom = pl.ds(0, n), pl.ds(n, n)
    nlocal = [0]

    def fetch(src, dst):
        copy = pltpu.make_async_copy(src, dst, local.at[nlocal[0]])
        nlocal[0] += 1
        copy.start()
        return copy

    swap_ln2 = sems.remote(LN2.at[top], LN2.at[bottom], sib)
    swap_ct = sems.remote(CT.at[top], CT.at[bottom], sib)
    swap_gb = sems.remote(GB.at[top], GB.at[bottom], sib)
    back_bo = Exchange(place, sems, bo, bo_out)
    back_tg = Exchange(place, sems, tg, tg_out)
    rf, ra = [], []
    if weights:
        for i, (cols, first) in enumerate(REDUCE_F):
            rf.append(Reduce(place, sems, GF, cols, first, lands[3 * i : 3 * i + 3], sums, D + cols[0], R))
        for i, (cols, first) in enumerate(REDUCE_A, len(REDUCE_F)):
            ra.append(Reduce(place, sems, GA, cols, first, lands[3 * i : 3 * i + 3], sums, cols[0], R))

    def serve(parts, s):
        for part in parts:
            part.stage(s)

    get_ln2 = fetch(ln2, LN2.at[top])

    def feed(WFv, cinv, midv, gate, up, act, gh, out, XT):
        w0 = nlocal[0]
        nlocal[0] += 2

        def get_w(t, start, size):
            slot = lax.rem(t, 2)
            return pltpu.make_async_copy(
                WF.at[t, :, pl.ds(start, size)], WFv.at[slot, :, pl.ds(0, size)], local.at[w0 + slot]
            )

        def through(body, start, size, init):
            def step(t, c):
                get_w(t, start, size).wait()
                c = body(t, lax.rem(t, 2), c)

                @pl.when(t + 2 < T)
                def _():
                    get_w(t + 2, start, size).start()

                return c

            return lax.fori_loop(0, T, step, init)

        def ahead(start, size):
            for t in range(2):
                get_w(t, start, size).start()

        ahead(0, 2 * Hd)
        get_c = fetch(cin, cinv)
        get_mid = fetch(mid, midv)
        get_ln2.wait()

        def one(t, slot, c):
            s0, s1 = c
            gu = dot(LN2[top, :], WFv[slot])
            g, u = gu[:, :Hd], gu[:, Hd:]
            a = g * jax.nn.sigmoid(g) * u
            gate[t] = g.astype(gate.dtype)
            up[t] = u.astype(up.dtype)
            act[t] = a
            return s0 + jnp.sum(a, axis=1, keepdims=True), s1 + jnp.sum(a * a, axis=1, keepdims=True)

        z = jnp.zeros((n, 1), f32)
        s0, s1 = through(one, 0, 2 * Hd, (z, z))
        ahead(2 * Hd, Hd)
        width = T * Hd
        mean = s0 / width
        inv = lax.rsqrt(s1 / width - mean * mean + EPS)
        get_c.wait()
        spread(cinv, out)
        CT[top, :] = out[...].astype(bf)
        heard(partners)
        swap_ct.start()
        swap_ln2.start()
        get_mid.wait()
        out[...] = midv[...]

        def two(t, slot, c):
            r0, r1 = c
            n3 = (act[t] - mean) * inv
            act[t] = n3
            gt = ig[t, 0:1, :]
            hid = (n3 * gt + ig[t, 1:2, :]).astype(bf)
            XT[t, :, 2 * Hd : 3 * Hd] = hid
            out[...] += dot_t(hid, WFv[slot, :, 0:Hd])
            h = dot(CT[top, :], WFv[slot, :, 0:Hd])
            SM[0, pl.ds(8 + 2 * t, 1), 0:Hd] = jnp.sum(h * n3, axis=0, keepdims=True)
            SM[0, pl.ds(9 + 2 * t, 1), 0:Hd] = jnp.sum(h, axis=0, keepdims=True)
            e = h * gt
            gh[t] = e
            return r0 + jnp.sum(e, axis=1, keepdims=True), r1 + jnp.sum(e * n3, axis=1, keepdims=True)

        SM[0] = jnp.zeros(SM.shape[1:], f32)
        r0, r1 = through(two, 2 * Hd, Hd, (z, z))
        ahead(0, 2 * Hd)
        r0, r1 = r0 / width, r1 / width
        hidden_cols = pl.ds(2 * Hd, Hd)
        swap_h = [
            sems.remote(XT.at[2 * u + 1 - low, :, hidden_cols], XO.at[u, :, hidden_cols], sib) for u in range(H)
        ]
        for copy in swap_h:
            copy.start()
        for j in range(J):
            bo[j] = out[j * r : (j + 1) * r, :].astype(bf)
        back_bo.start()
        swap_ct.wait_recv()
        swap_ln2.wait_recv()

        def shrink_grad(u, _):
            t = 2 * u + low
            d = dot_l(CT[top, :], XT[t, :, 2 * Hd : 3 * Hd]) + dot_l(CT[bottom, :], XO[u, :, 2 * Hd : 3 * Hd])
            GF[u, :, 2 * Hd : 3 * Hd] = d.astype(bf)
            return 0

        for copy in swap_h:
            copy.wait_recv()
        lax.fori_loop(0, H, shrink_grad, 0)
        serve(rf[:2], 0)
        gln2 = out
        gln2[...] = jnp.zeros(gln2.shape, f32)

        def three(t, slot, _):
            ga = inv * (gh[t] - r0 - act[t] * r1)
            g, u = gate[t].astype(f32), up[t].astype(f32)
            s = jax.nn.sigmoid(g)
            gg = (ga * u * s * (1.0 + g * (1.0 - s))).astype(bf)
            gu = (ga * g * s).astype(bf)
            XT[t, :, 0:Hd] = gg
            XT[t, :, Hd : 2 * Hd] = gu
            gln2[...] += dot_t(XT[t, :, 0 : 2 * Hd], WFv[slot])
            return 0

        through(three, 0, 2 * Hd, 0)
        both_cols = pl.ds(0, 2 * Hd)
        swap_g = [
            sems.remote(XT.at[2 * u + 1 - low, :, both_cols], XO.at[u, :, both_cols], sib) for u in range(H)
        ]
        for copy in swap_g:
            copy.start()
        norm_back(midv, gln2, gains[2:3, :], CT, gmid, SM.at[0], 2, GB)
        swap_gb.start()
        serve(rf[:2], 1)
        for copy in swap_g:
            copy.wait_recv()

        def expand_grad(i, _):
            u = lax.div(i, 2)
            t = 2 * u + low
            c = pl.ds(pl.multiple_of(lax.rem(i, 2) * Hd, Hd), Hd)
            d = dot_l(LN2[top, :], XT[t, :, c]) + dot_l(LN2[bottom, :], XO[u, :, c])
            GF[u, :, c] = d.astype(bf)
            return 0

        lax.fori_loop(0, 2 * H, expand_grad, 0)
        serve(rf[2:], 0)
        for copy in swap_h + swap_g:
            copy.wait_send()
        pl.semaphore_signal(free, inc=1, device_id=sib, device_id_type=MESH)

    pl.run_scoped(
        feed,
        pltpu.VMEM((2, D, 2 * Hd), bf),
        pltpu.VMEM((J, r, D), bf),
        pltpu.VMEM((n, D), f32),
        pltpu.VMEM((T, n, Hd), bf),
        pltpu.VMEM((T, n, Hd), bf),
        pltpu.VMEM((T, n, Hd), f32),
        pltpu.VMEM((T, n, Hd), f32),
        pltpu.VMEM((n, D), f32),
        pltpu.VMEM((T, n, 3 * Hd), bf),
    )
    serve(rf[:2], 2)

    def attend(qv, Kv, Vv, lv, av, Wmv, gatt, dq, dK, dV, sK, sV):
        gets = [fetch(a, b) for a, b in ((Wm, Wmv), (att, av), (linv, lv), (q, qv), (K, Kv), (V, Vv))]
        half = (D // 256) * 128
        cuts = [pl.ds(0, half), pl.ds(half, D - half)]
        give = [
            [sems.remote(S.at[:, cut], XO.at[0, :, pl.ds(off + cut.start, cut.size)], sib) for off, S in ((0, sK), (D, sV))]
            for cut in cuts
        ]
        e0 = nlocal[0]
        nlocal[0] += 2

        def pairs(Es):
            def get_e(p, slot):
                return pltpu.make_async_copy(E.at[pl.ds(2 * p, 2)], Es.at[slot], local.at[e0 + slot])

            for p in range(2):
                get_e(p, p).start()
            for copy in gets:
                copy.wait()
            gatt[...] = dot(GB[top, :], Wmv[...]).astype(bf)

            def pair(p, _):
                for k, (parts, s) in {
                    0: (rf[:2], 3), 2: (rf[2:4], 1), 3: (rf[4:], 1), 4: (rf[2:4], 2), 5: (rf[4:], 2)
                }.items():
                    if parts:

                        @pl.when(p == k)
                        def _(parts=parts, s=s):
                            serve(parts, s)

                slot = lax.rem(p, 2)
                get_e(p, slot).wait()
                c = pl.ds(pl.multiple_of(p * 128, 128), 128)
                k2, v2, q2 = Kv[:, c], Vv[:, c], qv[:, c]
                dob = (gatt[:, c].astype(f32) * lv[:, c]).astype(bf)
                dl = dob.astype(f32) * av[:, c].astype(f32)
                m = 2 * n
                dqv = dkv = dvv = None
                for a in (0, 1):
                    ka = jnp.where(lanes(m, a), k2, jnp.zeros_like(k2))
                    va = jnp.where(lanes(m, a), v2, jnp.zeros_like(v2))
                    qa = jnp.where(lanes(n, a), q2, jnp.zeros_like(q2))
                    da = jnp.where(lanes(n, a), dob, jnp.zeros_like(dob))
                    delta = jnp.sum(jnp.where(lanes(n, a), dl, 0.0), axis=1, keepdims=True)
                    e = Es[slot, a]
                    dS = (e.astype(f32) * (dot_t(dob, va) - delta)).astype(bf)
                    x1, x2, x3 = dot(dS, ka), dot_l(dS, qa), dot_l(e, da)
                    dqv = x1 if a == 0 else dqv + x1
                    dkv = x2 if a == 0 else dkv + x2
                    dvv = x3 if a == 0 else dvv + x3
                dq[:, c] = dqv * 0.125
                dK[:, c] = dkv[:n]
                dV[:, c] = dvv[:n]
                sK[:, c] = dkv[n:].astype(bf)
                sV[:, c] = dvv[n:].astype(bf)

                @pl.when(p + 2 < D // 128)
                def _():
                    get_e(p + 2, slot).start()

                @pl.when(p == half // 128 - 1)
                def _():
                    pl.semaphore_wait(free, 1)
                    for copy in give[0]:
                        copy.start()

                return 0

            lax.fori_loop(0, D // 128, pair, 0)

        pl.run_scoped(pairs, pltpu.VMEM((2, 2, n, 2 * n), bf))
        for copy in give[1]:
            copy.start()

        def final(XT, LN1, Wqv, Wkv, Wvv, xv, *rawv):
            gln1, tok = dK, dq
            late = [fetch(a, b) for a, b in ((Wq, Wqv), (Wk, Wkv), (Wv, Wvv), (ln1, LN1), (x, xv))]
            states = [fetch(a, b) for a, b in zip(raw, rawv)] if weights else []
            for group in give:
                for copy in group:
                    copy.wait_recv()
            Gq, Gk, Gv = gatt, qv, Kv

            def rows(i, _):
                p = pl.ds(pl.multiple_of(i * 48, 48), 48)
                co, si, sj = cos[p, :], -sa[p, :], -sb[p, :]
                g_q = turn(dq[p, :], co, si, sj)
                g_k = turn(dK[p, :] + XO[0, p, 0:D].astype(f32), co, si, sj)
                g_v = dV[p, :] + XO[0, p, D : 2 * D].astype(f32)
                Gq[p, :] = g_q.astype(bf)
                Gk[p, :] = g_k.astype(bf)
                Gv[p, :] = g_v.astype(bf)
                split = [own_and_other(v, low, H) for v in (g_q, g_k, g_v, av[p, :].astype(f32))]
                for u in range(H):
                    for side in (0, 1):
                        XT[side, u, p, :] = jnp.concatenate([z[side][u] for z in split], axis=1).astype(bf)
                return 0

            lax.fori_loop(0, n // 48, rows, 0)
            swap_a = [sems.remote(XT.at[1, u], XO.at[1, :, pl.ds(u * D, D)], sib) for u in range(H)]
            for copy in swap_a:
                copy.start()
            for copy in late:
                copy.wait()
            gln1[...] = dot_t(Gq[...], Wqv[...])
            gln1[...] += dot_t(Gk[...], Wkv[...])
            gln1[...] += dot_t(Gv[top, :], Wvv[...])
            for copy in swap_a + [swap_gb]:
                copy.wait_recv()
            w = D // T
            for u in range(H):
                o = XO[1, :, u * D : (u + 1) * D]
                m = XT[0, u]
                d = dot_l(LN1[top, :], m[:, : 3 * w]) + dot_l(LN1[bottom, :], o[:, : 3 * w])
                e = dot_l(GB[top, :], m[:, 3 * w :]) + dot_l(GB[bottom, :], o[:, 3 * w :])
                GA[u] = jnp.concatenate([d, e], axis=1).astype(bf)
            serve(ra, 0)
            serve(rf[2:], 3)
            norm_back(xv, gln1, gains[0:1, :], gmid, tok, SM.at[0], 0)
            for j in range(J):
                tg[j] = tok[j * r : (j + 1) * r, :].astype(bf)
            back_tg.start()
            hops = [
                place.tees(),
                [place.at_x(k) for k in range(1, F)],
                [place.at_z(k) for k in range(1, C)],
            ]

            def add_up(own, land, between):
                at = 0
                for s, devices in enumerate(hops):
                    copies = [sems.remote(own.at[s], land.at[at + i], d) for i, d in enumerate(devices)]
                    for copy in copies:
                        copy.start()
                    between(s)
                    total = own[s]
                    for i, copy in enumerate(copies):
                        copy.wait_recv()
                        total = total + land[at + i]
                    for copy in copies:
                        copy.wait_send()
                    at += len(copies)
                    own[s + 1] = total

            add_up(SM, SML, lambda s: serve(ra, s + 1))
            small[...] = SM[len(hops)]
            if weights:
                for copy in states:
                    copy.wait()
                for i, (w, m, v, g) in enumerate(matrices(rawv, sums)):
                    NV[0, 2 * i : 2 * i + 1, :] = jnp.broadcast_to(jnp.sum(w * w, keepdims=True), (1, 128))
                    u = moments(g, m, v)[2] + DECAY * w
                    NV[0, 2 * i + 1 : 2 * i + 2, :] = jnp.broadcast_to(jnp.sum(u * u, keepdims=True), (1, 128))
                add_up(NV, NVL, lambda s: None)
                norms[...] = NV[len(hops)]
            else:
                norms[...] = jnp.zeros(norms.shape, f32)
            for copy in swap_a:
                copy.wait_send()

        pl.run_scoped(
            final, pltpu.VMEM((2, H, n, D), bf), pltpu.VMEM((2 * n, D), bf), *[pltpu.VMEM((D, D), bf)] * 3, pltpu.VMEM((n, D), f32),
            *[pltpu.VMEM(a.shape, f32) for a in raw],
        )
        for group in give:
            for copy in group:
                copy.wait_send()

    pl.run_scoped(
        attend,
        pltpu.VMEM((n, D), bf),
        pltpu.VMEM((2 * n, D), bf),
        pltpu.VMEM((2 * n, D), bf),
        pltpu.VMEM((n, D), f32),
        pltpu.VMEM((n, D), bf),
        pltpu.VMEM((D, D), bf),
        pltpu.VMEM((n, D), bf),
        *[pltpu.VMEM((n, D), f32)] * 3,
        *[pltpu.VMEM((n, D), bf)] * 2,
    )
    for part in rf + ra:
        part.settle()
    for back in (back_bo, back_tg):
        back.wait()
        back.finish()
    for copy in (swap_ln2, swap_ct, swap_gb):
        copy.wait_send()


def backward_call(F, C, T, R, weights, shape, saved, raw, ig, gains, cos, sa, sb):
    J, r, D = shape
    H, Hd = T // 2, ig.shape[2]
    n = cos.shape[0]
    heads = D // T
    outs = [(shape, bf), (shape, bf), ((R, 4 * heads + 3 * Hd), f32), ((16, D), f32), ((8, 128), f32)]
    grads = [((H, D, 3 * Hd), bf), ((H, D, D), bf)]
    out_specs = [HBM, HBM, VMEM, VMEM, VMEM]
    if not weights:
        outs += grads
        out_specs += [VMEM, VMEM]
    small = (8, 128)
    scratch = [((2 * n, D), bf)] * 3 + [((H, n, 3 * Hd), bf), ((n, D), f32), (shape, bf), (shape, bf)]
    hops = T + F + C - 3
    scratch += [((4, 16, D), f32), ((hops, 16, D), f32), ((4, 8, 128), f32), ((hops, 8, 128), f32)]
    scratch += grads if weights else [(small, bf)] * 2
    scratch = [pltpu.VMEM(s, d) for s, d in scratch]
    scratch += [
        pltpu.SemaphoreType.DMA((128,)),
        pltpu.SemaphoreType.DMA((128,)),
        pltpu.SemaphoreType.DMA((32,)),
        pltpu.SemaphoreType.REGULAR,
    ]
    if weights:
        scratch += reduce_lands(REDUCE_F + REDUCE_A, F, C, H, D, R)
    return pl.pallas_call(
        functools.partial(backward_kernel, F, C, T, R, weights),
        out_shape=[jax.ShapeDtypeStruct(s, d) for s, d in outs],
        in_specs=[HBM] * (len(saved) + len(raw)) + [VMEM] * 5,
        out_specs=out_specs,
        scratch_shapes=scratch,
        compiler_params=pltpu.CompilerParams(collective_id=2, has_side_effects=True, vmem_limit_bytes=LIMIT),
    )(*saved, *raw, ig, gains, cos, sa, sb)


def matrices(raw, sums):
    heads, hidden = raw[0].shape[2], raw[6].shape[2]
    base = 4 * heads
    a = [sums[:, i * heads : (i + 1) * heads] for i in range(4)]
    f = [sums[:, base + i * hidden : base + (i + 1) * hidden] for i in range(3)]
    out = []
    for i in range(3):
        out.append(tuple(r[i] for r in raw[0:3]) + (a[i],))
    merge = tuple(r[...] for r in raw[3:6]) + (a[3].T,)
    up = [tuple(r[i] for r in raw[6:9]) + (f[i],) for i in range(2)]
    shrink = tuple(r[...] for r in raw[9:12]) + (f[2].T,)
    join = lambda parts: tuple(jnp.concatenate(p, axis=0) for p in zip(*parts))
    return [join(out), merge, join(up), shrink]


def step_kernel(T, *refs):
    raw, (sums, norms, small, bo, tg), rest = refs[:12], refs[12:17], refs[17:]
    lg, lm, lv, ig, im, iv = rest[:6]
    bo_out, tg_out = rest[6:8]
    outs, (lg_out, lm_out, lv_out, ig_out, im_out, iv_out, trust) = rest[8:20], rest[20:27]
    bo_out[...] = bo[...]
    tg_out[...] = tg[...].astype(f32)
    size = jnp.sqrt(norms[:, 0:1])
    for i, (w, m, v, g) in enumerate(matrices(raw, sums)):
        m, v, u = moments(g, m, v)
        u = u + DECAY * w
        ratio = size[2 * i : 2 * i + 1] / size[2 * i + 1 : 2 * i + 2]
        w = w - RATE * ratio * u
        for k, value in enumerate((w, m, v)):
            outs[3 * i + k][...] = value.reshape(outs[3 * i + k].shape)
        trust[i : i + 1, 0:1] = size[2 * i : 2 * i + 1]
        trust[i : i + 1, 1:2] = size[2 * i + 1 : 2 * i + 2]
    hidden = ig.shape[1]
    me = lax.axis_index("tp")
    mine = small[8:10, 0:hidden]
    for t in range(1, T):
        mine = jnp.where(me == t, small[8 + 2 * t : 10 + 2 * t, 0:hidden], mine)
    for grad, old, new in (
        (small[0:4, :], (lg, lm, lv), (lg_out, lm_out, lv_out)),
        (mine, (ig, im, iv), (ig_out, im_out, iv_out)),
    ):
        m, v, u = moments(grad, old[1][...], old[2][...])
        new[0][...] = old[0][...] - RATE_GAINS * u
        new[1][...] = m
        new[2][...] = v

def moments(gradient, moment, square):
    moment = BETA_ONE * moment + (1.0 - BETA_ONE) * gradient
    square = BETA_TWO * square + (1.0 - BETA_TWO) * gradient * gradient
    update = (
        moment / (1.0 - BETA_ONE**STEP) / (jnp.sqrt(square / (1.0 - BETA_TWO**STEP)) + EPS_ADAM)
    )
    return (moment, square, update)


def body(
    F, C, T,
    tokens, cotangent, layer_gains, layer_first, layer_second, inner_gains, inner_first, inner_second,
    attend_weight, attend_first, attend_second, merge_weight, merge_first, merge_second,
    expand_weight, expand_first, expand_second, shrink_weight, shrink_first, shrink_second,
):
    bf, f32 = jnp.bfloat16, jnp.float32
    D = tokens.shape[-1]
    R = attend_weight.shape[1]
    rows = tokens.shape[1]
    J = C * T // 2
    assert J == tokens.shape[0]
    n = -(-J * rows // 48) * 48
    heads = attend_weight.shape[2]
    hidden = expand_weight.shape[2]
    fast = R % 16 == 0
    low = lax.axis_index("tp") % 2
    slots = jnp.arange(J, dtype=jnp.int32) * 2
    cos, sa, sb = rotary_tables(slots + low, rows, n)
    bias = jnp.concatenate([key_bias(slots + low, rows, n), key_bias(slots + 1 - low, rows, n)])[None]
    pack_a = jnp.concatenate([attend_weight[0], attend_weight[1], attend_weight[2], merge_weight.T], axis=1).astype(bf)
    pack_f = jnp.concatenate([expand_weight[0], expand_weight[1], shrink_weight.T], axis=1).astype(bf)
    if not fast:
        pack_a, pack_f = (
            lax.all_gather(lax.all_gather(p, ("fsdp", "ctx"), axis=0, tiled=True), "tp", axis=0)
            for p in (pack_a, pack_f)
        )
    inner_all, cin, WF, x, ln1, q, K, V, Wq, Wk, Wv, Wm, E, linv, att, mid, ln2 = forward_call(
        F, C, T, n, tokens, cotangent, pack_a, pack_f, layer_gains, cos, sa, sb, bias, inner_gains
    )
    if not fast:
        WF = pack_f
    saved = (cin, WF, ln2, mid, x, ln1, q, K, V, Wq, Wk, Wv, Wm, E, linv, att)
    raw = (
        attend_weight, attend_first, attend_second, merge_weight, merge_first, merge_second,
        expand_weight, expand_first, expand_second, shrink_weight, shrink_first, shrink_second,
    )
    out = backward_call(F, C, T, R, fast, tokens.shape, saved, raw, inner_all, layer_gains, cos, sa, sb)
    bo, tg, sums, small, norms = out[:5]
    if not fast:
        sums = jnp.concatenate([out[6], out[5]], axis=2).astype(f32)
        same = [[t for t in range(T) if t % 2 == k] for k in range(2)]
        sums = lax.psum_scatter(sums, "tp", scatter_dimension=0, axis_index_groups=same, tiled=False)
        sums = lax.psum_scatter(sums, ("fsdp", "ctx"), scatter_dimension=0, tiled=True)
        parts = []
        for w, m, v, g in matrices(raw, sums):
            u = moments(g, m, v)[2] + DECAY * w
            parts += [jnp.sum(w * w), jnp.sum(u * u)]
        parts = lax.psum(jnp.stack(parts), ("fsdp", "ctx", "tp"))
        norms = jnp.broadcast_to(parts[:, None], (8, 128))
    gains = (layer_gains, layer_first, layer_second, inner_gains, inner_first, inner_second)
    outs = [(tokens.shape, bf), (tokens.shape, f32)] + [(a.shape, f32) for a in raw + gains] + [((4, 2), f32)]
    return tuple(local_call(functools.partial(step_kernel, T), [*raw, sums, norms, small, bo, tg, *gains], outs))


def solution(mesh):
    tok = P("fsdp", ("ctx", "tp"), None)
    wide = P(None, ("fsdp", "ctx"), "tp")
    tall = P("tp", ("fsdp", "ctx"))
    split = P(None, "tp")
    sizes = (mesh.shape["fsdp"], mesh.shape["ctx"], mesh.shape["tp"])
    return jax.shard_map(
        functools.partial(body, *sizes),
        mesh=mesh,
        in_specs=(tok, tok, P(), P(), P(), split, split, split)
        + (wide,) * 3 + (tall,) * 3 + (wide,) * 3 + (tall,) * 3,
        out_specs=(tok, tok) + (wide,) * 3 + (tall,) * 3 + (wide,) * 3 + (tall,) * 3
        + (P(),) * 3 + (split,) * 3 + (P(),),
        check_vma=False,
    )
```

```python
import functools
import jax
import jax.numpy as jnp
from jax import lax
from jax.experimental import pallas as pl
from jax.experimental.pallas import tpu as pltpu
from jax.sharding import PartitionSpec as P

HD = 64
GRID = 32
STEP = 5
VALID = 1025
BETA_ONE = 0.5
BETA_TWO = 0.5
EPS_ADAM = 1e-06
DECAY = 0.01
RATE = 0.5
RATE_GAINS = 0.3
MESH = pl.DeviceIdType.MESH
f32 = jnp.float32
bf = jnp.bfloat16


class Place:
    def __init__(self, F, C, T):
        self.F, self.C, self.T, self.H = F, C, T, T // 2
        self.f = lax.axis_index("fsdp")
        self.c = lax.axis_index("ctx")
        self.t = lax.axis_index("tp")
        self.low = lax.rem(self.t, 2)
        self.high = lax.div(self.t, 2)
        self.pair = self.c * self.H + self.high
        self.pairs = C * self.H
        self.sibling = {"tp": self.t + 1 - 2 * self.low}
        self.xs = [lax.rem(self.f + k, F) for k in range(F)]
        self.ys = [lax.rem(self.high + k, self.H) for k in range(self.H)]
        self.zs = [lax.rem(self.c + k, C) for k in range(C)]

    def at_x(self, k):
        return {"fsdp": self.xs[k]}

    def at_y(self, k):
        return {"tp": self.ys[k] * 2 + self.low}

    def at_z(self, k):
        return {"ctx": self.zs[k]}

    def pair_at(self, k):
        i = lax.rem(self.pair + k, self.pairs)
        return i, {"ctx": lax.div(i, self.H), "tp": lax.rem(i, self.H) * 2 + self.low}

    def tees(self):
        return [{"tp": lax.rem(self.t + k, self.T)} for k in range(1, self.T)]

    def everyone(self):
        return [
            {"fsdp": self.xs[a], "ctx": self.zs[b], "tp": lax.rem(self.t + d, self.T)}
            for a in range(self.F) for b in range(self.C) for d in range(self.T) if a + b + d
        ]

    def partners(self, with_x):
        out = self.tees() + [
            {"ctx": self.zs[c], "tp": self.ys[y] * 2 + self.low} for c in range(1, self.C) for y in range(self.H)
        ]
        if with_x:
            out += [self.at_x(k) for k in range(1, self.F)]
        return out


def hail(partners):
    barrier = pltpu.get_barrier_semaphore()
    for partner in partners:
        pl.semaphore_signal(barrier, inc=1, device_id=partner, device_id_type=MESH)


def heard(partners):
    pl.semaphore_wait(pltpu.get_barrier_semaphore(), len(partners))


class Sems:
    def __init__(self, send, recv):
        self.send, self.recv, self.n = send, recv, 0

    def remote(self, src, dst, device):
        i = self.n
        self.n += 1
        return pltpu.make_async_remote_copy(
            src, dst, self.send.at[i], self.recv.at[i], device_id=device, device_id_type=MESH
        )

    def local(self, src, dst):
        i = self.n
        self.n += 1
        return pltpu.make_async_copy(src, dst, self.send.at[i])


class Exchange:
    def __init__(self, place, sems, src, dst):
        self.own = sems.local(src.at[place.pair], dst.at[place.pair])
        self.copies = []
        for k in range(1, place.pairs):
            i, device = place.pair_at(k)
            self.copies.append(sems.remote(src.at[i], dst.at[place.pair], device))

    def start(self):
        self.own.start()
        for copy in self.copies:
            copy.start()

    def wait(self):
        self.own.wait()
        for copy in self.copies:
            copy.wait_recv()

    def finish(self):
        for copy in self.copies:
            copy.wait_send()


class Gather:
    def __init__(self, place, sems, pack, whole, cols, first):
        P, R = place, pack.shape[0]
        C, F, H = P.C, P.F, P.H
        n = C * R
        window = pl.ds(*cols)

        def push(t, row, rows, device):
            block = whole.at[t, pl.ds(pl.multiple_of(row, 16), rows), window]
            return sems.remote(block, block, device)

        row = (P.f * C + P.c) * R
        base = P.f * n
        self.own = sems.local(
            pack.at[:, window], whole.at[P.t, pl.ds(pl.multiple_of(row, 16), R), window]
        )
        along_z = [push(P.t, row, R, P.at_z(k)) for k in range(1, C)]
        tees = [y * 2 + P.low for y in P.ys]
        if first == "y":
            second = [push(P.t, base, n, P.at_y(k)) for k in range(1, H)]
            third = [push(t, base, n, P.at_x(k)) for k in range(1, F) for t in tees]
            over_3 = [push(t, base, n, P.sibling) for t in tees[1:]]
            over_4 = [push(t, P.xs[k] * n, n, P.sibling) for k in range(1, F) for t in tees]
        else:
            second = [push(P.t, base, n, P.at_x(k)) for k in range(1, F)]
            third = [push(P.t, 0, n * F, P.at_y(k)) for k in range(1, H)]
            over_3 = [push(P.t, P.xs[k] * n, n, P.sibling) for k in range(1, F)]
            over_4 = [push(t, 0, n * F, P.sibling) for t in tees[1:]]
        over_2 = [push(P.t, base, n, P.sibling)]
        self.waits = [[], along_z, second, third]
        self.starts = [along_z, second + over_2, third + over_3, over_4]
        self.sent_over = over_2 + over_3 + over_4

    def stage(self, s):
        if s == 0:
            self.own.wait()
        for copy in self.waits[s]:
            copy.wait_recv()
        for copy in self.starts[s]:
            copy.start()

    def finish(self):
        for copy in self.sent_over:
            copy.wait_recv()

    def settle(self):
        for group in self.starts:
            for copy in group:
                copy.wait_send()


def by_rows(rows, step, body):
    def it(i, _):
        body(pl.multiple_of(i * step, step), step)
        return 0

    lax.fori_loop(0, rows // step, it, 0)


class Reduce:
    def __init__(self, place, sems, view, D, width, first, lands, out, out_col, R):
        P, n = place, place.C * R
        C, F, H = P.C, P.F, P.H
        L1, L2, L3 = lands
        self.out, self.to, self.R = out, pl.ds(out_col, width), R
        base = pl.multiple_of(P.f * n, 16)
        mine = pl.multiple_of(base + P.c * R, 16)
        self.copies = [[], [], []]

        def rows(u, start, count):
            return view(u, pl.ds(start, count))

        def send(stage, src, dst, device):
            self.copies[stage].append(sems.remote(src, dst, device))

        if first == "x":
            for k in range(1, F):
                for u in range(H):
                    send(0, rows(u, pl.multiple_of(P.xs[k] * n, 16), n), L1.at[k - 1, u], P.at_x(k))
            for k in range(1, H):
                send(1, rows(P.ys[k], base, n), L2.at[k - 1], P.at_y(k))
            self.adds = [
                [(rows(u, base, n), [L1.at[k - 1, u] for k in range(1, F)]) for u in range(H)],
                [(rows(P.high, base, n), [L2.at[k - 1] for k in range(1, H)])],
            ]
        else:
            for k in range(1, H):
                send(0, rows(P.ys[k], 0, D), L1.at[k - 1], P.at_y(k))
            for k in range(1, F):
                send(1, rows(P.high, pl.multiple_of(P.xs[k] * n, 16), n), L2.at[k - 1], P.at_x(k))
            self.adds = [
                [(rows(P.high, 0, D), [L1.at[k - 1] for k in range(1, H)])],
                [(rows(P.high, base, n), [L2.at[k - 1] for k in range(1, F)])],
            ]
        for k in range(1, C):
            send(2, rows(P.high, pl.multiple_of(base + P.zs[k] * R, 16), R), L3.at[k - 1], P.at_z(k))
        self.last = (rows(P.high, mine, R), [L3.at[k - 1] for k in range(1, C)])

    def stage(self, s):
        if s > 0:
            for copy in self.copies[s - 1]:
                copy.wait_recv()
        if s in (1, 2):
            for dst, lands in self.adds[s - 1]:

                def add(r, k, dst=dst, lands=lands):
                    v = dst[pl.ds(r, k), :].astype(f32)
                    for land in lands:
                        v = v + land[pl.ds(r, k), :].astype(f32)
                    dst[pl.ds(r, k), :] = v.astype(bf)

                by_rows(dst.shape[0], 96, add)
        if s == 3:
            dst, lands = self.last
            v = dst[...].astype(f32)
            for land in lands:
                v = v + land[...].astype(f32)
            self.out[:, self.to] = v
        else:
            for copy in self.copies[s]:
                copy.start()

    def settle(self):
        for group in self.copies:
            for copy in group:
                copy.wait_send()


def reduce_lands(parts, F, C, H, D, R):
    out = []
    for (_, n), first in parts:
        if first == "x":
            out += [(F - 1, H, C * R, n), (H - 1, C * R, n)]
        else:
            out += [(H - 1, D, n), (F - 1, C * R, n)]
        out.append((C - 1, R, n))
    return [pltpu.VMEM(s, bf) for s in out]
EPS=1e-6
def dot(a,b): return jnp.dot(a,b,preferred_element_type=f32)
def dot_t(a,b): return lax.dot_general(a,b,(((1,),(1,)),((),())),preferred_element_type=f32)
def dot_l(a,b): return lax.dot_general(a,b,(((0,),(0,)),((),())),preferred_element_type=f32)

def chunks(rows, step, body):
    def it(i,_):
        body(pl.ds(pl.multiple_of(i*step,step),step)); return 0
    lax.fori_loop(0,rows//step,it,0)

def norm(v):
    mean=jnp.mean(v,axis=-1,keepdims=True)
    var=jnp.mean(v*v,axis=-1,keepdims=True)-mean*mean
    inv=lax.rsqrt(var+EPS)
    return (v-mean)*inv, inv

def spread(src3, dst):
    J,r,D=src3.shape
    n=dst.shape[0]
    pad=n-J*r
    if pad: dst[n-16:n,:]=jnp.zeros((16,D),f32)
    for j in range(J):
        dst[j*r:(j+1)*r,:]=src3[j].astype(f32)

def join(WA, g, dst, T):
    def it(i,_):
        s=pl.ds(pl.multiple_of(i*96,96),96)
        for t in range(T):
            dst[s,128*t:128*t+128]=WA[t,s,128*g:128*g+128]
        for u in range(T//2):
            c=pl.ds(512+128*(g//2),128)
            a=WA[2*u,s,c].astype(f32); b=WA[2*u+1,s,c].astype(f32)
            if g%2==0: b=pltpu.roll(b,64,1)
            else: a=pltpu.roll(a,64,1)
            dst[s,128*(T+u):128*(T+u)+128]=jnp.where(lanes(96,0),a,b).astype(bf)
        return 0
    lax.fori_loop(0,WA.shape[1]//96,it,0)

def turn(v, cos, sa, sb):
    n=v.shape[1]
    out=[]
    for i in range(n//128):
        a=v[:,i*128:(i+1)*128]
        out.append(a*cos+pltpu.roll(a,128-16,1)*sa+pltpu.roll(a,16,1)*sb)
    return jnp.concatenate(out,axis=1)

def normal(x, gains, ln1):
    def ln(s):
        v,_=norm(x[s,:])
        ln1[s,:]=(v*gains[0:1,:]+gains[1:2,:]).astype(bf)
    chunks(x.shape[0],48,ln)


def project(ln1, W, cos, sa, sb, dst, scale=None):
    n=ln1.shape[0]//2
    y=dot(ln1[0:n,:],W[...])
    if cos is not None: y=turn(y,cos[...],sa[...],sb[...])
    if scale is not None: y=y*scale
    dst[0:n,:]=y.astype(bf)


def lanes(n, a):
    return (lax.broadcasted_iota(jnp.int32,(n,128),1)//64==a)

def attention(q,K,V,bias,Es,linv,att,before,after):
    n=q.shape[0]; m=K.shape[0]
    def pair(p,_):
        c=pl.ds(pl.multiple_of(p*128,128),128)
        k2=K[:,c]; v2=V[:,c]
        q2=q[:,c]
        o=None; li=[]
        for a in (0,1):
            before(p,a)
            ka=jnp.where(lanes(m,a),k2,jnp.zeros_like(k2))
            va=jnp.where(lanes(m,a),v2,jnp.zeros_like(v2))
            S=dot_t(q2,ka)+bias[0:1,:]
            mx=jnp.max(S,axis=1,keepdims=True)
            e=jnp.exp(S-mx)
            l=1.0/jnp.sum(e,axis=1,keepdims=True)
            eb=e.astype(bf)
            Es[a]=eb
            after(p,a)
            oa=dot(eb,va)*l
            o=oa if o is None else o+oa
            li.append(l)
        att[:,c]=o.astype(bf)
        linv[:,c]=jnp.where(lanes(n,0),li[0],li[1])
        return 0
    lax.fori_loop(0,q.shape[1]//128,pair,0)

def merge(att,Wm,x,mid,gains,ln2,n):
    mid[...]=x[...]+dot_t(att[...],Wm[...])
    def ln(s):
        v,_=norm(mid[s,:])
        ln2[s,:]=(v*gains[2:3,:]+gains[3:4,:]).astype(bf)
    chunks(n,48,ln)

def norm_back(src, e_src, gain, add, dst, lay, row):
    n=src.shape[0]
    lay[row:row+2,:]=jnp.zeros((2,src.shape[1]),f32)
    def it(s):
        a,inv=norm(src[s,:]); e=e_src[s,:]
        lay[row:row+1,:]+=jnp.sum(e*a,axis=0,keepdims=True)
        lay[row+1:row+2,:]+=jnp.sum(e,axis=0,keepdims=True)
        eg=e*gain
        d=add[s,:].astype(f32)+inv*(eg-jnp.mean(eg,axis=1,keepdims=True)-a*jnp.mean(eg*a,axis=1,keepdims=True))
        dst[s,:]=d.astype(dst.dtype)
    chunks(n,48,it)


VMEM = pl.BlockSpec(memory_space=pltpu.VMEM)
HBM = pl.BlockSpec(memory_space=pl.ANY)
LIMIT = 60 * 2**20


def local_call(body, ins, outs, scratch=(), flops=0):
    return pl.pallas_call(
        body,
        out_shape=[jax.ShapeDtypeStruct(s, d) for s, d in outs],
        in_specs=[VMEM] * len(ins),
        out_specs=[VMEM] * len(outs),
        scratch_shapes=[pltpu.VMEM(s, d) for s, d in scratch],
        compiler_params=pltpu.CompilerParams(vmem_limit_bytes=LIMIT),
    )(*ins)


def rotary_tables(slots, rows, total):
    quarter = HD // 4
    positions = (slots[:, None] * rows + jnp.arange(rows, dtype=jnp.int32)).reshape(-1)
    inside = (positions >= 1) & (positions <= GRID * GRID)
    patch = jnp.where(inside, positions - 1, 0)
    frequency = 10000.0 ** (-jnp.arange(quarter, dtype=jnp.float32) / quarter)
    row_angle = (patch // GRID).astype(jnp.float32)[:, None] * frequency
    column_angle = (patch % GRID).astype(jnp.float32)[:, None] * frequency
    angles = jnp.concatenate([row_angle, row_angle, column_angle, column_angle], axis=-1)
    angles = jnp.pad(angles, ((0, total - angles.shape[0]), (0, 0)))
    angles = jnp.concatenate([angles, angles], axis=-1)
    sine = jnp.sin(angles)
    first = (jnp.arange(2 * HD) // quarter) % 2 == 0
    return jnp.cos(angles), jnp.where(first, -sine, 0.0), jnp.where(first, 0.0, sine)


def key_bias(slots, rows, total):
    positions = (slots[:, None] * rows + jnp.arange(rows, dtype=jnp.int32)).reshape(-1)
    bias = jnp.where(positions < VALID, 0.0, -1e30).astype(jnp.float32)
    return jnp.pad(bias, (0, total - bias.shape[0]), constant_values=-1e30)


GATHER_A = (((0, 384), "y"), ((384, 384), "x"))
GATHER_F = tuple(((256 * i, 256), k) for i, k in enumerate("yxyxyx"))
FIRST_F = 4
REDUCE_H = (((1024, 256), "x"), ((1280, 256), "y"))
REDUCE_G = (((0, 256), "x"), ((256, 256), "y"), ((512, 256), "x"), ((768, 256), "y"))
REDUCE_A = (((0, 256), "x"), ((256, 256), "y"), ((512, 128), "x"), ((640, 128), "y"))
PLAN = {
    "start": ("A00", "A10"),
    "z": ("A01", "A11"),
    "early": ("A02", "A12"),
    "tokens": ("F00", "F10"),
    "last": ("A03", "A13"),
    "k": ("F01", "F11", "F20", "F30"),
    "q": ("F02", "F12"),
    "p0": ("F21", "F31", "F40", "F50"),
    "p1": ("F03", "F13"),
    "p2": ("F22", "F32"),
    "p3": ("F41", "F51", "cot"),
    "p4": ("F23", "F33"),
    "p5": ("F42", "F52"),
    "merged": ("F43", "F53"),
    "shrunk": ("H00", "H10"),
    "threes": ("H01", "H11"),
    "expanded1": ("G00", "G10"),
    "expanded3": ("G20", "G30", "H02", "H12"),
    "back0": ("H03", "H13"),
    "back1": ("G01", "G11"),
    "back2": ("G21", "G31"),
    "back3": ("G02", "G12"),
    "back4": ("G22", "G32"),
    "back5": ("G03", "G13"),
    "main": ("B00", "B10", "G23", "G33"),
    "tail": ("B20", "B30"),
    "back_out": ("B01", "B11"),
    "hop0": ("B21", "B31"),
    "hop1": ("B02", "B12"),
    "hop2": ("B22", "B32"),
    "end": ("B03", "B13", "B23", "B33"),
}


def mine_and_theirs(tiles, low):
    a, b = tiles
    return jnp.where(low == 0, a, b), jnp.where(low == 0, b, a)


def halves(tile, low):
    other = pltpu.roll(tile, 64, 1)
    return jnp.where(low == 0, tile, other), jnp.where(low == 0, other, tile)


def block_kernel(F, C, T, R, n, weights, plan, tok, cot, *rest):
    if weights:
        WF_in = None
    else:
        (WA_in, WF_in), rest = rest[:2], rest[2:]
    raw, rest = rest[:12], rest[12:]
    gains, inner, cos, sa, sb, bias = rest[:6]
    bo_out, tg_out, sums, small, norms = rest[6:11]
    WF, x_h, ln1_h, q_h, K_h, V_h, E, linv_h, att_h = rest[11:20]
    W_h = rest[20:24]
    rest = rest[24:]
    if not weights:
        (GF, GA), rest = rest[:2], rest[2:]
    (IG, LN2, CT, GB, XO, mid, cin, tg, SM, SML, NV, NVL, big, GA_s, pa, pf, send, recv, local, free) = rest[:20]
    lands = rest[20:]
    place = Place(F, C, T)
    H, low, sib = place.H, place.low, place.sibling
    sems = Sems(send, recv)
    partners = place.everyone() if weights else place.partners(True)
    hail(partners)
    bo = cin
    J, r, D = bo.shape
    Hd = IG.shape[2]
    tiles = D // 128
    main = T * 128
    wide = D // T * 2 // 3
    top, bottom = pl.ds(0, n), pl.ds(n, n)
    nlocal = [0]
    ig = IG

    def slots(count):
        nlocal[0] += count
        return nlocal[0] - count

    def fetch(src, dst):
        copy = pltpu.make_async_copy(src, dst, local.at[slots(1)])
        copy.start()
        return copy

    if weights:
        GA = GA_s

        def GF(u, rows, start, size):
            return big.at[2 * u + start // D, rows, pl.ds(start % D, size)]

        WA = big
    else:
        WA = WA_in

    tokens = Exchange(place, sems, tok, tg)
    cots = Exchange(place, sems, cot, cin)
    swap_ln2 = sems.remote(LN2.at[top], LN2.at[bottom], sib)
    swap_ct = sems.remote(CT.at[top], CT.at[bottom], sib)
    swap_gb = sems.remote(GB.at[top], GB.at[bottom], sib)
    back_bo = Exchange(place, sems, bo, bo_out)
    back_tg = Exchange(place, sems, tg, tg_out)
    share = [sems.remote(inner, IG.at[place.t], device) for device in place.tees()]
    groups = {"A": [], "F": [], "H": [], "G": [], "B": []}
    if weights:
        for key, pack, whole, parts in (("A", pa, WA, GATHER_A), ("F", pf, WF, GATHER_F)):
            groups[key] = [Gather(place, sems, pack, whole, cols, first) for cols, first in parts]
        i = 0
        for key, parts in (("H", REDUCE_H), ("G", REDUCE_G), ("B", REDUCE_A)):
            for (start, size), first in parts:
                if key == "B":
                    view = lambda u, rows, c=pl.ds(start, size): GA.at[u, rows, c]
                    col = start
                else:
                    view = lambda u, rows, start=start, size=size: GF(u, rows, start, size)
                    col = D + start
                groups[key].append(
                    Reduce(place, sems, view, D, size, first, lands[3 * i : 3 * i + 3], sums, col, R)
                )
                i += 1

    def at(point):
        for step in plan.get(point, ()) if weights else ():
            if step == "cot":
                cots.start()
                continue
            groups[step[0]][int(step[1])].stage(int(step[2]))

    def at_loop(name, index, count):
        for k in range(count):
            if weights and plan.get(f"{name}{k}"):

                @pl.when(index == k)
                def _(k=k):
                    at(f"{name}{k}")

    def wait_all(key):
        for g in groups[key]:
            g.finish()

    def forward(x, ln1, q, K, V, Wq, Wk, Wv, Wm, att, linv, Es, *states):
        Ws = (Wq, Wk, Wv, Wm)
        if weights:
            gets = [fetch(raw[k], states[i]) for i, k in enumerate((0, 3, 6, 9))]
            for copy in gets:
                copy.wait()
            aw, mw, ew, sw = states
            four = [aw[0], aw[1], aw[2], mw[...]]
            for g, w in enumerate(four):
                pa[:, wide * g : wide * (g + 1)] = w[:, :wide].astype(bf)
            for g in (0, 2):
                pair = [w[:, wide:] for w in four[g : g + 2]]
                pa[:, 4 * wide + 64 * g : 4 * wide + 64 * g + 128] = jnp.concatenate(pair, axis=1).astype(bf)
            for g, w in enumerate((ew[0], ew[1], sw[...])):
                pf[:, Hd * g : Hd * (g + 1)] = w.astype(bf)
            for g in groups["A"] + groups["F"]:
                g.own.start()
        heard(partners)
        IG[place.t] = inner[...]
        at("start")
        if not weights:
            tokens.start()
            cots.start()
        for copy in share:
            copy.start()
        at("z")
        if weights:
            tokens.start()
        at("early")
        tokens.wait()
        at("tokens")
        spread(tg, x)
        normal(x, gains, ln1)
        swap_ln1 = sems.remote(ln1.at[top], XO.at[1, :, pl.ds(0, D)], sib)
        swap_ln1.start()
        at("normed")
        if weights:
            at("last")
            wait_all("A")
        else:
            whole = pltpu.make_async_copy(WA_in, big, local.at[slots(1)])
            whole.start()
            whole.wait()
        saves = [fetch(x, x_h), fetch(ln1.at[top], ln1_h.at[top])]
        swap = [sems.remote(X.at[top], XO.at[0, :, pl.ds(o, D)], sib) for X, o in ((K, 0), (V, D))]
        join(big, 1, Wk, T)
        project(ln1, Wk, cos, sa, sb, K)
        swap[0].start()
        at("k")
        join(big, 2, Wv, T)
        project(ln1, Wv, None, None, None, V)
        swap[1].start()
        at("v")
        join(big, 0, Wq, T)
        project(ln1, Wq, cos, sa, sb, q, 0.125)
        join(big, 3, Wm, T)
        at("q")
        saves += [fetch(a, b) for a, b in zip(Ws, W_h)] + [fetch(q, q_h)]
        for copy, X in zip(swap, (K, V)):
            copy.wait_recv()
        K[bottom, :] = XO[0, :, 0:D]
        V[bottom, :] = XO[0, :, D : 2 * D]
        saves += [fetch(K, K_h), fetch(V, V_h)]
        swap_ln1.wait_recv()
        saves += [fetch(XO.at[1, :, pl.ds(0, D)], ln1_h.at[bottom])]
        e0 = slots(2)

        def put_e(h):
            slot = lax.rem(h, 2)
            return pltpu.make_async_copy(Es.at[slot], E.at[h], local.at[e0 + slot])

        def before(p, a):
            at_loop("p" if a == 0 else "o", p, tiles)

            @pl.when(p > 0)
            def _():
                put_e(2 * p + a - 2).wait()

        def after(p, a):
            put_e(2 * p + a).start()

        attention(q, K, V, bias, Es, linv, att, before, after)
        at("attended")
        late = [fetch(linv, linv_h), fetch(att, att_h)]
        merge(att, Wm, x, mid, gains, LN2, n)
        swap_ln2.start()
        at("merged")
        for h in (2 * tiles - 2, 2 * tiles - 1):
            put_e(h).wait()
        for copy in saves + late:
            copy.wait()
        for copy in swap + [swap_ln1]:
            copy.wait_send()
        pl.semaphore_signal(free.at[0], inc=1, device_id=sib, device_id_type=MESH)

    pl.run_scoped(
        forward,
        pltpu.VMEM((n, D), f32),
        pltpu.VMEM((2 * n, D), bf),
        pltpu.VMEM((n, D), bf),
        pltpu.VMEM((2 * n, D), bf),
        pltpu.VMEM((2 * n, D), bf),
        *[pltpu.VMEM((D, D), bf)] * 4,
        pltpu.VMEM((n, D), bf),
        pltpu.VMEM((n, D), f32),
        pltpu.VMEM((2, n, 2 * n), bf),
        *[pltpu.VMEM(raw[k].shape, f32) for k in (0, 3, 6, 9)],
    )
    tokens.finish()
    for part in groups["A"]:
        part.settle()

    def feed(WFv, gate, up, act, gh, out, XT):
        w0 = slots(2)
        WF_from = WF if weights else WF_in

        def get_w(t, start, size):
            slot = lax.rem(t, 2)
            return pltpu.make_async_copy(
                WF_from.at[t, :, pl.ds(start, size)], WFv.at[slot, :, pl.ds(0, size)], local.at[w0 + slot]
            )

        def through(body, start, size, init):
            def step(t, c):
                get_w(t, start, size).wait()
                c = body(t, lax.rem(t, 2), c)

                @pl.when(t + 2 < T)
                def _():
                    get_w(t + 2, start, size).start()

                return c

            return lax.fori_loop(0, T, step, init)

        def ahead(start, size):
            for t in range(2):
                get_w(t, start, size).start()

        def swaps(cols):
            return [sems.remote(XT.at[2 * u + 1 - low, :, cols], XO.at[u, :, cols], sib) for u in range(H)]

        def pass_on(copies, t):
            for u, copy in enumerate(copies):

                @pl.when(t == 2 * u + 1 - low)
                def _(copy=copy):
                    copy.start()

        swap_h = swaps(pl.ds(2 * Hd, Hd))
        swap_g = swaps(pl.ds(0, 2 * Hd))
        at("feed")
        for g in groups["F"][:FIRST_F]:
            g.finish()
        ahead(0, 2 * Hd)
        def one(t, slot, c):
            at_loop("one", t, T)
            s0, s1 = c
            gu = dot(LN2[top, :], WFv[slot])
            g, u = gu[:, :Hd], gu[:, Hd:]
            a = g * jax.nn.sigmoid(g) * u
            gate[t] = g.astype(gate.dtype)
            up[t] = u.astype(up.dtype)
            act[t] = a
            return s0 + jnp.sum(a, axis=1, keepdims=True), s1 + jnp.sum(a * a, axis=1, keepdims=True)

        z = jnp.zeros((n, 1), f32)
        s0, s1 = through(one, 0, 2 * Hd, (z, z))
        at("ones")
        for g in groups["F"][FIRST_F:]:
            g.finish()
        ahead(2 * Hd, Hd)
        width = T * Hd
        mean = s0 / width
        inv = lax.rsqrt(s1 / width - mean * mean + EPS)
        SM[0] = jnp.zeros(SM.shape[1:], f32)
        cots.wait()
        spread(cin, out)
        CT[top, :] = out[...].astype(bf)
        swap_ct.start()
        out[...] = mid[...]
        pl.semaphore_wait(free.at[0], 1)
        for copy in share:
            copy.wait()

        def two(t, slot, c):
            r0, r1 = c
            n3 = (act[t] - mean) * inv
            act[t] = n3
            gt = ig[t, 0:1, :]
            hid = (n3 * gt + ig[t, 1:2, :]).astype(bf)
            XT[t, :, 2 * Hd : 3 * Hd] = hid
            pass_on(swap_h, t)
            out[...] += dot_t(hid, WFv[slot, :, 0:Hd])
            h = dot(CT[top, :], WFv[slot, :, 0:Hd])
            SM[0, pl.ds(8 + 2 * t, 1), 0:Hd] = jnp.sum(h * n3, axis=0, keepdims=True)
            SM[0, pl.ds(9 + 2 * t, 1), 0:Hd] = jnp.sum(h, axis=0, keepdims=True)
            e = h * gt
            gh[t] = e.astype(gh.dtype)
            return r0 + jnp.sum(e, axis=1, keepdims=True), r1 + jnp.sum(e * n3, axis=1, keepdims=True)

        r0, r1 = through(two, 2 * Hd, Hd, (z, z))
        ahead(0, 2 * Hd)
        r0, r1 = r0 / width, r1 / width
        swap_ct.wait_recv()
        swap_ln2.wait_recv()

        def put_f(u, start, value):
            if weights:
                GF(u, pl.ds(0, D), start, value.shape[1])[...] = value.astype(bf)
            else:
                GF[u, :, start : start + value.shape[1]] = value.astype(bf)

        for copy in swap_h:
            copy.wait_recv()
        for u in range(H):
            t = 2 * u + low
            c = pl.ds(2 * Hd, Hd)
            put_f(u, 2 * Hd, dot_l(CT[top, :], XT[t, :, c]) + dot_l(CT[bottom, :], XO[u, :, c]))
        at("shrunk")
        for j in range(J):
            bo[j] = out[j * r : (j + 1) * r, :].astype(bf)
        back_bo.start()
        gln2 = out
        gln2[...] = jnp.zeros(gln2.shape, f32)

        def three(t, slot, _):
            at_loop("three", t, T)
            ga = inv * (gh[t].astype(f32) - r0 - act[t] * r1)
            g, u = gate[t].astype(f32), up[t].astype(f32)
            s = jax.nn.sigmoid(g)
            gg = (ga * u * s * (1.0 + g * (1.0 - s))).astype(bf)
            gu = (ga * g * s).astype(bf)
            XT[t, :, 0:Hd] = gg
            XT[t, :, Hd : 2 * Hd] = gu
            pass_on(swap_g, t)
            gln2[...] += dot_t(XT[t, :, 0 : 2 * Hd], WFv[slot])
            return 0

        through(three, 0, 2 * Hd, 0)
        at("threes")
        for copy in swap_g:
            copy.wait_recv()
        for k in range(4):
            for u in range(H):
                t = 2 * u + low
                c = pl.ds(k * Hd // 2, Hd // 2)
                put_f(u, k * Hd // 2, dot_l(LN2[top, :], XT[t, :, c]) + dot_l(LN2[bottom, :], XO[u, :, c]))
            at(f"expanded{k}")
        norm_back(mid, gln2, gains[2:3, :], CT, GB, SM.at[0], 2)
        swap_gb.start()
        at("fed")
        for copy in swap_h + swap_g + [swap_ln2, swap_ct]:
            copy.wait_send()
        pl.semaphore_signal(free.at[1], inc=1, device_id=sib, device_id_type=MESH)

    pl.run_scoped(
        feed,
        pltpu.VMEM((2, D, 2 * Hd), bf),
        pltpu.VMEM((T, n, Hd), bf),
        pltpu.VMEM((T, n, Hd), bf),
        pltpu.VMEM((T, n, Hd), f32),
        pltpu.VMEM((T, n, Hd), f32),
        pltpu.VMEM((n, D), f32),
        pltpu.VMEM((T, n, 3 * Hd), bf),
    )
    cots.finish()

    def attend(qv, lv, av, Wmv, gatt, dq, dK, dV, sK, sV, XT, LN1, Wqv, Wkv, Wvv):
        e0 = slots(2)

        cuts = [pl.ds(0, main), pl.ds(main, D - main)]
        give = [
            [sems.remote(S.at[:, cut], XO.at[0, :, pl.ds(off + cut.start, cut.size)], sib) for off, S in ((0, sK), (D, sV))]
            for cut in cuts
        ]
        swap_a = [
            [sems.remote(XT.at[1, u, :, cut], XO.at[1, :, pl.ds(H * cut.start + u * cut.size, cut.size)], sib) for u in range(H)]
            for cut in cuts
        ]
        Kv, Vv = LN2, CT
        Gq, Gk, Gv = gatt, qv, Kv

        def gradients(p, c):
            co, si, sj = cos[p, :], -sa[p, :], -sb[p, :]
            k0, v0 = pl.ds(c.start, c.size), pl.ds(D + c.start, c.size)
            g_q = turn(dq[p, c], co, si, sj)
            g_k = turn(dK[p, c] + XO[0, p, k0].astype(f32), co, si, sj)
            g_v = dV[p, c] + XO[0, p, v0].astype(f32)
            return g_q, g_k, g_v, av[p, c].astype(f32)

        def keep(p, c, values):
            for ref, v in zip((Gq, Gk, Gv), values):
                ref[p, c] = v.astype(bf)

        def main_rows(i, _):
            p = pl.ds(pl.multiple_of(i * 48, 48), 48)
            values = gradients(p, cuts[0])
            keep(p, cuts[0], values)
            for u in range(H):
                for g, v in enumerate(values):
                    two = v[:, 256 * u : 256 * u + 128], v[:, 256 * u + 128 : 256 * u + 256]
                    for side, z in enumerate(mine_and_theirs(two, low)):
                        XT[side, u, p, 128 * g : 128 * g + 128] = z.astype(bf)
            return 0

        def tail_rows(i, _):
            p = pl.ds(pl.multiple_of(i * 48, 48), 48)
            values = gradients(p, cuts[1])
            keep(p, cuts[1], values)
            first = lanes(48, 0)
            for u in range(H):
                split = [halves(v[:, 128 * u : 128 * u + 128], low) for v in values]
                for g in (0, 1):
                    (a0, b0), (a1, b1) = split[2 * g], split[2 * g + 1]
                    c = pl.ds(main + 128 * g, 128)
                    XT[0, u, p, c] = jnp.where(first, a0, b1).astype(bf)
                    XT[1, u, p, c] = jnp.where(first, b0, a1).astype(bf)
            return 0

        def weight_grad(k):
            for copy in swap_a[k]:
                copy.wait_recv()
            cut = cuts[k]
            for u in range(H):
                m = XT[0, u, :, cut]
                o = XO[1, :, H * cut.start + u * cut.size : H * cut.start + (u + 1) * cut.size]
                w = cut.size // 4
                if k == 0:
                    d = dot_l(LN1[top, :], m[:, : 3 * w]) + dot_l(LN1[bottom, :], o[:, : 3 * w])
                    e = dot_l(GB[top, :], m[:, 3 * w :]) + dot_l(GB[bottom, :], o[:, 3 * w :])
                    GA[u, :, 0 : 3 * w] = d.astype(bf)
                    GA[u, :, 3 * w : 4 * w] = e.astype(bf)
                else:
                    d = dot_l(LN1[top, :], m) + dot_l(LN1[bottom, :], o)
                    e = dot_l(GB[top, :], m) + dot_l(GB[bottom, :], o)
                    lane = lax.broadcasted_iota(jnp.int32, d.shape, 1)
                    GA[u, :, cut] = jnp.where(lane < 3 * w, d, e).astype(bf)

        def pairs(Es):
            def get_e(h):
                slot = lax.rem(h, 2)
                return pltpu.make_async_copy(E.at[h], Es.at[slot], local.at[e0 + slot])

            for h in range(2):
                get_e(h).start()
            gets = [fetch(a, b) for a, b in ((W_h[3], Wmv), (q_h, qv), (K_h, Kv), (V_h, Vv), (att_h, av), (linv_h, lv))]
            late = [fetch(a, b) for a, b in ((ln1_h, LN1), (W_h[0], Wqv), (W_h[1], Wkv), (W_h[2], Wvv))]
            gets[0].wait()
            gatt[...] = dot(GB[top, :], Wmv[...]).astype(bf)
            for copy in gets[1:]:
                copy.wait()

            def pair(p, _):
                at_loop("back", p, tiles)

                @pl.when(p == tiles - 1)
                def _():
                    for copy in give[0]:
                        copy.wait_recv()
                    lax.fori_loop(0, n // 48, main_rows, 0)
                    for copy in swap_a[0]:
                        copy.start()

                c = pl.ds(pl.multiple_of(p * 128, 128), 128)
                k2, v2, q2 = Kv[:, c], Vv[:, c], qv[:, c]
                dob = (gatt[:, c].astype(f32) * lv[:, c]).astype(bf)
                dl = dob.astype(f32) * av[:, c].astype(f32)
                m = 2 * n
                dqv = dkv = dvv = None
                for a in (0, 1):
                    ka = jnp.where(lanes(m, a), k2, jnp.zeros_like(k2))
                    va = jnp.where(lanes(m, a), v2, jnp.zeros_like(v2))
                    qa = jnp.where(lanes(n, a), q2, jnp.zeros_like(q2))
                    da = jnp.where(lanes(n, a), dob, jnp.zeros_like(dob))
                    delta = jnp.sum(jnp.where(lanes(n, a), dl, 0.0), axis=1, keepdims=True)
                    get_e(2 * p + a).wait()
                    e = Es[a]
                    dS = (e.astype(f32) * (dot_t(dob, va) - delta)).astype(bf)
                    x1, x2, x3 = dot(dS, ka), dot_l(dS, qa), dot_l(e, da)

                    @pl.when(p + 1 < tiles)
                    def _(a=a):
                        get_e(2 * p + 2 + a).start()

                    dqv = x1 if a == 0 else dqv + x1
                    dkv = x2 if a == 0 else dkv + x2
                    dvv = x3 if a == 0 else dvv + x3
                dq[:, c] = dqv * 0.125
                dK[:, c] = dkv[:n]
                dV[:, c] = dvv[:n]
                sK[:, c] = dkv[n:].astype(bf)
                sV[:, c] = dvv[n:].astype(bf)

                @pl.when(p == main // 128 - 1)
                def _():
                    pl.semaphore_wait(free.at[1], 1)
                    for copy in give[0]:
                        copy.start()

                return 0

            lax.fori_loop(0, tiles, pair, 0)
            return late

        def run(Es):
            late = pairs(Es)
            for copy in give[1]:
                copy.start()
            for copy in late:
                copy.wait()

        pl.run_scoped(run, pltpu.VMEM((2, n, 2 * n), bf))
        swap_gb.wait_recv()
        weight_grad(0)
        at("main")
        for copy in give[1]:
            copy.wait_recv()
        lax.fori_loop(0, n // 48, tail_rows, 0)
        for copy in swap_a[1]:
            copy.start()

        def final(*rawv):
            states = [fetch(a, b) for a, b in zip(raw, rawv)] if weights else []
            gln1, tok, xv = dK, dq, lv
            get_x = fetch(x_h, xv)
            gln1[...] = dot_t(Gq[...], Wqv[...])
            gln1[...] += dot_t(Gk[...], Wkv[...])
            weight_grad(1)
            at("tail")
            gln1[...] += dot_t(Gv[top, :], Wvv[...])
            get_x.wait()
            norm_back(xv, gln1, gains[0:1, :], GB, tok, SM.at[0], 0)
            for j in range(J):
                tg[j] = tok[j * r : (j + 1) * r, :].astype(bf)
            back_tg.start()
            at("back_out")
            hops = [
                place.tees(),
                [place.at_x(k) for k in range(1, F)],
                [place.at_z(k) for k in range(1, C)],
            ]
            landed = 0
            for s, devices in enumerate(hops):
                copies = [sems.remote(SM.at[s], SML.at[landed + i], d) for i, d in enumerate(devices)]
                for copy in copies:
                    copy.start()
                at(f"hop{s}")
                total = SM[s]
                for i, copy in enumerate(copies):
                    copy.wait_recv()
                    total = total + SML[landed + i]
                for copy in copies:
                    copy.wait_send()
                landed += len(copies)
                SM[s + 1] = total
            small[...] = SM[len(hops)]
            if weights:
                for copy in states:
                    copy.wait()
                at("end")
                for i, pieces in enumerate(matrices(rawv, sums)):
                    for k, total in enumerate(squares(pieces)):
                        NV[2 * i + k : 2 * i + k + 1, :] = jnp.broadcast_to(total, (1, 128))
                copies = [sems.remote(NV, NVL.at[i], d) for i, d in enumerate(partners)]
                for copy in copies:
                    copy.start()
                for copy in copies:
                    copy.wait_recv()
                total = NV[...]
                for i in range(len(copies)):
                    total = total + NVL[i]
                norms[...] = total
                for copy in copies:
                    copy.wait_send()
            else:
                norms[...] = jnp.zeros(norms.shape, f32)
            for copy in swap_a[0] + swap_a[1] + give[0] + give[1]:
                copy.wait_send()

        pl.run_scoped(final, *[pltpu.VMEM(a.shape, f32) for a in raw])

    pl.run_scoped(
        attend,
        pltpu.VMEM((n, D), bf),
        pltpu.VMEM((n, D), f32),
        pltpu.VMEM((n, D), bf),
        pltpu.VMEM((D, D), bf),
        pltpu.VMEM((n, D), bf),
        *[pltpu.VMEM((n, D), f32)] * 3,
        *[pltpu.VMEM((n, D), bf)] * 2,
        pltpu.VMEM((2, H, n, D), bf),
        pltpu.VMEM((2 * n, D), bf),
        *[pltpu.VMEM((D, D), bf)] * 3,
    )
    for key in "FHGB":
        for part in groups[key]:
            part.settle()
    for back in (back_bo, back_tg):
        back.wait()
        back.finish()
    swap_gb.wait_send()


def block_call(F, C, T, R, n, weights, tokens, cotangent, wholes, raw, gains, inner, cos, sa, sb, bias):
    shape = tokens.shape
    J, r, D = shape
    H, Hd = T // 2, inner.shape[1]
    heads = D // T
    nh = D // HD
    outs = [(shape, bf), (shape, bf), ((R, 4 * heads + 3 * Hd), f32), ((16, D), f32), ((8, 128), f32)]
    out_specs = [HBM, HBM, VMEM, VMEM, VMEM]
    saved = [((T, D, 3 * Hd) if weights else (8, 128), bf), ((n, D), f32), ((2 * n, D), bf), ((n, D), bf)]
    saved += [((2 * n, D), bf)] * 2 + [((nh, n, 2 * n), bf), ((n, D), f32), ((n, D), bf)] + [((D, D), bf)] * 4
    outs += saved
    out_specs += [HBM] * len(saved)
    grads = [((H, D, 3 * Hd), bf), ((H, D, D), bf)]
    if not weights:
        outs += grads
        out_specs += [VMEM, VMEM]
    small = (8, 128)
    scratch = [((T,) + inner.shape, f32)] + [((2 * n, D), bf)] * 3
    scratch += [((H, n, 3 * Hd), bf), ((n, D), f32), (shape, bf), (shape, bf)]
    everyone = F * C * T - 1 if weights else 1
    scratch += [((4, 16, D), f32), ((T + F + C - 3, 16, D), f32), (small, f32), ((everyone,) + small, f32)]
    scratch += [((T, D, D), bf), grads[1] if weights else (small, bf)]
    scratch += [((R, D), bf), ((R, 3 * Hd), bf)] if weights else [(small, bf)] * 2
    scratch = [pltpu.VMEM(s, d) for s, d in scratch]
    scratch += [
        pltpu.SemaphoreType.DMA((320,)),
        pltpu.SemaphoreType.DMA((320,)),
        pltpu.SemaphoreType.DMA((64,)),
        pltpu.SemaphoreType.REGULAR((2,)),
    ]
    if weights:
        scratch += reduce_lands(REDUCE_H + REDUCE_G + REDUCE_A, F, C, H, D, R)
    return pl.pallas_call(
        functools.partial(block_kernel, F, C, T, R, n, weights, PLAN),
        out_shape=[jax.ShapeDtypeStruct(s, d) for s, d in outs],
        in_specs=[HBM] * (2 + len(wholes) + len(raw)) + [VMEM] * 6,
        out_specs=out_specs,
        scratch_shapes=scratch,
        compiler_params=pltpu.CompilerParams(collective_id=1, has_side_effects=True, vmem_limit_bytes=LIMIT),
    )(tokens, cotangent, *wholes, *raw, gains, inner, cos, sa, sb, bias)


def matrices(raw, sums):
    heads, hidden = raw[0].shape[2], raw[6].shape[2]
    base, wide = 4 * heads, heads * 2 // 3

    def of_heads(g):
        a, b = sums[:, g * wide : (g + 1) * wide], 4 * wide + g * (heads - wide)
        return jnp.concatenate([a, sums[:, b : b + heads - wide]], axis=1)

    f = [sums[:, base + i * hidden : base + (i + 1) * hidden] for i in range(3)]
    return [
        [tuple(r[i] for r in raw[0:3]) + (of_heads(i),) for i in range(3)],
        [tuple(r[...] for r in raw[3:6]) + (of_heads(3),)],
        [tuple(r[i] for r in raw[6:9]) + (f[i],) for i in range(2)],
        [tuple(r[...] for r in raw[9:12]) + (f[2],)],
    ]


def squares(pieces):
    a = b = 0.0
    for w, m, v, g in pieces:
        u = moments(g, m, v)[2] + DECAY * w
        a = a + jnp.sum(w * w, keepdims=True)
        b = b + jnp.sum(u * u, keepdims=True)
    return a, b


def step_kernel(T, *refs):
    raw, (sums, norms, small, bo, tg), rest = refs[:12], refs[12:17], refs[17:]
    lg, lm, lv, ig, im, iv = rest[:6]
    bo_out, tg_out = rest[6:8]
    outs, (lg_out, lm_out, lv_out, ig_out, im_out, iv_out, trust) = rest[8:20], rest[20:27]
    bo_out[...] = bo[...]
    tg_out[...] = tg[...].astype(f32)
    size = jnp.sqrt(norms[:, 0:1])
    for i, pieces in enumerate(matrices(raw, sums)):
        ratio = size[2 * i : 2 * i + 1] / size[2 * i + 1 : 2 * i + 2]
        for j, (w, m, v, g) in enumerate(pieces):
            m, v, u = moments(g, m, v)
            w = w - RATE * ratio * (u + DECAY * w)
            for k, value in enumerate((w, m, v)):
                if outs[3 * i + k].ndim == 3:
                    outs[3 * i + k][j] = value
                else:
                    outs[3 * i + k][...] = value
        trust[i : i + 1, 0:1] = size[2 * i : 2 * i + 1]
        trust[i : i + 1, 1:2] = size[2 * i + 1 : 2 * i + 2]
    hidden = ig.shape[1]
    me = lax.axis_index("tp")
    mine = small[8:10, 0:hidden]
    for t in range(1, T):
        mine = jnp.where(me == t, small[8 + 2 * t : 10 + 2 * t, 0:hidden], mine)
    for grad, old, new in (
        (small[0:4, :], (lg, lm, lv), (lg_out, lm_out, lv_out)),
        (mine, (ig, im, iv), (ig_out, im_out, iv_out)),
    ):
        m, v, u = moments(grad, old[1][...], old[2][...])
        new[0][...] = old[0][...] - RATE_GAINS * u
        new[1][...] = m
        new[2][...] = v

def moments(gradient, moment, square):
    moment = BETA_ONE * moment + (1.0 - BETA_ONE) * gradient
    square = BETA_TWO * square + (1.0 - BETA_TWO) * gradient * gradient
    update = (
        moment / (1.0 - BETA_ONE**STEP) / (jnp.sqrt(square / (1.0 - BETA_TWO**STEP)) + EPS_ADAM)
    )
    return (moment, square, update)


def body(
    F, C, T,
    tokens, cotangent, layer_gains, layer_first, layer_second, inner_gains, inner_first, inner_second,
    attend_weight, attend_first, attend_second, merge_weight, merge_first, merge_second,
    expand_weight, expand_first, expand_second, shrink_weight, shrink_first, shrink_second,
):
    bf, f32 = jnp.bfloat16, jnp.float32
    D = tokens.shape[-1]
    R = attend_weight.shape[1]
    rows = tokens.shape[1]
    J = C * T // 2
    assert J == tokens.shape[0]
    n = -(-J * rows // 48) * 48
    heads = attend_weight.shape[2]
    hidden = expand_weight.shape[2]
    fast = R % 16 == 0
    low = lax.axis_index("tp") % 2
    slots = jnp.arange(J, dtype=jnp.int32) * 2
    cos, sa, sb = rotary_tables(slots + low, rows, n)
    bias = jnp.concatenate([key_bias(slots + low, rows, n), key_bias(slots + 1 - low, rows, n)])[None]
    raw = (
        attend_weight, attend_first, attend_second, merge_weight.T, merge_first.T, merge_second.T,
        expand_weight, expand_first, expand_second, shrink_weight.T, shrink_first.T, shrink_second.T,
    )
    wholes = ()
    if not fast:
        wide = heads * 2 // 3
        four = [raw[0][0], raw[0][1], raw[0][2], raw[3]]
        pack_a = jnp.concatenate([w[:, :wide] for w in four] + [w[:, wide:] for w in four], axis=1).astype(bf)
        pack_f = jnp.concatenate([raw[6][0], raw[6][1], raw[9]], axis=1).astype(bf)
        wholes = tuple(
            lax.all_gather(lax.all_gather(p, ("fsdp", "ctx"), axis=0, tiled=True), "tp", axis=0)
            for p in (pack_a, pack_f)
        )
    out = block_call(
        F, C, T, R, n, fast, tokens, cotangent, wholes, raw, layer_gains, inner_gains, cos, sa, sb, bias
    )
    bo, tg, sums, small, norms = out[:5]
    if not fast:
        sums = jnp.concatenate([out[-1], out[-2]], axis=2).astype(f32)
        same = [[t for t in range(T) if t % 2 == k] for k in range(2)]
        sums = lax.psum_scatter(sums, "tp", scatter_dimension=0, axis_index_groups=same, tiled=False)
        sums = lax.psum_scatter(sums, ("fsdp", "ctx"), scatter_dimension=0, tiled=True)
        parts = []
        for pieces in matrices(raw, sums):
            parts += [a[0, 0] for a in squares(pieces)]
        parts = lax.psum(jnp.stack(parts), ("fsdp", "ctx", "tp"))
        norms = jnp.broadcast_to(parts[:, None], (8, 128))
    gains = (layer_gains, layer_first, layer_second, inner_gains, inner_first, inner_second)
    outs = [(tokens.shape, bf), (tokens.shape, f32)] + [(a.shape, f32) for a in raw + gains] + [((4, 2), f32)]
    outs = local_call(functools.partial(step_kernel, T), [*raw, sums, norms, small, bo, tg, *gains], outs)
    return tuple(a.T if 5 <= i < 8 or 11 <= i < 14 else a for i, a in enumerate(outs))


def solution(mesh):
    tok = P("fsdp", ("ctx", "tp"), None)
    wide = P(None, ("fsdp", "ctx"), "tp")
    tall = P("tp", ("fsdp", "ctx"))
    split = P(None, "tp")
    sizes = (mesh.shape["fsdp"], mesh.shape["ctx"], mesh.shape["tp"])
    return jax.shard_map(
        functools.partial(body, *sizes),
        mesh=mesh,
        in_specs=(tok, tok, P(), P(), P(), split, split, split)
        + (wide,) * 3 + (tall,) * 3 + (wide,) * 3 + (tall,) * 3,
        out_specs=(tok, tok) + (wide,) * 3 + (tall,) * 3 + (wide,) * 3 + (tall,) * 3
        + (P(),) * 3 + (split,) * 3 + (P(),),
        check_vma=False,
    )
```

```python
import functools
import jax
import jax.numpy as jnp
from jax import lax
from jax.experimental import pallas as pl
from jax.experimental.pallas import tpu as pltpu
from jax.sharding import PartitionSpec as P

HD = 64
GRID = 32
STEP = 5
VALID = 1025
BETA_ONE = 0.5
BETA_TWO = 0.5
EPS_ADAM = 1e-06
DECAY = 0.01
RATE = 0.5
RATE_GAINS = 0.3
MESH = pl.DeviceIdType.MESH
f32 = jnp.float32
bf = jnp.bfloat16


class Place:
    def __init__(self, F, C, T):
        self.F, self.C, self.T, self.H = F, C, T, T // 2
        self.f = lax.axis_index("fsdp")
        self.c = lax.axis_index("ctx")
        self.t = lax.axis_index("tp")
        self.low = lax.rem(self.t, 2)
        self.high = lax.div(self.t, 2)
        self.pair = self.c * self.H + self.high
        self.pairs = C * self.H
        self.sibling = {"tp": self.t + 1 - 2 * self.low}
        self.xs = [lax.rem(self.f + k, F) for k in range(F)]
        self.ys = [lax.rem(self.high + k, self.H) for k in range(self.H)]
        self.zs = [lax.rem(self.c + k, C) for k in range(C)]

    def at_x(self, k):
        return {"fsdp": self.xs[k]}

    def at_y(self, k):
        return {"tp": self.ys[k] * 2 + self.low}

    def at_z(self, k):
        return {"ctx": self.zs[k]}

    def pair_at(self, k):
        i = lax.rem(self.pair + k, self.pairs)
        return i, {"ctx": lax.div(i, self.H), "tp": lax.rem(i, self.H) * 2 + self.low}

    def tees(self):
        return [{"tp": lax.rem(self.t + k, self.T)} for k in range(1, self.T)]

    def everyone(self):
        return [
            {"fsdp": self.xs[a], "ctx": self.zs[b], "tp": lax.rem(self.t + d, self.T)}
            for a in range(self.F) for b in range(self.C) for d in range(self.T) if a + b + d
        ]

    def partners(self, with_x):
        out = self.tees() + [
            {"ctx": self.zs[c], "tp": self.ys[y] * 2 + self.low} for c in range(1, self.C) for y in range(self.H)
        ]
        if with_x:
            out += [self.at_x(k) for k in range(1, self.F)]
        return out


def hail(partners):
    barrier = pltpu.get_barrier_semaphore()
    for partner in partners:
        pl.semaphore_signal(barrier, inc=1, device_id=partner, device_id_type=MESH)


def heard(partners):
    pl.semaphore_wait(pltpu.get_barrier_semaphore(), len(partners))


class Sems:
    def __init__(self, send, recv):
        self.send, self.recv, self.n = send, recv, 0

    def remote(self, src, dst, device):
        i = self.n
        self.n += 1
        return pltpu.make_async_remote_copy(
            src, dst, self.send.at[i], self.recv.at[i], device_id=device, device_id_type=MESH
        )

    def local(self, src, dst):
        i = self.n
        self.n += 1
        return pltpu.make_async_copy(src, dst, self.send.at[i])


class Exchange:
    def __init__(self, place, sems, src, dst):
        self.own = sems.local(src.at[place.pair], dst.at[place.pair])
        self.copies = []
        for k in range(1, place.pairs):
            i, device = place.pair_at(k)
            self.copies.append(sems.remote(src.at[i], dst.at[place.pair], device))

    def start(self, first=0, last=None):
        for copy in ([self.own] + self.copies)[first:last]:
            copy.start()

    def wait(self):
        self.own.wait()
        for copy in self.copies:
            copy.wait_recv()

    def finish(self):
        for copy in self.copies:
            copy.wait_send()


class Gather:
    def __init__(self, place, sems, pack, whole, cols, first):
        P, R = place, pack.shape[0]
        C, F, H = P.C, P.F, P.H
        n = C * R
        window = pl.ds(*cols)

        def push(t, row, rows, device):
            block = whole.at[t, pl.ds(pl.multiple_of(row, 16), rows), window]
            return sems.remote(block, block, device)

        row = (P.f * C + P.c) * R
        base = P.f * n
        self.own = sems.local(
            pack.at[:, window], whole.at[P.t, pl.ds(pl.multiple_of(row, 16), R), window]
        )
        chain = []
        for j in range(1, C):
            right = push(P.t, (P.f * C + jnp.maximum(P.c - j + 1, 0)) * R, R, P.at_z(1))
            left = push(P.t, (P.f * C + jnp.minimum(P.c + j - 1, C - 1)) * R, R, P.at_z(C - 1))
            chain.append([
                (right, jnp.logical_and(P.c + 1 < C, P.c - j + 1 >= 0), P.c - j >= 0),
                (left, jnp.logical_and(P.c >= 1, P.c + j - 1 < C), P.c + j < C),
            ])
        self.chain = chain
        tees = [y * 2 + P.low for y in P.ys]
        if first == "y":
            second = [push(P.t, base, n, P.at_y(k)) for k in range(1, H)]
            third = [push(t, base, n, P.at_x(k)) for k in range(1, F) for t in tees]
            over_3 = [push(t, base, n, P.sibling) for t in tees[1:]]
            over_4 = [push(t, P.xs[k] * n, n, P.sibling) for k in range(1, F) for t in tees]
        else:
            second = [push(P.t, base, n, P.at_x(k)) for k in range(1, F)]
            third = [push(P.t, 0, n * F, P.at_y(k)) for k in range(1, H)]
            over_3 = [push(P.t, P.xs[k] * n, n, P.sibling) for k in range(1, F)]
            over_4 = [push(t, 0, n * F, P.sibling) for t in tees[1:]]
        over_2 = [push(P.t, base, n, P.sibling)]
        none = [[] for _ in chain]
        self.waits = none + [[], second, third]
        self.starts = none + [second + over_2, third + over_3, over_4]
        self.sent_over = over_2 + over_3 + over_4

    def stage(self, s):
        if s == 0:
            self.own.wait()
        if 0 < s <= len(self.chain):
            for copy, _, gets in self.chain[s - 1]:
                pl.when(gets)(copy.wait_recv)
        for copy in self.waits[s]:
            copy.wait_recv()
        if s < len(self.chain):
            for copy, sends, _ in self.chain[s]:
                pl.when(sends)(copy.start)
        for copy in self.starts[s]:
            copy.start()

    def finish(self):
        for copy in self.sent_over:
            copy.wait_recv()

    def settle(self):
        for step in self.chain:
            for copy, sends, _ in step:
                pl.when(sends)(copy.wait_send)
        for group in self.starts:
            for copy in group:
                copy.wait_send()


def by_rows(rows, step, body):
    def it(i, _):
        body(pl.multiple_of(i * step, step), step)
        return 0

    lax.fori_loop(0, rows // step, it, 0)


class Reduce:
    def __init__(self, place, sems, view, D, width, first, lands, out, out_col, R):
        P, n = place, place.C * R
        C, F, H = P.C, P.F, P.H
        L1, L2, L3 = lands
        self.out, self.to, self.R = out, pl.ds(out_col, width), R
        base = pl.multiple_of(P.f * n, 16)
        mine = pl.multiple_of(base + P.c * R, 16)
        self.copies = [[], [], []]

        def rows(u, start, count):
            return view(u, pl.ds(start, count))

        def send(stage, src, dst, device):
            self.copies[stage].append(sems.remote(src, dst, device))

        if first == "x":
            for k in range(1, F):
                for u in range(H):
                    send(0, rows(u, pl.multiple_of(P.xs[k] * n, 16), n), L1.at[k - 1, u], P.at_x(k))
            for k in range(1, H):
                send(1, rows(P.ys[k], base, n), L2.at[k - 1], P.at_y(k))
            self.adds = [
                [(rows(u, base, n), [L1.at[k - 1, u] for k in range(1, F)]) for u in range(H)],
                [(rows(P.high, base, n), [L2.at[k - 1] for k in range(1, H)])],
            ]
        else:
            for k in range(1, H):
                send(0, rows(P.ys[k], 0, D), L1.at[k - 1], P.at_y(k))
            for k in range(1, F):
                send(1, rows(P.high, pl.multiple_of(P.xs[k] * n, 16), n), L2.at[k - 1], P.at_x(k))
            self.adds = [
                [(rows(P.high, 0, D), [L1.at[k - 1] for k in range(1, H)])],
                [(rows(P.high, base, n), [L2.at[k - 1] for k in range(1, F)])],
            ]
        for k in range(1, C):
            send(2, rows(P.high, pl.multiple_of(base + P.zs[k] * R, 16), R), L3.at[k - 1], P.at_z(k))
        self.last = (rows(P.high, mine, R), [L3.at[k - 1] for k in range(1, C)])

    def stage(self, s):
        if s > 0:
            for copy in self.copies[s - 1]:
                copy.wait_recv()
        if s in (1, 2):
            for dst, lands in self.adds[s - 1]:

                def add(r, k, dst=dst, lands=lands):
                    v = dst[pl.ds(r, k), :].astype(f32)
                    for land in lands:
                        v = v + land[pl.ds(r, k), :].astype(f32)
                    dst[pl.ds(r, k), :] = v.astype(bf)

                by_rows(dst.shape[0], 96, add)
        if s == 3:
            dst, lands = self.last
            v = dst[...].astype(f32)
            for land in lands:
                v = v + land[...].astype(f32)
            self.out[:, self.to] = v
        else:
            for copy in self.copies[s]:
                copy.start()

    def settle(self):
        for group in self.copies:
            for copy in group:
                copy.wait_send()


def reduce_lands(parts, F, C, H, D, R):
    out = []
    for (_, n), first in parts:
        if first == "x":
            out += [(F - 1, H, C * R, n), (H - 1, C * R, n)]
        else:
            out += [(H - 1, D, n), (F - 1, C * R, n)]
        out.append((C - 1, R, n))
    return [pltpu.VMEM(s, bf) for s in out]
EPS=1e-6
def dot(a,b): return jnp.dot(a,b,preferred_element_type=f32)
def dot_t(a,b): return lax.dot_general(a,b,(((1,),(1,)),((),())),preferred_element_type=f32)
def dot_l(a,b): return lax.dot_general(a,b,(((0,),(0,)),((),())),preferred_element_type=f32)

def chunks(rows, step, body):
    def it(i,_):
        body(pl.ds(pl.multiple_of(i*step,step),step)); return 0
    lax.fori_loop(0,rows//step,it,0)

def norm(v):
    mean=jnp.mean(v,axis=-1,keepdims=True)
    var=jnp.mean(v*v,axis=-1,keepdims=True)-mean*mean
    inv=lax.rsqrt(var+EPS)
    return (v-mean)*inv, inv

def spread(src3, dst):
    J,r,D=src3.shape
    n=dst.shape[0]
    pad=n-J*r
    if pad: dst[n-16:n,:]=jnp.zeros((16,D),f32)
    for j in range(J):
        dst[j*r:(j+1)*r,:]=src3[j].astype(f32)

def join(WA, g, dst, T):
    def it(i,_):
        s=pl.ds(pl.multiple_of(i*96,96),96)
        for t in range(T):
            dst[s,128*t:128*t+128]=WA[t,s,128*g:128*g+128]
        for u in range(T//2):
            c=pl.ds(512+128*(g//2),128)
            a=WA[2*u,s,c].astype(f32); b=WA[2*u+1,s,c].astype(f32)
            if g%2==0: b=pltpu.roll(b,64,1)
            else: a=pltpu.roll(a,64,1)
            dst[s,128*(T+u):128*(T+u)+128]=jnp.where(lanes(96,0),a,b).astype(bf)
        return 0
    lax.fori_loop(0,WA.shape[1]//96,it,0)

def turn(v, cos, sa, sb):
    n=v.shape[1]
    out=[]
    for i in range(n//128):
        a=v[:,i*128:(i+1)*128]
        out.append(a*cos+pltpu.roll(a,128-16,1)*sa+pltpu.roll(a,16,1)*sb)
    return jnp.concatenate(out,axis=1)

def normal(x, gains, ln1):
    def ln(s):
        v,_=norm(x[s,:])
        ln1[s,:]=(v*gains[0:1,:]+gains[1:2,:]).astype(bf)
    chunks(x.shape[0],48,ln)


def project(ln1, W, cos, sa, sb, dst, scale=None):
    n=ln1.shape[0]//2
    y=dot(ln1[0:n,:],W[...])
    if cos is not None: y=turn(y,cos[...],sa[...],sb[...])
    if scale is not None: y=y*scale
    dst[0:n,:]=y.astype(bf)


def lanes(n, a):
    return (lax.broadcasted_iota(jnp.int32,(n,128),1)//64==a)

def attention(q,K,V,bias,Es,linv,att,before,after):
    n=q.shape[0]; m=K.shape[0]
    def pair(p,_):
        c=pl.ds(pl.multiple_of(p*128,128),128)
        k2=K[:,c]; v2=V[:,c]
        q2=q[:,c]
        o=None; li=[]
        for a in (0,1):
            before(p,a)
            ka=jnp.where(lanes(m,a),k2,jnp.zeros_like(k2))
            va=jnp.where(lanes(m,a),v2,jnp.zeros_like(v2))
            S=dot_t(q2,ka)+bias[0:1,:]
            mx=jnp.max(S,axis=1,keepdims=True)
            e=jnp.exp(S-mx)
            l=1.0/jnp.sum(e,axis=1,keepdims=True)
            eb=e.astype(bf)
            Es[a]=eb
            after(p,a)
            oa=dot(eb,va)*l
            o=oa if o is None else o+oa
            li.append(l)
        att[:,c]=o.astype(bf)
        linv[:,c]=jnp.where(lanes(n,0),li[0],li[1])
        return 0
    lax.fori_loop(0,q.shape[1]//128,pair,0)

def merge(att,Wm,x,mid,gains,ln2,n):
    mid[...]=x[...]+dot_t(att[...],Wm[...])
    def ln(s):
        v,_=norm(mid[s,:])
        ln2[s,:]=(v*gains[2:3,:]+gains[3:4,:]).astype(bf)
    chunks(n,48,ln)

def norm_back(src, e_src, gain, add, dst, lay, row):
    n=src.shape[0]
    lay[row:row+2,:]=jnp.zeros((2,src.shape[1]),f32)
    def it(s):
        a,inv=norm(src[s,:]); e=e_src[s,:]
        lay[row:row+1,:]+=jnp.sum(e*a,axis=0,keepdims=True)
        lay[row+1:row+2,:]+=jnp.sum(e,axis=0,keepdims=True)
        eg=e*gain
        d=add[s,:].astype(f32)+inv*(eg-jnp.mean(eg,axis=1,keepdims=True)-a*jnp.mean(eg*a,axis=1,keepdims=True))
        dst[s,:]=d.astype(dst.dtype)
    chunks(n,48,it)


VMEM = pl.BlockSpec(memory_space=pltpu.VMEM)
HBM = pl.BlockSpec(memory_space=pl.ANY)
LIMIT = 60 * 2**20


def local_call(body, ins, outs, scratch=(), flops=0):
    return pl.pallas_call(
        body,
        out_shape=[jax.ShapeDtypeStruct(s, d) for s, d in outs],
        in_specs=[VMEM] * len(ins),
        out_specs=[VMEM] * len(outs),
        scratch_shapes=[pltpu.VMEM(s, d) for s, d in scratch],
        compiler_params=pltpu.CompilerParams(vmem_limit_bytes=LIMIT),
    )(*ins)


def rotary_tables(slots, rows, total):
    quarter = HD // 4
    positions = (slots[:, None] * rows + jnp.arange(rows, dtype=jnp.int32)).reshape(-1)
    inside = (positions >= 1) & (positions <= GRID * GRID)
    patch = jnp.where(inside, positions - 1, 0)
    frequency = 10000.0 ** (-jnp.arange(quarter, dtype=jnp.float32) / quarter)
    row_angle = (patch // GRID).astype(jnp.float32)[:, None] * frequency
    column_angle = (patch % GRID).astype(jnp.float32)[:, None] * frequency
    angles = jnp.concatenate([row_angle, row_angle, column_angle, column_angle], axis=-1)
    angles = jnp.pad(angles, ((0, total - angles.shape[0]), (0, 0)))
    angles = jnp.concatenate([angles, angles], axis=-1)
    sine = jnp.sin(angles)
    first = (jnp.arange(2 * HD) // quarter) % 2 == 0
    return jnp.cos(angles), jnp.where(first, -sine, 0.0), jnp.where(first, 0.0, sine)


def key_bias(slots, rows, total):
    positions = (slots[:, None] * rows + jnp.arange(rows, dtype=jnp.int32)).reshape(-1)
    bias = jnp.where(positions < VALID, 0.0, -1e30).astype(jnp.float32)
    return jnp.pad(bias, (0, total - bias.shape[0]), constant_values=-1e30)


GATHER_A = (((0, 384), "y"), ((384, 384), "x"))
GATHER_F = tuple(((256 * i, 256), k) for i, k in enumerate("yxyxyx"))
FIRST_F = 4
REDUCE_H = (((1024, 256), "x"), ((1280, 256), "y"))
REDUCE_G = (((0, 256), "x"), ((256, 256), "y"), ((512, 256), "x"), ((768, 256), "y"))
REDUCE_A = (((0, 256), "x"), ((256, 256), "y"), ((512, 128), "x"), ((640, 128), "y"))
PLAN = {
    "start": ("A00", "A10"),
    "line1": ("A01", "A11", "F00", "F10"),
    "line2": ("A02", "A12", "F01", "F11"),
    "z": ("A03", "A13", "F02", "F12"),
    "early": ("A04", "A14", "F03", "F13", "F20", "F30", "F40", "F50"),
    "tokens": ("F21", "F31", "F41", "F51"),
    "last": ("A05", "A15", "F22", "F32", "F42", "F52"),
    "k": ("F04", "F14"),
    "v": ("F23", "F33"),
    "q": ("F43", "F53"),
    "p1": ("cot",),
    "p2": ("F24", "F34"),
    "o3": ("F05", "F15"),
    "o5": ("F44", "F54"),
    "merged": ("F25", "F35"),
    "ones": ("F45", "F55"),
    "shrunk": ("H00", "H10"),
    "expanded0": ("H01", "H11", "G00"),
    "expanded1": ("G10",),
    "expanded2": ("G20",),
    "expanded3": ("G30",),
    "back1": ("H02", "H12", "G01"),
    "back3": ("G11",),
    "back4": ("G21", "H03", "H13"),
    "back5": ("G12",),
    "looped": ("G31", "G02"),
    "main": ("B00", "B10", "G22"),
    "tailed": ("G32",),
    "tail": ("B20", "B30"),
    "back_out": ("B01", "B11"),
    "hop0": ("B21", "B31"),
    "hop1": ("B02", "B12"),
    "hop2": ("B22", "B32", "tg", "G03", "G13", "G23", "G33"),
    "end": ("B03", "B13", "B23", "B33"),
}


def mine_and_theirs(tiles, low):
    a, b = tiles
    return jnp.where(low == 0, a, b), jnp.where(low == 0, b, a)


def halves(tile, low):
    other = pltpu.roll(tile, 64, 1)
    return jnp.where(low == 0, tile, other), jnp.where(low == 0, other, tile)


def block_kernel(F, C, T, R, n, weights, plan, tok, cot, *rest):
    if weights:
        WF_in = None
    else:
        (WA_in, WF_in), rest = rest[:2], rest[2:]
    raw, rest = rest[:12], rest[12:]
    gains, inner, cos, sa, sb, bias = rest[:6]
    bo_out, tg_out, sums, small, norms = rest[6:11]
    WF, x_h, ln1_h, q_h, K_h, V_h, E, linv_h, att_h = rest[11:20]
    W_h = rest[20:24]
    rest = rest[24:]
    if not weights:
        (GF, GA), rest = rest[:2], rest[2:]
    (IG, LN2, CT, GB, XO, mid, cin, tg, SM, SML, NV, NVL, big, GA_s, pa, pf, send, recv, local, free) = rest[:20]
    lands = rest[20:]
    place = Place(F, C, T)
    H, low, sib = place.H, place.low, place.sibling
    sems = Sems(send, recv)
    partners = place.everyone() if weights else place.partners(True)
    hail(partners)
    bo = cin
    J, r, D = bo.shape
    Hd = IG.shape[2]
    tiles = D // 128
    main = T * 128
    wide = D // T * 2 // 3
    top, bottom = pl.ds(0, n), pl.ds(n, n)
    nlocal = [0]
    ig = IG

    def slots(count):
        nlocal[0] += count
        return nlocal[0] - count

    def fetch(src, dst):
        copy = pltpu.make_async_copy(src, dst, local.at[slots(1)])
        copy.start()
        return copy

    if weights:
        GA = GA_s

        def GF(u, rows, start, size):
            return big.at[2 * u + start // D, rows, pl.ds(start % D, size)]

        WA = big
    else:
        WA = WA_in

    tokens = Exchange(place, sems, tok, tg)
    cots = Exchange(place, sems, cot, cin)
    swap_ln2 = sems.remote(LN2.at[top], LN2.at[bottom], sib)
    swap_ct = sems.remote(CT.at[top], CT.at[bottom], sib)
    swap_gb = sems.remote(GB.at[top], GB.at[bottom], sib)
    back_bo = Exchange(place, sems, bo, bo_out)
    back_tg = Exchange(place, sems, tg, tg_out)
    share = [sems.remote(inner, IG.at[place.t], device) for device in place.tees()]
    groups = {"A": [], "F": [], "H": [], "G": [], "B": []}
    if weights:
        for key, pack, whole, parts in (("A", pa, WA, GATHER_A), ("F", pf, WF, GATHER_F)):
            groups[key] = [Gather(place, sems, pack, whole, cols, first) for cols, first in parts]
        i = 0
        for key, parts in (("H", REDUCE_H), ("G", REDUCE_G), ("B", REDUCE_A)):
            for (start, size), first in parts:
                if key == "B":
                    view = lambda u, rows, c=pl.ds(start, size): GA.at[u, rows, c]
                    col = start
                else:
                    view = lambda u, rows, start=start, size=size: GF(u, rows, start, size)
                    col = D + start
                groups[key].append(
                    Reduce(place, sems, view, D, size, first, lands[3 * i : 3 * i + 3], sums, col, R)
                )
                i += 1

    def at(point):
        for step in plan.get(point, ()) if weights else ():
            if step == "cot":
                cots.start()
                continue
            if step == "tg":
                back_tg.start(place.pairs // 2, place.pairs)
                continue
            groups[step[0]][int(step[1])].stage(int(step[2]))

    def at_loop(name, index, count):
        for k in range(count):
            if weights and plan.get(f"{name}{k}"):

                @pl.when(index == k)
                def _(k=k):
                    at(f"{name}{k}")

    def wait_all(key):
        for g in groups[key]:
            g.finish()

    def forward(x, ln1, q, K, V, Wq, Wk, Wv, Wm, att, linv, Es, *states):
        Ws = (Wq, Wk, Wv, Wm)
        if weights:
            gets = [fetch(raw[k], states[i]) for i, k in enumerate((0, 3, 6, 9))]
            for copy in gets:
                copy.wait()
            aw, mw, ew, sw = states
            four = [aw[0], aw[1], aw[2], mw[...].T]
            for g, w in enumerate(four):
                pa[:, wide * g : wide * (g + 1)] = w[:, :wide].astype(bf)
            for g in (0, 2):
                pair = [w[:, wide:] for w in four[g : g + 2]]
                pa[:, 4 * wide + 64 * g : 4 * wide + 64 * g + 128] = jnp.concatenate(pair, axis=1).astype(bf)
            for g, w in enumerate((ew[0], ew[1], sw[...])):
                pf[:, Hd * g : Hd * (g + 1)] = w.astype(bf)
            for g in groups["A"] + groups["F"]:
                g.own.start()
        heard(partners)
        IG[place.t] = inner[...]
        at("start")
        for copy in share:
            copy.start()
        at("line1")
        at("line2")
        tokens.start()
        if not weights:
            cots.start()
        at("z")
        at("early")
        tokens.wait()
        at("tokens")
        spread(tg, x)
        normal(x, gains, ln1)
        swap_ln1 = sems.remote(ln1.at[top], XO.at[1, :, pl.ds(0, D)], sib)
        swap_ln1.start()
        at("normed")
        if weights:
            at("last")
            wait_all("A")
        else:
            whole = pltpu.make_async_copy(WA_in, big, local.at[slots(1)])
            whole.start()
            whole.wait()
        saves = [fetch(x, x_h), fetch(ln1.at[top], ln1_h.at[top])]
        swap = [sems.remote(X.at[top], XO.at[0, :, pl.ds(o, D)], sib) for X, o in ((K, 0), (V, D))]
        join(big, 1, Wk, T)
        project(ln1, Wk, cos, sa, sb, K)
        swap[0].start()
        at("k")
        join(big, 2, Wv, T)
        project(ln1, Wv, None, None, None, V)
        swap[1].start()
        at("v")
        join(big, 0, Wq, T)
        project(ln1, Wq, cos, sa, sb, q, 0.125)
        join(big, 3, Wm, T)
        at("q")
        saves += [fetch(a, b) for a, b in zip(Ws, W_h)] + [fetch(q, q_h)]
        for copy, X in zip(swap, (K, V)):
            copy.wait_recv()
        K[bottom, :] = XO[0, :, 0:D]
        V[bottom, :] = XO[0, :, D : 2 * D]
        saves += [fetch(K, K_h), fetch(V, V_h)]
        swap_ln1.wait_recv()
        saves += [fetch(XO.at[1, :, pl.ds(0, D)], ln1_h.at[bottom])]
        e0 = slots(2)

        def put_e(h):
            slot = lax.rem(h, 2)
            return pltpu.make_async_copy(Es.at[slot], E.at[h], local.at[e0 + slot])

        def before(p, a):
            at_loop("p" if a == 0 else "o", p, tiles)

            @pl.when(p > 0)
            def _():
                put_e(2 * p + a - 2).wait()

        def after(p, a):
            put_e(2 * p + a).start()

        attention(q, K, V, bias, Es, linv, att, before, after)
        at("attended")
        late = [fetch(linv, linv_h), fetch(att, att_h)]
        merge(att, Wm, x, mid, gains, LN2, n)
        swap_ln2.start()
        at("merged")
        for h in (2 * tiles - 2, 2 * tiles - 1):
            put_e(h).wait()
        for copy in saves + late:
            copy.wait()
        for copy in swap + [swap_ln1]:
            copy.wait_send()
        pl.semaphore_signal(free.at[0], inc=1, device_id=sib, device_id_type=MESH)

    pl.run_scoped(
        forward,
        pltpu.VMEM((n, D), f32),
        pltpu.VMEM((2 * n, D), bf),
        pltpu.VMEM((n, D), bf),
        pltpu.VMEM((2 * n, D), bf),
        pltpu.VMEM((2 * n, D), bf),
        *[pltpu.VMEM((D, D), bf)] * 4,
        pltpu.VMEM((n, D), bf),
        pltpu.VMEM((n, D), f32),
        pltpu.VMEM((2, n, 2 * n), bf),
        *[pltpu.VMEM(raw[k].shape, f32) for k in (0, 3, 6, 9)],
    )
    tokens.finish()
    for part in groups["A"]:
        part.settle()

    def feed(WFv, gate, up, act, gh, out, XT):
        w0 = slots(2)
        WF_from = WF if weights else WF_in

        def get_w(t, start, size):
            slot = lax.rem(t, 2)
            return pltpu.make_async_copy(
                WF_from.at[t, :, pl.ds(start, size)], WFv.at[slot, :, pl.ds(0, size)], local.at[w0 + slot]
            )

        def through(body, start, size, init):
            def step(t, c):
                get_w(t, start, size).wait()
                c = body(t, lax.rem(t, 2), c)

                @pl.when(t + 2 < T)
                def _():
                    get_w(t + 2, start, size).start()

                return c

            return lax.fori_loop(0, T, step, init)

        def ahead(start, size):
            for t in range(2):
                get_w(t, start, size).start()

        def swaps(cols):
            return [sems.remote(XT.at[2 * u + 1 - low, :, cols], XO.at[u, :, cols], sib) for u in range(H)]

        def pass_on(copies, t):
            for u, copy in enumerate(copies):

                @pl.when(t == 2 * u + 1 - low)
                def _(copy=copy):
                    copy.start()

        swap_h = swaps(pl.ds(2 * Hd, Hd))
        swap_g = swaps(pl.ds(0, 2 * Hd))
        at("feed")
        for g in groups["F"][:FIRST_F]:
            g.finish()
        ahead(0, 2 * Hd)
        def one(t, slot, c):
            at_loop("one", t, T)
            s0, s1 = c
            gu = dot(LN2[top, :], WFv[slot])
            g, u = gu[:, :Hd], gu[:, Hd:]
            a = g * jax.nn.sigmoid(g) * u
            gate[t] = g.astype(gate.dtype)
            up[t] = u.astype(up.dtype)
            act[t] = a
            return s0 + jnp.sum(a, axis=1, keepdims=True), s1 + jnp.sum(a * a, axis=1, keepdims=True)

        z = jnp.zeros((n, 1), f32)
        s0, s1 = through(one, 0, 2 * Hd, (z, z))
        at("ones")
        for g in groups["F"][FIRST_F:]:
            g.finish()
        ahead(2 * Hd, Hd)
        width = T * Hd
        mean = s0 / width
        inv = lax.rsqrt(s1 / width - mean * mean + EPS)
        SM[0] = jnp.zeros(SM.shape[1:], f32)
        cots.wait()
        spread(cin, out)
        CT[top, :] = out[...].astype(bf)
        swap_ct.start()
        out[...] = mid[...]
        pl.semaphore_wait(free.at[0], 1)
        for copy in share:
            copy.wait()

        def two(t, slot, c):
            r0, r1 = c
            n3 = (act[t] - mean) * inv
            act[t] = n3
            gt = ig[t, 0:1, :]
            hid = (n3 * gt + ig[t, 1:2, :]).astype(bf)
            XT[t, :, 2 * Hd : 3 * Hd] = hid
            pass_on(swap_h, t)
            out[...] += dot_t(hid, WFv[slot, :, 0:Hd])
            h = dot(CT[top, :], WFv[slot, :, 0:Hd])
            SM[0, pl.ds(8 + 2 * t, 1), 0:Hd] = jnp.sum(h * n3, axis=0, keepdims=True)
            SM[0, pl.ds(9 + 2 * t, 1), 0:Hd] = jnp.sum(h, axis=0, keepdims=True)
            e = h * gt
            gh[t] = e.astype(gh.dtype)
            return r0 + jnp.sum(e, axis=1, keepdims=True), r1 + jnp.sum(e * n3, axis=1, keepdims=True)

        r0, r1 = through(two, 2 * Hd, Hd, (z, z))
        ahead(0, 2 * Hd)
        r0, r1 = r0 / width, r1 / width
        swap_ct.wait_recv()
        swap_ln2.wait_recv()

        def put_f(u, start, value):
            if weights:
                GF(u, pl.ds(0, D), start, value.shape[1])[...] = value.astype(bf)
            else:
                GF[u, :, start : start + value.shape[1]] = value.astype(bf)

        for u in range(H):
            swap_h[u].wait_recv()
            t = 2 * u + low
            c = pl.ds(2 * Hd, Hd)
            put_f(u, 2 * Hd, dot_l(CT[top, :], XT[t, :, c]) + dot_l(CT[bottom, :], XO[u, :, c]))
        at("shrunk")
        for j in range(J):
            bo[j] = out[j * r : (j + 1) * r, :].astype(bf)
        back_bo.start()
        gln2 = out
        gln2[...] = jnp.zeros(gln2.shape, f32)

        def three(t, slot, _):
            at_loop("three", t, T)
            ga = inv * (gh[t].astype(f32) - r0 - act[t] * r1)
            g, u = gate[t].astype(f32), up[t].astype(f32)
            s = jax.nn.sigmoid(g)
            gg = (ga * u * s * (1.0 + g * (1.0 - s))).astype(bf)
            gu = (ga * g * s).astype(bf)
            XT[t, :, 0:Hd] = gg
            XT[t, :, Hd : 2 * Hd] = gu
            pass_on(swap_g, t)
            gln2[...] += dot_t(XT[t, :, 0 : 2 * Hd], WFv[slot])
            return 0

        through(three, 0, 2 * Hd, 0)
        at("threes")
        for u in range(H):
            swap_g[u].wait_recv()
            t = 2 * u + low
            for k in range(4):
                c = pl.ds(k * Hd // 2, Hd // 2)
                put_f(u, k * Hd // 2, dot_l(LN2[top, :], XT[t, :, c]) + dot_l(LN2[bottom, :], XO[u, :, c]))
                if u == H - 1:
                    at(f"expanded{k}")
        norm_back(mid, gln2, gains[2:3, :], CT, GB, SM.at[0], 2)
        swap_gb.start()
        at("fed")
        for copy in swap_h + swap_g + [swap_ln2, swap_ct]:
            copy.wait_send()
        pl.semaphore_signal(free.at[1], inc=1, device_id=sib, device_id_type=MESH)

    pl.run_scoped(
        feed,
        pltpu.VMEM((2, D, 2 * Hd), bf),
        pltpu.VMEM((T, n, Hd), bf),
        pltpu.VMEM((T, n, Hd), bf),
        pltpu.VMEM((T, n, Hd), f32),
        pltpu.VMEM((T, n, Hd), f32),
        pltpu.VMEM((n, D), f32),
        pltpu.VMEM((T, n, 3 * Hd), bf),
    )
    cots.finish()

    def attend(qv, lv, av, Wmv, gatt, dq, dK, dV, sK, sV, XT, LN1, Wqv, Wkv, Wvv):
        e0 = slots(2)

        cuts = [pl.ds(0, main), pl.ds(main, D - main)]
        give = [
            [sems.remote(S.at[:, cut], XO.at[0, :, pl.ds(off + cut.start, cut.size)], sib) for off, S in ((0, sK), (D, sV))]
            for cut in cuts
        ]
        swap_a = [
            [sems.remote(XT.at[1, u, :, cut], XO.at[1, :, pl.ds(H * cut.start + u * cut.size, cut.size)], sib) for u in range(H)]
            for cut in cuts
        ]
        Kv, Vv = LN2, CT
        Gq, Gk, Gv = gatt, qv, Kv

        def gradients(p, c):
            co, si, sj = cos[p, :], -sa[p, :], -sb[p, :]
            k0, v0 = pl.ds(c.start, c.size), pl.ds(D + c.start, c.size)
            g_q = turn(dq[p, c], co, si, sj)
            g_k = turn(dK[p, c] + XO[0, p, k0].astype(f32), co, si, sj)
            g_v = dV[p, c] + XO[0, p, v0].astype(f32)
            return g_q, g_k, g_v, av[p, c].astype(f32)

        def keep(p, c, values):
            for ref, v in zip((Gq, Gk, Gv), values):
                ref[p, c] = v.astype(bf)

        def main_rows(i, _):
            p = pl.ds(pl.multiple_of(i * 48, 48), 48)
            values = gradients(p, cuts[0])
            keep(p, cuts[0], values)
            for u in range(H):
                for g, v in enumerate(values):
                    two = v[:, 256 * u : 256 * u + 128], v[:, 256 * u + 128 : 256 * u + 256]
                    for side, z in enumerate(mine_and_theirs(two, low)):
                        XT[side, u, p, 128 * g : 128 * g + 128] = z.astype(bf)
            return 0

        def tail_rows(i, _):
            p = pl.ds(pl.multiple_of(i * 48, 48), 48)
            values = gradients(p, cuts[1])
            keep(p, cuts[1], values)
            first = lanes(48, 0)
            for u in range(H):
                split = [halves(v[:, 128 * u : 128 * u + 128], low) for v in values]
                for g in (0, 1):
                    (a0, b0), (a1, b1) = split[2 * g], split[2 * g + 1]
                    c = pl.ds(main + 128 * g, 128)
                    XT[0, u, p, c] = jnp.where(first, a0, b1).astype(bf)
                    XT[1, u, p, c] = jnp.where(first, b0, a1).astype(bf)
            return 0

        def weight_grad(k):
            for copy in swap_a[k]:
                copy.wait_recv()
            cut = cuts[k]
            for u in range(H):
                m = XT[0, u, :, cut]
                o = XO[1, :, H * cut.start + u * cut.size : H * cut.start + (u + 1) * cut.size]
                w = cut.size // 4
                if k == 0:
                    d = dot_l(LN1[top, :], m[:, : 3 * w]) + dot_l(LN1[bottom, :], o[:, : 3 * w])
                    e = dot_l(GB[top, :], m[:, 3 * w :]) + dot_l(GB[bottom, :], o[:, 3 * w :])
                    GA[u, :, 0 : 3 * w] = d.astype(bf)
                    GA[u, :, 3 * w : 4 * w] = e.astype(bf)
                else:
                    d = dot_l(LN1[top, :], m) + dot_l(LN1[bottom, :], o)
                    e = dot_l(GB[top, :], m) + dot_l(GB[bottom, :], o)
                    lane = lax.broadcasted_iota(jnp.int32, d.shape, 1)
                    GA[u, :, cut] = jnp.where(lane < 3 * w, d, e).astype(bf)

        def pairs(Es):
            def get_e(h):
                slot = lax.rem(h, 2)
                return pltpu.make_async_copy(E.at[h], Es.at[slot], local.at[e0 + slot])

            for h in range(2):
                get_e(h).start()
            gets = [fetch(a, b) for a, b in ((W_h[3], Wmv), (q_h, qv), (K_h, Kv), (V_h, Vv), (att_h, av), (linv_h, lv))]
            late = [fetch(a, b) for a, b in ((ln1_h, LN1), (W_h[0], Wqv), (W_h[1], Wkv), (W_h[2], Wvv))]
            gets[0].wait()
            gatt[...] = dot(GB[top, :], Wmv[...]).astype(bf)
            for copy in gets[1:]:
                copy.wait()

            def pair(p, _):
                at_loop("back", p, tiles)

                @pl.when(p == tiles - 1)
                def _():
                    for copy in give[0]:
                        copy.wait_recv()
                    lax.fori_loop(0, n // 48, main_rows, 0)
                    for copy in swap_a[0]:
                        copy.start()

                c = pl.ds(pl.multiple_of(p * 128, 128), 128)
                k2, v2, q2 = Kv[:, c], Vv[:, c], qv[:, c]
                dob = (gatt[:, c].astype(f32) * lv[:, c]).astype(bf)
                dl = dob.astype(f32) * av[:, c].astype(f32)
                m = 2 * n
                dqv = dkv = dvv = None
                for a in (0, 1):
                    ka = jnp.where(lanes(m, a), k2, jnp.zeros_like(k2))
                    va = jnp.where(lanes(m, a), v2, jnp.zeros_like(v2))
                    qa = jnp.where(lanes(n, a), q2, jnp.zeros_like(q2))
                    da = jnp.where(lanes(n, a), dob, jnp.zeros_like(dob))
                    delta = jnp.sum(jnp.where(lanes(n, a), dl, 0.0), axis=1, keepdims=True)
                    get_e(2 * p + a).wait()
                    e = Es[a]
                    dS = (e.astype(f32) * (dot_t(dob, va) - delta)).astype(bf)
                    x1, x2, x3 = dot(dS, ka), dot_l(dS, qa), dot_l(e, da)

                    @pl.when(p + 1 < tiles)
                    def _(a=a):
                        get_e(2 * p + 2 + a).start()

                    dqv = x1 if a == 0 else dqv + x1
                    dkv = x2 if a == 0 else dkv + x2
                    dvv = x3 if a == 0 else dvv + x3
                dq[:, c] = dqv * 0.125
                dK[:, c] = dkv[:n]
                dV[:, c] = dvv[:n]
                sK[:, c] = dkv[n:].astype(bf)
                sV[:, c] = dvv[n:].astype(bf)

                @pl.when(p == main // 128 - 1)
                def _():
                    pl.semaphore_wait(free.at[1], 1)
                    for copy in give[0]:
                        copy.start()

                return 0

            lax.fori_loop(0, tiles, pair, 0)
            return late

        def run(Es):
            late = pairs(Es)
            for copy in give[1]:
                copy.start()
            at("looped")
            for copy in late:
                copy.wait()

        pl.run_scoped(run, pltpu.VMEM((2, n, 2 * n), bf))
        swap_gb.wait_recv()
        weight_grad(0)
        at("main")
        for copy in give[1]:
            copy.wait_recv()
        lax.fori_loop(0, n // 48, tail_rows, 0)
        for copy in swap_a[1]:
            copy.start()
        at("tailed")

        def final(*rawv):
            states = [fetch(a, b) for a, b in zip(raw, rawv)] if weights else []
            gln1, tok, xv = dK, dq, lv
            get_x = fetch(x_h, xv)
            gln1[...] = dot_t(Gq[...], Wqv[...])
            gln1[...] += dot_t(Gk[...], Wkv[...])
            weight_grad(1)
            at("tail")
            gln1[...] += dot_t(Gv[top, :], Wvv[...])
            get_x.wait()
            norm_back(xv, gln1, gains[0:1, :], GB, tok, SM.at[0], 0)
            for j in range(J):
                tg[j] = tok[j * r : (j + 1) * r, :].astype(bf)
            at("back_out")
            back_tg.start(0, place.pairs // 2 if weights else place.pairs)
            hops = [
                place.tees(),
                [place.at_x(k) for k in range(1, F)],
                [place.at_z(k) for k in range(1, C)],
            ]
            landed = 0
            for s, devices in enumerate(hops):
                copies = [sems.remote(SM.at[s], SML.at[landed + i], d) for i, d in enumerate(devices)]
                for copy in copies:
                    copy.start()
                at(f"hop{s}")
                total = SM[s]
                for i, copy in enumerate(copies):
                    copy.wait_recv()
                    total = total + SML[landed + i]
                for copy in copies:
                    copy.wait_send()
                landed += len(copies)
                SM[s + 1] = total
            small[...] = SM[len(hops)]
            if weights:
                for copy in states:
                    copy.wait()
                at("end")
                for i, pieces in enumerate(matrices(rawv, sums)):
                    for k, total in enumerate(squares(pieces)):
                        NV[2 * i + k : 2 * i + k + 1, :] = jnp.broadcast_to(total, (1, 128))
                copies = [sems.remote(NV, NVL.at[i], d) for i, d in enumerate(partners)]
                for copy in copies:
                    copy.start()
                for copy in copies:
                    copy.wait_recv()
                total = NV[...]
                for i in range(len(copies)):
                    total = total + NVL[i]
                norms[...] = total
                for copy in copies:
                    copy.wait_send()
            else:
                norms[...] = jnp.zeros(norms.shape, f32)
            for copy in swap_a[0] + swap_a[1] + give[0] + give[1]:
                copy.wait_send()

        pl.run_scoped(final, *[pltpu.VMEM(a.shape, f32) for a in raw])

    pl.run_scoped(
        attend,
        pltpu.VMEM((n, D), bf),
        pltpu.VMEM((n, D), f32),
        pltpu.VMEM((n, D), bf),
        pltpu.VMEM((D, D), bf),
        pltpu.VMEM((n, D), bf),
        *[pltpu.VMEM((n, D), f32)] * 3,
        *[pltpu.VMEM((n, D), bf)] * 2,
        pltpu.VMEM((2, H, n, D), bf),
        pltpu.VMEM((2 * n, D), bf),
        *[pltpu.VMEM((D, D), bf)] * 3,
    )
    for key in "FHGB":
        for part in groups[key]:
            part.settle()
    for back in (back_bo, back_tg):
        back.wait()
        back.finish()
    swap_gb.wait_send()


def block_call(F, C, T, R, n, weights, tokens, cotangent, wholes, raw, gains, inner, cos, sa, sb, bias):
    shape = tokens.shape
    J, r, D = shape
    H, Hd = T // 2, inner.shape[1]
    heads = D // T
    nh = D // HD
    outs = [(shape, bf), (shape, bf), ((R, 4 * heads + 3 * Hd), f32), ((16, D), f32), ((8, 128), f32)]
    out_specs = [HBM, HBM, VMEM, VMEM, VMEM]
    saved = [((T, D, 3 * Hd) if weights else (8, 128), bf), ((n, D), f32), ((2 * n, D), bf), ((n, D), bf)]
    saved += [((2 * n, D), bf)] * 2 + [((nh, n, 2 * n), bf), ((n, D), f32), ((n, D), bf)] + [((D, D), bf)] * 4
    outs += saved
    out_specs += [HBM] * len(saved)
    grads = [((H, D, 3 * Hd), bf), ((H, D, D), bf)]
    if not weights:
        outs += grads
        out_specs += [VMEM, VMEM]
    small = (8, 128)
    scratch = [((T,) + inner.shape, f32)] + [((2 * n, D), bf)] * 3
    scratch += [((H, n, 3 * Hd), bf), ((n, D), f32), (shape, bf), (shape, bf)]
    everyone = F * C * T - 1 if weights else 1
    scratch += [((4, 16, D), f32), ((T + F + C - 3, 16, D), f32), (small, f32), ((everyone,) + small, f32)]
    scratch += [((T, D, D), bf), grads[1] if weights else (small, bf)]
    scratch += [((R, D), bf), ((R, 3 * Hd), bf)] if weights else [(small, bf)] * 2
    scratch = [pltpu.VMEM(s, d) for s, d in scratch]
    scratch += [
        pltpu.SemaphoreType.DMA((320,)),
        pltpu.SemaphoreType.DMA((320,)),
        pltpu.SemaphoreType.DMA((64,)),
        pltpu.SemaphoreType.REGULAR((2,)),
    ]
    if weights:
        scratch += reduce_lands(REDUCE_H + REDUCE_G + REDUCE_A, F, C, H, D, R)
    return pl.pallas_call(
        functools.partial(block_kernel, F, C, T, R, n, weights, PLAN),
        out_shape=[jax.ShapeDtypeStruct(s, d) for s, d in outs],
        in_specs=[HBM] * (2 + len(wholes) + len(raw)) + [VMEM] * 6,
        out_specs=out_specs,
        scratch_shapes=scratch,
        compiler_params=pltpu.CompilerParams(collective_id=1, has_side_effects=True, vmem_limit_bytes=LIMIT),
    )(tokens, cotangent, *wholes, *raw, gains, inner, cos, sa, sb, bias)


def matrices(raw, sums):
    heads, hidden = raw[0].shape[2], raw[6].shape[2]
    base, wide = 4 * heads, heads * 2 // 3

    def of_heads(g):
        a, b = sums[:, g * wide : (g + 1) * wide], 4 * wide + g * (heads - wide)
        return jnp.concatenate([a, sums[:, b : b + heads - wide]], axis=1)

    f = [sums[:, base + i * hidden : base + (i + 1) * hidden] for i in range(3)]
    return [
        [tuple(r[i] for r in raw[0:3]) + (of_heads(i),) for i in range(3)],
        [tuple(r[...] for r in raw[3:6]) + (of_heads(3).T,)],
        [tuple(r[i] for r in raw[6:9]) + (f[i],) for i in range(2)],
        [tuple(r[...] for r in raw[9:12]) + (f[2],)],
    ]


def squares(pieces):
    a = b = 0.0
    for w, m, v, g in pieces:
        u = moments(g, m, v)[2] + DECAY * w
        a = a + jnp.sum(w * w, keepdims=True)
        b = b + jnp.sum(u * u, keepdims=True)
    return a, b


def step_kernel(T, *refs):
    raw, (sums, norms, small, bo, tg), rest = refs[:12], refs[12:17], refs[17:]
    lg, lm, lv, ig, im, iv = rest[:6]
    bo_out, tg_out = rest[6:8]
    outs, (lg_out, lm_out, lv_out, ig_out, im_out, iv_out, trust) = rest[8:20], rest[20:27]
    for j in range(bo.shape[0]):
        tg_out[:, j, :] = tg[j].astype(f32)
    bo_out[...] = jnp.swapaxes(bo[...].astype(f32), 0, 1).astype(bf)
    size = jnp.sqrt(norms[:, 0:1])
    for i, pieces in enumerate(matrices(raw, sums)):
        ratio = size[2 * i : 2 * i + 1] / size[2 * i + 1 : 2 * i + 2]
        for j, (w, m, v, g) in enumerate(pieces):
            m, v, u = moments(g, m, v)
            w = w - RATE * ratio * (u + DECAY * w)
            for k, value in enumerate((w, m, v)):
                if outs[3 * i + k].ndim == 3:
                    outs[3 * i + k][j] = value
                else:
                    outs[3 * i + k][...] = value
        trust[i : i + 1, 0:1] = size[2 * i : 2 * i + 1]
        trust[i : i + 1, 1:2] = size[2 * i + 1 : 2 * i + 2]
    hidden = ig.shape[1]
    me = lax.axis_index("tp")
    mine = small[8:10, 0:hidden]
    for t in range(1, T):
        mine = jnp.where(me == t, small[8 + 2 * t : 10 + 2 * t, 0:hidden], mine)
    for grad, old, new in (
        (small[0:4, :], (lg, lm, lv), (lg_out, lm_out, lv_out)),
        (mine, (ig, im, iv), (ig_out, im_out, iv_out)),
    ):
        m, v, u = moments(grad, old[1][...], old[2][...])
        new[0][...] = old[0][...] - RATE_GAINS * u
        new[1][...] = m
        new[2][...] = v

def moments(gradient, moment, square):
    moment = BETA_ONE * moment + (1.0 - BETA_ONE) * gradient
    square = BETA_TWO * square + (1.0 - BETA_TWO) * gradient * gradient
    update = (
        moment / (1.0 - BETA_ONE**STEP) / (jnp.sqrt(square / (1.0 - BETA_TWO**STEP)) + EPS_ADAM)
    )
    return (moment, square, update)


def body(
    F, C, T,
    tokens, cotangent, layer_gains, layer_first, layer_second, inner_gains, inner_first, inner_second,
    attend_weight, attend_first, attend_second, merge_weight, merge_first, merge_second,
    expand_weight, expand_first, expand_second, shrink_weight, shrink_first, shrink_second,
):
    bf, f32 = jnp.bfloat16, jnp.float32
    D = tokens.shape[-1]
    R = attend_weight.shape[1]
    rows = tokens.shape[1]
    J = C * T // 2
    assert J == tokens.shape[0]
    n = -(-J * rows // 48) * 48
    heads = attend_weight.shape[2]
    hidden = expand_weight.shape[2]
    fast = R % 16 == 0
    low = lax.axis_index("tp") % 2
    slots = jnp.arange(J, dtype=jnp.int32) * 2
    cos, sa, sb = rotary_tables(slots + low, rows, n)
    bias = jnp.concatenate([key_bias(slots + low, rows, n), key_bias(slots + 1 - low, rows, n)])[None]
    raw = (
        attend_weight, attend_first, attend_second, merge_weight, merge_first, merge_second,
        expand_weight, expand_first, expand_second, shrink_weight.T, shrink_first.T, shrink_second.T,
    )
    wholes = ()
    if not fast:
        wide = heads * 2 // 3
        four = [raw[0][0], raw[0][1], raw[0][2], raw[3].T]
        pack_a = jnp.concatenate([w[:, :wide] for w in four] + [w[:, wide:] for w in four], axis=1).astype(bf)
        pack_f = jnp.concatenate([raw[6][0], raw[6][1], raw[9]], axis=1).astype(bf)
        wholes = tuple(
            lax.all_gather(lax.all_gather(p, ("fsdp", "ctx"), axis=0, tiled=True), "tp", axis=0)
            for p in (pack_a, pack_f)
        )
    out = block_call(
        F, C, T, R, n, fast, tokens, cotangent, wholes, raw, layer_gains, inner_gains, cos, sa, sb, bias
    )
    bo, tg, sums, small, norms = out[:5]
    if not fast:
        sums = jnp.concatenate([out[-1], out[-2]], axis=2).astype(f32)
        same = [[t for t in range(T) if t % 2 == k] for k in range(2)]
        sums = lax.psum_scatter(sums, "tp", scatter_dimension=0, axis_index_groups=same, tiled=False)
        sums = lax.psum_scatter(sums, ("fsdp", "ctx"), scatter_dimension=0, tiled=True)
        parts = []
        for pieces in matrices(raw, sums):
            parts += [a[0, 0] for a in squares(pieces)]
        parts = lax.psum(jnp.stack(parts), ("fsdp", "ctx", "tp"))
        norms = jnp.broadcast_to(parts[:, None], (8, 128))
    gains = (layer_gains, layer_first, layer_second, inner_gains, inner_first, inner_second)
    turned = (rows, J, D)
    outs = [(turned, bf), (turned, f32)] + [(a.shape, f32) for a in raw + gains] + [((4, 2), f32)]
    outs = local_call(functools.partial(step_kernel, T), [*raw, sums, norms, small, bo, tg, *gains], outs)
    outs = list(outs)
    outs[:2] = [a.transpose(1, 0, 2) for a in outs[:2]]
    return tuple(a.T if 11 <= i < 14 else a for i, a in enumerate(outs))


def solution(mesh):
    tok = P("fsdp", ("ctx", "tp"), None)
    wide = P(None, ("fsdp", "ctx"), "tp")
    tall = P("tp", ("fsdp", "ctx"))
    split = P(None, "tp")
    sizes = (mesh.shape["fsdp"], mesh.shape["ctx"], mesh.shape["tp"])
    return jax.shard_map(
        functools.partial(body, *sizes),
        mesh=mesh,
        in_specs=(tok, tok, P(), P(), P(), split, split, split)
        + (wide,) * 3 + (tall,) * 3 + (wide,) * 3 + (tall,) * 3,
        out_specs=(tok, tok) + (wide,) * 3 + (tall,) * 3 + (wide,) * 3 + (tall,) * 3
        + (P(),) * 3 + (split,) * 3 + (P(),),
        check_vma=False,
    )
```

```python
import functools
import jax
import jax.numpy as jnp
import numpy as np
from jax import lax
from jax.experimental import pallas as pl
from jax.experimental.pallas import tpu as pltpu
from jax.sharding import PartitionSpec as P

HD = 64
GRID = 32
STEP = 5
VALID = 1025
BETA_ONE = 0.5
BETA_TWO = 0.5
EPS_ADAM = 1e-06
DECAY = 0.01
RATE = 0.5
RATE_GAINS = 0.3
MESH = pl.DeviceIdType.MESH
f32 = jnp.float32
bf = jnp.bfloat16


class Place:
    def __init__(self, F, C, T):
        self.F, self.C, self.T, self.H = F, C, T, T // 2
        self.f = lax.axis_index("fsdp")
        self.c = lax.axis_index("ctx")
        self.t = lax.axis_index("tp")
        self.low = lax.rem(self.t, 2)
        self.high = lax.div(self.t, 2)
        self.pair = self.c * self.H + self.high
        self.pairs = C * self.H
        self.sibling = {"tp": self.t + 1 - 2 * self.low}
        self.xs = [lax.rem(self.f + k, F) for k in range(F)]
        self.ys = [lax.rem(self.high + k, self.H) for k in range(self.H)]
        self.zs = [lax.rem(self.c + k, C) for k in range(C)]

    def at_x(self, k):
        return {"fsdp": self.xs[k]}

    def at_y(self, k):
        return {"tp": self.ys[k] * 2 + self.low}

    def at_z(self, k):
        return {"ctx": self.zs[k]}

    def pair_at(self, k):
        i = lax.rem(self.pair + k, self.pairs)
        return i, {"ctx": lax.div(i, self.H), "tp": lax.rem(i, self.H) * 2 + self.low}

    def tees(self):
        return [{"tp": lax.rem(self.t + k, self.T)} for k in range(1, self.T)]

    def across(self):
        return [
            {"fsdp": self.xs[a], "ctx": self.zs[b]} for a in range(self.F) for b in range(self.C) if a + b
        ]

    def partners(self, with_x):
        out = self.tees() + [
            {"ctx": self.zs[c], "tp": self.ys[y] * 2 + self.low} for c in range(1, self.C) for y in range(self.H)
        ]
        if with_x:
            out += [{"fsdp": self.xs[a], "ctx": self.zs[b]} for a in range(1, self.F) for b in range(self.C)]
        return out


def hail(partners):
    barrier = pltpu.get_barrier_semaphore()
    for partner in partners:
        pl.semaphore_signal(barrier, inc=1, device_id=partner, device_id_type=MESH)


def heard(partners):
    pl.semaphore_wait(pltpu.get_barrier_semaphore(), len(partners))


class Sems:
    def __init__(self, send, recv):
        self.send, self.recv, self.n = send, recv, 0

    def remote(self, src, dst, device):
        i = self.n
        self.n += 1
        return pltpu.make_async_remote_copy(
            src, dst, self.send.at[i], self.recv.at[i], device_id=device, device_id_type=MESH
        )

    def local(self, src, dst):
        i = self.n
        self.n += 1
        return pltpu.make_async_copy(src, dst, self.send.at[i])


class Exchange:
    def __init__(self, place, sems, src, dst):
        self.own = sems.local(src.at[place.pair], dst.at[place.pair])
        self.copies = []
        for k in range(1, place.pairs):
            i, device = place.pair_at(k)
            self.copies.append(sems.remote(src.at[i], dst.at[place.pair], device))

    def start(self, first=0, last=None):
        for copy in ([self.own] + self.copies)[first:last]:
            copy.start()

    def wait(self):
        self.own.wait()
        for copy in self.copies:
            copy.wait_recv()

    def finish(self):
        for copy in self.copies:
            copy.wait_send()


class Gather:
    def __init__(self, place, sems, pack, whole, cols, first):
        P, R = place, pack.shape[0]
        C, F, H = P.C, P.F, P.H
        n = C * R
        window = pl.ds(*cols)

        def push(t, row, rows, device):
            block = whole.at[t, pl.ds(pl.multiple_of(row, 16), rows), window]
            return sems.remote(block, block, device)

        row = (P.f * C + P.c) * R
        base = P.f * n
        self.own = sems.local(
            pack.at[:, window], whole.at[P.t, pl.ds(pl.multiple_of(row, 16), R), window]
        )
        chain = []
        for j in range(1, C):
            right = push(P.t, (P.f * C + jnp.maximum(P.c - j + 1, 0)) * R, R, P.at_z(1))
            left = push(P.t, (P.f * C + jnp.minimum(P.c + j - 1, C - 1)) * R, R, P.at_z(C - 1))
            chain.append([
                (right, jnp.logical_and(P.c + 1 < C, P.c - j + 1 >= 0), P.c - j >= 0),
                (left, jnp.logical_and(P.c >= 1, P.c + j - 1 < C), P.c + j < C),
            ])
        self.chain = chain
        tees = [y * 2 + P.low for y in P.ys]
        if first == "y":
            second = [push(P.t, base, n, P.at_y(k)) for k in range(1, H)]
            third = [push(t, base, n, P.at_x(k)) for k in range(1, F) for t in tees]
            over_3 = [push(t, base, n, P.sibling) for t in tees[1:]]
            over_4 = [push(t, P.xs[k] * n, n, P.sibling) for k in range(1, F) for t in tees]
        else:
            second = [push(P.t, base, n, P.at_x(k)) for k in range(1, F)]
            third = [push(P.t, 0, n * F, P.at_y(k)) for k in range(1, H)]
            over_3 = [push(P.t, P.xs[k] * n, n, P.sibling) for k in range(1, F)]
            over_4 = [push(t, 0, n * F, P.sibling) for t in tees[1:]]
        over_2 = [push(P.t, base, n, P.sibling)]
        none = [[] for _ in chain]
        self.waits = none + [[], second, third]
        self.starts = none + [second + over_2, third + over_3, over_4]
        self.sent_over = over_2 + over_3 + over_4

    def stage(self, s):
        if s == 0:
            self.own.wait()
        if 0 < s <= len(self.chain):
            for copy, _, gets in self.chain[s - 1]:
                pl.when(gets)(copy.wait_recv)
        for copy in self.waits[s]:
            copy.wait_recv()
        if s < len(self.chain):
            for copy, sends, _ in self.chain[s]:
                pl.when(sends)(copy.start)
        for copy in self.starts[s]:
            copy.start()

    def finish(self):
        for copy in self.sent_over:
            copy.wait_recv()

    def settle(self):
        for step in self.chain:
            for copy, sends, _ in step:
                pl.when(sends)(copy.wait_send)
        for group in self.starts:
            for copy in group:
                copy.wait_send()


def by_rows(rows, step, body):
    def it(i, _):
        body(pl.multiple_of(i * step, step), step)
        return 0

    lax.fori_loop(0, rows // step, it, 0)


class Reduce:
    def __init__(self, place, sems, view, D, width, first, lands, out, out_col, R):
        P, n = place, place.C * R
        C, F, H = P.C, P.F, P.H
        L1, L2, L3 = lands
        self.out, self.to, self.R = out, pl.ds(out_col, width), R
        base = pl.multiple_of(P.f * n, 16)
        mine = pl.multiple_of(base + P.c * R, 16)
        self.copies = [[], [], []]

        def rows(u, start, count):
            return view(u, pl.ds(start, count))

        def send(stage, src, dst, device):
            self.copies[stage].append(sems.remote(src, dst, device))

        if first == "x":
            for k in range(1, F):
                for u in range(H):
                    send(0, rows(u, pl.multiple_of(P.xs[k] * n, 16), n), L1.at[k - 1, u], P.at_x(k))
            for k in range(1, H):
                send(1, rows(P.ys[k], base, n), L2.at[k - 1], P.at_y(k))
            self.adds = [
                [(rows(u, base, n), [L1.at[k - 1, u] for k in range(1, F)]) for u in range(H)],
                [(rows(P.high, base, n), [L2.at[k - 1] for k in range(1, H)])],
            ]
        else:
            for k in range(1, H):
                send(0, rows(P.ys[k], 0, D), L1.at[k - 1], P.at_y(k))
            for k in range(1, F):
                send(1, rows(P.high, pl.multiple_of(P.xs[k] * n, 16), n), L2.at[k - 1], P.at_x(k))
            self.adds = [
                [(rows(P.high, 0, D), [L1.at[k - 1] for k in range(1, H)])],
                [(rows(P.high, base, n), [L2.at[k - 1] for k in range(1, F)])],
            ]
        for k in range(1, C):
            send(2, rows(P.high, pl.multiple_of(base + P.zs[k] * R, 16), R), L3.at[k - 1], P.at_z(k))
        self.last = (rows(P.high, mine, R), [L3.at[k - 1] for k in range(1, C)])

    def stage(self, s):
        if s > 0:
            for copy in self.copies[s - 1]:
                copy.wait_recv()
        if s in (1, 2):
            for dst, lands in self.adds[s - 1]:

                def add(r, k, dst=dst, lands=lands):
                    v = dst[pl.ds(r, k), :].astype(f32)
                    for land in lands:
                        v = v + land[pl.ds(r, k), :].astype(f32)
                    dst[pl.ds(r, k), :] = v.astype(bf)

                by_rows(dst.shape[0], 96, add)
        if s == 3:
            dst, lands = self.last
            v = dst[...].astype(f32)
            for land in lands:
                v = v + land[...].astype(f32)
            self.out[:, self.to] = v
        else:
            for copy in self.copies[s]:
                copy.start()

    def settle(self):
        for group in self.copies:
            for copy in group:
                copy.wait_send()


def reduce_lands(parts, F, C, H, D, R):
    out = []
    for (_, n), first in parts:
        if first == "x":
            out += [(F - 1, H, C * R, n), (H - 1, C * R, n)]
        else:
            out += [(H - 1, D, n), (F - 1, C * R, n)]
        out.append((C - 1, R, n))
    return [pltpu.VMEM(s, bf) for s in out]
EPS=1e-6
def dot(a,b): return jnp.dot(a,b,preferred_element_type=f32)
def dot_t(a,b): return lax.dot_general(a,b,(((1,),(1,)),((),())),preferred_element_type=f32)
def dot_l(a,b): return lax.dot_general(a,b,(((0,),(0,)),((),())),preferred_element_type=f32)

def chunks(rows, step, body):
    def it(i,_):
        body(pl.ds(pl.multiple_of(i*step,step),step)); return 0
    lax.fori_loop(0,rows//step,it,0)

def norm(v):
    mean=jnp.mean(v,axis=-1,keepdims=True)
    var=jnp.mean(v*v,axis=-1,keepdims=True)-mean*mean
    inv=lax.rsqrt(var+EPS)
    return (v-mean)*inv, inv

def spread(src3, dst):
    J,r,D=src3.shape
    n=dst.shape[0]
    pad=n-J*r
    if pad: dst[n-16:n,:]=jnp.zeros((16,D),f32)
    for j in range(J):
        dst[j*r:(j+1)*r,:]=src3[j].astype(f32)

def join(WA, g, dst, T):
    def it(i,_):
        s=pl.ds(pl.multiple_of(i*96,96),96)
        for t in range(T):
            dst[s,128*t:128*t+128]=WA[t,s,128*g:128*g+128]
        for u in range(T//2):
            c=pl.ds(512+128*(g//2),128)
            a=WA[2*u,s,c].astype(f32); b=WA[2*u+1,s,c].astype(f32)
            if g%2==0: b=pltpu.roll(b,64,1)
            else: a=pltpu.roll(a,64,1)
            dst[s,128*(T+u):128*(T+u)+128]=jnp.where(lanes(96,0),a,b).astype(bf)
        return 0
    lax.fori_loop(0,WA.shape[1]//96,it,0)

def turn(v, cos, sa, sb):
    n=v.shape[1]
    out=[]
    for i in range(n//128):
        a=v[:,i*128:(i+1)*128]
        out.append(a*cos+pltpu.roll(a,128-16,1)*sa+pltpu.roll(a,16,1)*sb)
    return jnp.concatenate(out,axis=1)

def normal(x, gains, ln1):
    def ln(s):
        v,_=norm(x[s,:])
        ln1[s,:]=(v*gains[0:1,:]+gains[1:2,:]).astype(bf)
    chunks(x.shape[0],48,ln)


def project(ln1, W, cos, sa, sb, dst, scale=None):
    n=ln1.shape[0]//2
    y=dot(ln1[0:n,:],W[...])
    if cos is not None: y=turn(y,cos[...],sa[...],sb[...])
    if scale is not None: y=y*scale
    dst[0:n,:]=y.astype(bf)


def lanes(n, a):
    return (lax.broadcasted_iota(jnp.int32,(n,128),1)//64==a)

def attention(q,K,V,bias,Es,linv,att,before,after):
    n=q.shape[0]; m=K.shape[0]
    def pair(p,_):
        c=pl.ds(pl.multiple_of(p*128,128),128)
        k2=K[:,c]; v2=V[:,c]
        q2=q[:,c]
        o=None; li=[]
        for a in (0,1):
            before(p,a)
            ka=jnp.where(lanes(m,a),k2,jnp.zeros_like(k2))
            va=jnp.where(lanes(m,a),v2,jnp.zeros_like(v2))
            S=dot_t(q2,ka)+bias[0:1,:]
            mx=jnp.max(S,axis=1,keepdims=True)
            e=jnp.exp(S-mx)
            l=1.0/jnp.sum(e,axis=1,keepdims=True)
            eb=e.astype(bf)
            Es[a]=eb
            after(p,a)
            oa=dot(eb,va)*l
            o=oa if o is None else o+oa
            li.append(l)
        att[:,c]=o.astype(bf)
        linv[:,c]=jnp.where(lanes(n,0),li[0],li[1])
        return 0
    lax.fori_loop(0,q.shape[1]//128,pair,0)

def merge(att,Wm,x,mid,gains,ln2,n):
    mid[...]=x[...]+dot_t(att[...],Wm[...])
    def ln(s):
        v,_=norm(mid[s,:])
        ln2[s,:]=(v*gains[2:3,:]+gains[3:4,:]).astype(bf)
    chunks(n,48,ln)

def norm_back(src, e_src, gain, add, dst, lay, row):
    n=src.shape[0]
    lay[row:row+2,:]=jnp.zeros((2,src.shape[1]),f32)
    def it(s):
        a,inv=norm(src[s,:]); e=e_src[s,:]
        lay[row:row+1,:]+=jnp.sum(e*a,axis=0,keepdims=True)
        lay[row+1:row+2,:]+=jnp.sum(e,axis=0,keepdims=True)
        eg=e*gain
        d=add[s,:].astype(f32)+inv*(eg-jnp.mean(eg,axis=1,keepdims=True)-a*jnp.mean(eg*a,axis=1,keepdims=True))
        dst[s,:]=d.astype(dst.dtype)
    chunks(n,48,it)


VMEM = pl.BlockSpec(memory_space=pltpu.VMEM)
HBM = pl.BlockSpec(memory_space=pl.ANY)
LIMIT = 60 * 2**20


def local_call(body, ins, outs, scratch=(), flops=0):
    return pl.pallas_call(
        body,
        out_shape=[jax.ShapeDtypeStruct(s, d) for s, d in outs],
        in_specs=[VMEM] * len(ins),
        out_specs=[VMEM] * len(outs),
        scratch_shapes=[pltpu.VMEM(s, d) for s, d in scratch],
        compiler_params=pltpu.CompilerParams(vmem_limit_bytes=LIMIT),
    )(*ins)


def rotary_tables(low, pairs, rows, total):
    quarter = HD // 4

    def places(half):
        return ((np.arange(pairs)[:, None] * 2 + half) * rows + np.arange(rows)).reshape(-1)

    def bias(half):
        out = np.full((total,), -1e30, np.float32)
        out[: pairs * rows] = np.where(places(half) < VALID, 0.0, -1e30)
        return out

    positions = places(low)
    inside = (positions >= 1) & (positions <= GRID * GRID)
    patch = np.where(inside, positions - 1, 0)
    frequency = 10000.0 ** (-np.arange(quarter) / quarter)
    row_angle = (patch // GRID)[:, None] * frequency
    column_angle = (patch % GRID)[:, None] * frequency
    angles = np.zeros((total, HD))
    angles[: pairs * rows] = np.concatenate([row_angle, row_angle, column_angle, column_angle], axis=-1)
    angles = np.concatenate([angles, angles], axis=-1)
    sine = np.sin(angles)
    first = (np.arange(2 * HD) // quarter) % 2 == 0
    turns = np.stack([np.cos(angles), np.where(first, -sine, 0.0), np.where(first, 0.0, sine)])
    return turns.astype(np.float32), np.concatenate([bias(low), bias(1 - low)])[None]


GATHER_A = (((0, 384), "y"), ((384, 384), "x"))
GATHER_F = tuple(((256 * i, 256), k) for i, k in enumerate("yxyxyx"))
FIRST_F = 4
REDUCE_H = (((1024, 256), "x"), ((1280, 256), "y"))
REDUCE_G = (((0, 256), "x"), ((256, 256), "y"), ((512, 256), "x"), ((768, 256), "y"))
REDUCE_A = (((0, 256), "x"), ((256, 256), "y"), ((512, 128), "x"), ((640, 128), "y"))
PLAN = {
    "start": ("A00", "A10"),
    "line1": ("A01", "A11", "F00", "F10"),
    "line2": ("A02", "A12", "F01", "F11"),
    "z": ("A03", "A13", "F02", "F12"),
    "early": ("A04", "A14", "F03", "F13", "F20", "F30", "F40", "F50"),
    "tokens": ("F21", "F31", "F41", "F51"),
    "last": ("A05", "A15", "F22", "F32", "F42", "F52"),
    "k": ("F04", "F14"),
    "v": ("F23", "F33"),
    "q": ("F43", "F53"),
    "p1": ("cot",),
    "p2": ("F24", "F34"),
    "o3": ("F05", "F15"),
    "o5": ("F44", "F54"),
    "merged": ("F25", "F35"),
    "ones": ("F45", "F55"),
    "shrunk": ("H00", "H10"),
    "expanded0": ("H01", "H11", "G00"),
    "expanded1": ("G10",),
    "expanded2": ("G20",),
    "expanded3": ("G30",),
    "back1": ("H02", "H12", "G01"),
    "back3": ("G11",),
    "back4": ("G21", "H03", "H13"),
    "back5": ("G12",),
    "looped": ("G31", "G02"),
    "main": ("B00", "B10", "G22"),
    "tailed": ("G32",),
    "tail": ("B20", "B30"),
    "back_out": ("B01", "B11"),
    "hop0": ("B21", "B31"),
    "hop1": ("B02", "B12"),
    "hop2": ("B22", "B32", "G03", "G13", "G23", "G33"),
    "end": ("B03", "B13", "B23", "B33"),
}


def mine_and_theirs(tiles, low):
    a, b = tiles
    return jnp.where(low == 0, a, b), jnp.where(low == 0, b, a)


def halves(tile, low):
    other = pltpu.roll(tile, 64, 1)
    return jnp.where(low == 0, tile, other), jnp.where(low == 0, other, tile)


def block_kernel(F, C, T, R, n, weights, plan, tok, cot, *rest):
    if weights:
        WF_in = None
    else:
        (WA_in, WF_in), rest = rest[:2], rest[2:]
    raw, rest = rest[:12], rest[12:]
    gains, inner, tables, biases = rest[:4]
    bo_out, tg_out, sums, small, norms = rest[4:9]
    WF, x_h, ln1_h, q_h, K_h, V_h, E, linv_h, att_h = rest[9:18]
    W_h = rest[18:22]
    rest = rest[22:]
    if not weights:
        (GF, GA), rest = rest[:2], rest[2:]
    (IG, LN2, CT, GB, XO, mid, cin, tg, SM, SML, NV, NVL, big, GA_s, pa, pf, turns, bias, send, recv, local, free) = rest[:22]
    lands = rest[22:]
    place = Place(F, C, T)
    H, low, sib = place.H, place.low, place.sibling
    sems = Sems(send, recv)
    partners = place.partners(True)
    hail(partners)
    bo = cin
    J, r, D = bo.shape
    Hd = IG.shape[2]
    tiles = D // 128
    main = T * 128
    wide = D // T * 2 // 3
    top, bottom = pl.ds(0, n), pl.ds(n, n)
    nlocal = [0]
    ig = IG

    def slots(count):
        nlocal[0] += count
        return nlocal[0] - count

    def fetch(src, dst):
        copy = pltpu.make_async_copy(src, dst, local.at[slots(1)])
        copy.start()
        return copy

    cos, sa, sb = (turns.at[k] for k in range(3))
    if weights:
        GA = GA_s

        def GF(u, rows, start, size):
            return big.at[2 * u + start // D, rows, pl.ds(start % D, size)]

        WA = big
    else:
        WA = WA_in

    tokens = Exchange(place, sems, tok, tg)
    cots = Exchange(place, sems, cot, cin)
    swap_ln2 = sems.remote(LN2.at[top], LN2.at[bottom], sib)
    swap_ct = sems.remote(CT.at[top], CT.at[bottom], sib)
    swap_gb = sems.remote(GB.at[top], GB.at[bottom], sib)
    back_bo = Exchange(place, sems, bo, bo_out)
    back_tg = Exchange(place, sems, tg, tg_out)
    share = [sems.remote(inner, IG.at[place.t], device) for device in place.tees()]
    groups = {"A": [], "F": [], "H": [], "G": [], "B": []}
    if weights:
        for key, pack, whole, parts in (("A", pa, WA, GATHER_A), ("F", pf, WF, GATHER_F)):
            groups[key] = [Gather(place, sems, pack, whole, cols, first) for cols, first in parts]
        i = 0
        for key, parts in (("H", REDUCE_H), ("G", REDUCE_G), ("B", REDUCE_A)):
            for (start, size), first in parts:
                if key == "B":
                    view = lambda u, rows, c=pl.ds(start, size): GA.at[u, rows, c]
                    col = start
                else:
                    view = lambda u, rows, start=start, size=size: GF(u, rows, start, size)
                    col = D + start
                groups[key].append(
                    Reduce(place, sems, view, D, size, first, lands[3 * i : 3 * i + 3], sums, col, R)
                )
                i += 1

    def at(point):
        for step in plan.get(point, ()) if weights else ():
            if step == "cot":
                cots.start()
                continue
            groups[step[0]][int(step[1])].stage(int(step[2]))

    def at_loop(name, index, count):
        for k in range(count):
            if weights and plan.get(f"{name}{k}"):

                @pl.when(index == k)
                def _(k=k):
                    at(f"{name}{k}")

    def wait_all(key):
        for g in groups[key]:
            g.finish()

    def forward(x, ln1, q, K, V, Wq, Wk, Wv, Wm, att, linv, Es, *states):
        Ws = (Wq, Wk, Wv, Wm)
        tabs = [fetch(tables.at[low], turns), fetch(biases.at[low], bias)]
        if weights:
            gets = [fetch(raw[k], states[i]) for i, k in enumerate((0, 3, 6, 9))]
            for copy in gets:
                copy.wait()
            aw, mw, ew, sw = states
            four = [aw[0], aw[1], aw[2], mw[...].T]
            for g, w in enumerate(four):
                pa[:, wide * g : wide * (g + 1)] = w[:, :wide].astype(bf)
            for g in (0, 2):
                pair = [w[:, wide:] for w in four[g : g + 2]]
                pa[:, 4 * wide + 64 * g : 4 * wide + 64 * g + 128] = jnp.concatenate(pair, axis=1).astype(bf)
            for g, w in enumerate((ew[0], ew[1], sw[...])):
                pf[:, Hd * g : Hd * (g + 1)] = w.astype(bf)
            for g in groups["A"] + groups["F"]:
                g.own.start()
        heard(partners)
        IG[place.t] = inner[...]
        at("start")
        for copy in share:
            copy.start()
        at("line1")
        at("line2")
        tokens.start()
        if not weights:
            cots.start()
        at("z")
        at("early")
        tokens.wait()
        at("tokens")
        spread(tg, x)
        normal(x, gains, ln1)
        swap_ln1 = sems.remote(ln1.at[top], XO.at[1, :, pl.ds(0, D)], sib)
        swap_ln1.start()
        at("normed")
        if weights:
            at("last")
            wait_all("A")
        else:
            whole = pltpu.make_async_copy(WA_in, big, local.at[slots(1)])
            whole.start()
            whole.wait()
        saves = [fetch(x, x_h), fetch(ln1.at[top], ln1_h.at[top])]
        swap = [sems.remote(X.at[top], XO.at[0, :, pl.ds(o, D)], sib) for X, o in ((K, 0), (V, D))]
        for copy in tabs:
            copy.wait()
        join(big, 1, Wk, T)
        project(ln1, Wk, cos, sa, sb, K)
        swap[0].start()
        at("k")
        join(big, 2, Wv, T)
        project(ln1, Wv, None, None, None, V)
        swap[1].start()
        at("v")
        join(big, 0, Wq, T)
        project(ln1, Wq, cos, sa, sb, q, 0.125)
        join(big, 3, Wm, T)
        at("q")
        saves += [fetch(a, b) for a, b in zip(Ws, W_h)] + [fetch(q, q_h)]
        for copy, X in zip(swap, (K, V)):
            copy.wait_recv()
        K[bottom, :] = XO[0, :, 0:D]
        V[bottom, :] = XO[0, :, D : 2 * D]
        saves += [fetch(K, K_h), fetch(V, V_h)]
        swap_ln1.wait_recv()
        saves += [fetch(XO.at[1, :, pl.ds(0, D)], ln1_h.at[bottom])]
        e0 = slots(2)

        def put_e(h):
            slot = lax.rem(h, 2)
            return pltpu.make_async_copy(Es.at[slot], E.at[h], local.at[e0 + slot])

        def before(p, a):
            at_loop("p" if a == 0 else "o", p, tiles)

            @pl.when(p > 0)
            def _():
                put_e(2 * p + a - 2).wait()

        def after(p, a):
            put_e(2 * p + a).start()

        attention(q, K, V, bias, Es, linv, att, before, after)
        at("attended")
        late = [fetch(linv, linv_h), fetch(att, att_h)]
        merge(att, Wm, x, mid, gains, LN2, n)
        swap_ln2.start()
        at("merged")
        for h in (2 * tiles - 2, 2 * tiles - 1):
            put_e(h).wait()
        for copy in saves + late:
            copy.wait()
        for copy in swap + [swap_ln1]:
            copy.wait_send()
        pl.semaphore_signal(free.at[0], inc=1, device_id=sib, device_id_type=MESH)

    pl.run_scoped(
        forward,
        pltpu.VMEM((n, D), f32),
        pltpu.VMEM((2 * n, D), bf),
        pltpu.VMEM((n, D), bf),
        pltpu.VMEM((2 * n, D), bf),
        pltpu.VMEM((2 * n, D), bf),
        *[pltpu.VMEM((D, D), bf)] * 4,
        pltpu.VMEM((n, D), bf),
        pltpu.VMEM((n, D), f32),
        pltpu.VMEM((2, n, 2 * n), bf),
        *[pltpu.VMEM(raw[k].shape, f32) for k in (0, 3, 6, 9)],
    )
    tokens.finish()
    for part in groups["A"]:
        part.settle()

    def feed(WFv, gate, up, act, gh, out, XT):
        w0 = slots(2)
        WF_from = WF if weights else WF_in

        def get_w(t, start, size):
            slot = lax.rem(t, 2)
            return pltpu.make_async_copy(
                WF_from.at[t, :, pl.ds(start, size)], WFv.at[slot, :, pl.ds(0, size)], local.at[w0 + slot]
            )

        def through(body, start, size, init):
            def step(t, c):
                get_w(t, start, size).wait()
                c = body(t, lax.rem(t, 2), c)

                @pl.when(t + 2 < T)
                def _():
                    get_w(t + 2, start, size).start()

                return c

            return lax.fori_loop(0, T, step, init)

        def ahead(start, size):
            for t in range(2):
                get_w(t, start, size).start()

        def swaps(cols):
            return [sems.remote(XT.at[2 * u + 1 - low, :, cols], XO.at[u, :, cols], sib) for u in range(H)]

        def pass_on(copies, t):
            for u, copy in enumerate(copies):

                @pl.when(t == 2 * u + 1 - low)
                def _(copy=copy):
                    copy.start()

        swap_h = swaps(pl.ds(2 * Hd, Hd))
        swap_g = swaps(pl.ds(0, 2 * Hd))
        at("feed")
        for g in groups["F"][:FIRST_F]:
            g.finish()
        ahead(0, 2 * Hd)
        def one(t, slot, c):
            at_loop("one", t, T)
            s0, s1 = c
            gu = dot(LN2[top, :], WFv[slot])
            g, u = gu[:, :Hd], gu[:, Hd:]
            a = g * jax.nn.sigmoid(g) * u
            gate[t] = g.astype(gate.dtype)
            up[t] = u.astype(up.dtype)
            act[t] = a
            return s0 + jnp.sum(a, axis=1, keepdims=True), s1 + jnp.sum(a * a, axis=1, keepdims=True)

        z = jnp.zeros((n, 1), f32)
        s0, s1 = through(one, 0, 2 * Hd, (z, z))
        at("ones")
        for g in groups["F"][FIRST_F:]:
            g.finish()
        ahead(2 * Hd, Hd)
        width = T * Hd
        mean = s0 / width
        inv = lax.rsqrt(s1 / width - mean * mean + EPS)
        SM[0] = jnp.zeros(SM.shape[1:], f32)
        cots.wait()
        spread(cin, out)
        CT[top, :] = out[...].astype(bf)
        swap_ct.start()
        out[...] = mid[...]
        pl.semaphore_wait(free.at[0], 1)
        for copy in share:
            copy.wait()

        def two(t, slot, c):
            r0, r1 = c
            n3 = (act[t] - mean) * inv
            act[t] = n3
            gt = ig[t, 0:1, :]
            hid = (n3 * gt + ig[t, 1:2, :]).astype(bf)
            XT[t, :, 2 * Hd : 3 * Hd] = hid
            pass_on(swap_h, t)
            out[...] += dot_t(hid, WFv[slot, :, 0:Hd])
            h = dot(CT[top, :], WFv[slot, :, 0:Hd])
            SM[0, pl.ds(8 + 2 * t, 1), 0:Hd] = jnp.sum(h * n3, axis=0, keepdims=True)
            SM[0, pl.ds(9 + 2 * t, 1), 0:Hd] = jnp.sum(h, axis=0, keepdims=True)
            e = h * gt
            gh[t] = e.astype(gh.dtype)
            return r0 + jnp.sum(e, axis=1, keepdims=True), r1 + jnp.sum(e * n3, axis=1, keepdims=True)

        r0, r1 = through(two, 2 * Hd, Hd, (z, z))
        ahead(0, 2 * Hd)
        r0, r1 = r0 / width, r1 / width
        swap_ct.wait_recv()
        swap_ln2.wait_recv()

        def put_f(u, start, value):
            if weights:
                GF(u, pl.ds(0, D), start, value.shape[1])[...] = value.astype(bf)
            else:
                GF[u, :, start : start + value.shape[1]] = value.astype(bf)

        for u in range(H):
            swap_h[u].wait_recv()
            t = 2 * u + low
            c = pl.ds(2 * Hd, Hd)
            put_f(u, 2 * Hd, dot_l(CT[top, :], XT[t, :, c]) + dot_l(CT[bottom, :], XO[u, :, c]))
        at("shrunk")
        for j in range(J):
            bo[j] = out[j * r : (j + 1) * r, :].astype(bf)
        back_bo.start()
        gln2 = out
        gln2[...] = jnp.zeros(gln2.shape, f32)

        def three(t, slot, _):
            at_loop("three", t, T)
            ga = inv * (gh[t].astype(f32) - r0 - act[t] * r1)
            g, u = gate[t].astype(f32), up[t].astype(f32)
            s = jax.nn.sigmoid(g)
            gg = (ga * u * s * (1.0 + g * (1.0 - s))).astype(bf)
            gu = (ga * g * s).astype(bf)
            XT[t, :, 0:Hd] = gg
            XT[t, :, Hd : 2 * Hd] = gu
            pass_on(swap_g, t)
            gln2[...] += dot_t(XT[t, :, 0 : 2 * Hd], WFv[slot])
            return 0

        through(three, 0, 2 * Hd, 0)
        at("threes")
        for u in range(H):
            swap_g[u].wait_recv()
            t = 2 * u + low
            for k in range(4):
                c = pl.ds(k * Hd // 2, Hd // 2)
                put_f(u, k * Hd // 2, dot_l(LN2[top, :], XT[t, :, c]) + dot_l(LN2[bottom, :], XO[u, :, c]))
                if u == H - 1:
                    at(f"expanded{k}")
        norm_back(mid, gln2, gains[2:3, :], CT, GB, SM.at[0], 2)
        swap_gb.start()
        at("fed")
        for copy in swap_h + swap_g + [swap_ln2, swap_ct]:
            copy.wait_send()
        pl.semaphore_signal(free.at[1], inc=1, device_id=sib, device_id_type=MESH)

    pl.run_scoped(
        feed,
        pltpu.VMEM((2, D, 2 * Hd), bf),
        pltpu.VMEM((T, n, Hd), bf),
        pltpu.VMEM((T, n, Hd), bf),
        pltpu.VMEM((T, n, Hd), f32),
        pltpu.VMEM((T, n, Hd), f32),
        pltpu.VMEM((n, D), f32),
        pltpu.VMEM((T, n, 3 * Hd), bf),
    )
    cots.finish()

    def attend(qv, lv, av, Wmv, gatt, dq, dK, dV, sK, sV, XT, LN1, Wqv, Wkv, Wvv):
        e0 = slots(2)

        cuts = [pl.ds(0, main), pl.ds(main, D - main)]
        give = [
            [sems.remote(S.at[:, cut], XO.at[0, :, pl.ds(off + cut.start, cut.size)], sib) for off, S in ((0, sK), (D, sV))]
            for cut in cuts
        ]
        swap_a = [
            [sems.remote(XT.at[1, u, :, cut], XO.at[1, :, pl.ds(H * cut.start + u * cut.size, cut.size)], sib) for u in range(H)]
            for cut in cuts
        ]
        Kv, Vv = LN2, CT
        Gq, Gk, Gv = gatt, qv, Kv

        def gradients(p, c):
            co, si, sj = cos[p, :], -sa[p, :], -sb[p, :]
            k0, v0 = pl.ds(c.start, c.size), pl.ds(D + c.start, c.size)
            g_q = turn(dq[p, c], co, si, sj)
            g_k = turn(dK[p, c] + XO[0, p, k0].astype(f32), co, si, sj)
            g_v = dV[p, c] + XO[0, p, v0].astype(f32)
            return g_q, g_k, g_v, av[p, c].astype(f32)

        def keep(p, c, values):
            for ref, v in zip((Gq, Gk, Gv), values):
                ref[p, c] = v.astype(bf)

        def main_rows(i, _):
            p = pl.ds(pl.multiple_of(i * 48, 48), 48)
            values = gradients(p, cuts[0])
            keep(p, cuts[0], values)
            for u in range(H):
                for g, v in enumerate(values):
                    two = v[:, 256 * u : 256 * u + 128], v[:, 256 * u + 128 : 256 * u + 256]
                    for side, z in enumerate(mine_and_theirs(two, low)):
                        XT[side, u, p, 128 * g : 128 * g + 128] = z.astype(bf)
            return 0

        def tail_rows(i, _):
            p = pl.ds(pl.multiple_of(i * 48, 48), 48)
            values = gradients(p, cuts[1])
            keep(p, cuts[1], values)
            first = lanes(48, 0)
            for u in range(H):
                split = [halves(v[:, 128 * u : 128 * u + 128], low) for v in values]
                for g in (0, 1):
                    (a0, b0), (a1, b1) = split[2 * g], split[2 * g + 1]
                    c = pl.ds(main + 128 * g, 128)
                    XT[0, u, p, c] = jnp.where(first, a0, b1).astype(bf)
                    XT[1, u, p, c] = jnp.where(first, b0, a1).astype(bf)
            return 0

        def weight_grad(k):
            for copy in swap_a[k]:
                copy.wait_recv()
            cut = cuts[k]
            for u in range(H):
                m = XT[0, u, :, cut]
                o = XO[1, :, H * cut.start + u * cut.size : H * cut.start + (u + 1) * cut.size]
                w = cut.size // 4
                if k == 0:
                    d = dot_l(LN1[top, :], m[:, : 3 * w]) + dot_l(LN1[bottom, :], o[:, : 3 * w])
                    e = dot_l(GB[top, :], m[:, 3 * w :]) + dot_l(GB[bottom, :], o[:, 3 * w :])
                    GA[u, :, 0 : 3 * w] = d.astype(bf)
                    GA[u, :, 3 * w : 4 * w] = e.astype(bf)
                else:
                    d = dot_l(LN1[top, :], m) + dot_l(LN1[bottom, :], o)
                    e = dot_l(GB[top, :], m) + dot_l(GB[bottom, :], o)
                    lane = lax.broadcasted_iota(jnp.int32, d.shape, 1)
                    GA[u, :, cut] = jnp.where(lane < 3 * w, d, e).astype(bf)

        def pairs(Es):
            def get_e(h):
                slot = lax.rem(h, 2)
                return pltpu.make_async_copy(E.at[h], Es.at[slot], local.at[e0 + slot])

            for h in range(2):
                get_e(h).start()
            gets = [fetch(a, b) for a, b in ((W_h[3], Wmv), (q_h, qv), (K_h, Kv), (V_h, Vv), (att_h, av), (linv_h, lv))]
            late = [fetch(a, b) for a, b in ((ln1_h, LN1), (W_h[0], Wqv), (W_h[1], Wkv), (W_h[2], Wvv))]
            gets[0].wait()
            gatt[...] = dot(GB[top, :], Wmv[...]).astype(bf)
            for copy in gets[1:]:
                copy.wait()

            def pair(p, _):
                at_loop("back", p, tiles)

                @pl.when(p == tiles - 1)
                def _():
                    for copy in give[0]:
                        copy.wait_recv()
                    lax.fori_loop(0, n // 48, main_rows, 0)
                    for copy in swap_a[0]:
                        copy.start()

                c = pl.ds(pl.multiple_of(p * 128, 128), 128)
                k2, v2, q2 = Kv[:, c], Vv[:, c], qv[:, c]
                dob = (gatt[:, c].astype(f32) * lv[:, c]).astype(bf)
                dl = dob.astype(f32) * av[:, c].astype(f32)
                m = 2 * n
                dqv = dkv = dvv = None
                for a in (0, 1):
                    ka = jnp.where(lanes(m, a), k2, jnp.zeros_like(k2))
                    va = jnp.where(lanes(m, a), v2, jnp.zeros_like(v2))
                    qa = jnp.where(lanes(n, a), q2, jnp.zeros_like(q2))
                    da = jnp.where(lanes(n, a), dob, jnp.zeros_like(dob))
                    delta = jnp.sum(jnp.where(lanes(n, a), dl, 0.0), axis=1, keepdims=True)
                    get_e(2 * p + a).wait()
                    e = Es[a]
                    dS = (e.astype(f32) * (dot_t(dob, va) - delta)).astype(bf)
                    x1, x2, x3 = dot(dS, ka), dot_l(dS, qa), dot_l(e, da)

                    @pl.when(p + 1 < tiles)
                    def _(a=a):
                        get_e(2 * p + 2 + a).start()

                    dqv = x1 if a == 0 else dqv + x1
                    dkv = x2 if a == 0 else dkv + x2
                    dvv = x3 if a == 0 else dvv + x3
                dq[:, c] = dqv * 0.125
                dK[:, c] = dkv[:n]
                dV[:, c] = dvv[:n]
                sK[:, c] = dkv[n:].astype(bf)
                sV[:, c] = dvv[n:].astype(bf)

                @pl.when(p == main // 128 - 1)
                def _():
                    pl.semaphore_wait(free.at[1], 1)
                    for copy in give[0]:
                        copy.start()

                return 0

            lax.fori_loop(0, tiles, pair, 0)
            return late

        def run(Es):
            late = pairs(Es)
            for copy in give[1]:
                copy.start()
            at("looped")
            for copy in late:
                copy.wait()

        pl.run_scoped(run, pltpu.VMEM((2, n, 2 * n), bf))
        swap_gb.wait_recv()
        weight_grad(0)
        at("main")
        for copy in give[1]:
            copy.wait_recv()
        lax.fori_loop(0, n // 48, tail_rows, 0)
        for copy in swap_a[1]:
            copy.start()
        at("tailed")

        def final(*rawv):
            states = [fetch(a, b) for a, b in zip(raw, rawv)] if weights else []
            gln1, tok, xv = dK, dq, lv
            get_x = fetch(x_h, xv)
            gln1[...] = dot_t(Gq[...], Wqv[...])
            gln1[...] += dot_t(Gk[...], Wkv[...])
            weight_grad(1)
            at("tail")
            gln1[...] += dot_t(Gv[top, :], Wvv[...])
            get_x.wait()
            norm_back(xv, gln1, gains[0:1, :], GB, tok, SM.at[0], 0)
            for j in range(J):
                tg[j] = tok[j * r : (j + 1) * r, :].astype(bf)
            back_tg.start()
            at("back_out")
            hops = [
                place.tees(),
                [place.at_x(k) for k in range(1, F)],
                [place.at_z(k) for k in range(1, C)],
            ]
            landed = 0
            for s, devices in enumerate(hops):
                copies = [sems.remote(SM.at[s], SML.at[landed + i], d) for i, d in enumerate(devices)]
                for copy in copies:
                    copy.start()
                at(f"hop{s}")
                total = SM[s]
                for i, copy in enumerate(copies):
                    copy.wait_recv()
                    total = total + SML[landed + i]
                for copy in copies:
                    copy.wait_send()
                landed += len(copies)
                SM[s + 1] = total
            small[...] = SM[len(hops)]
            if weights:
                for copy in states:
                    copy.wait()
                at("end")
                for i, pieces in enumerate(matrices(rawv, sums)):
                    for k, total in enumerate(squares(pieces)):
                        NV[0, 2 * i + k : 2 * i + k + 1, :] = jnp.broadcast_to(total, (1, 128))
                landed = 0
                for s, devices in enumerate((place.tees(), place.across())):
                    copies = [sems.remote(NV.at[s], NVL.at[landed + i], d) for i, d in enumerate(devices)]
                    for copy in copies:
                        copy.start()
                    total = NV[s]
                    for i, copy in enumerate(copies):
                        copy.wait_recv()
                        total = total + NVL[landed + i]
                    for copy in copies:
                        copy.wait_send()
                    landed += len(copies)
                    NV[s + 1] = total
                norms[...] = total
            else:
                norms[...] = jnp.zeros(norms.shape, f32)
            for copy in swap_a[0] + swap_a[1] + give[0] + give[1]:
                copy.wait_send()

        pl.run_scoped(final, *[pltpu.VMEM(a.shape, f32) for a in raw])

    pl.run_scoped(
        attend,
        pltpu.VMEM((n, D), bf),
        pltpu.VMEM((n, D), f32),
        pltpu.VMEM((n, D), bf),
        pltpu.VMEM((D, D), bf),
        pltpu.VMEM((n, D), bf),
        *[pltpu.VMEM((n, D), f32)] * 3,
        *[pltpu.VMEM((n, D), bf)] * 2,
        pltpu.VMEM((2, H, n, D), bf),
        pltpu.VMEM((2 * n, D), bf),
        *[pltpu.VMEM((D, D), bf)] * 3,
    )
    for key in "FHGB":
        for part in groups[key]:
            part.settle()
    for back in (back_bo, back_tg):
        back.wait()
        back.finish()
    swap_gb.wait_send()


def block_call(F, C, T, R, n, weights, tokens, cotangent, wholes, raw, gains, inner, tables, biases):
    shape = tokens.shape
    J, r, D = shape
    H, Hd = T // 2, inner.shape[1]
    heads = D // T
    nh = D // HD
    outs = [(shape, bf), (shape, bf), ((R, 4 * heads + 3 * Hd), f32), ((16, D), f32), ((8, 128), f32)]
    out_specs = [HBM, HBM, VMEM, VMEM, VMEM]
    saved = [((T, D, 3 * Hd) if weights else (8, 128), bf), ((n, D), f32), ((2 * n, D), bf), ((n, D), bf)]
    saved += [((2 * n, D), bf)] * 2 + [((nh, n, 2 * n), bf), ((n, D), f32), ((n, D), bf)] + [((D, D), bf)] * 4
    outs += saved
    out_specs += [HBM] * len(saved)
    grads = [((H, D, 3 * Hd), bf), ((H, D, D), bf)]
    if not weights:
        outs += grads
        out_specs += [VMEM, VMEM]
    small = (8, 128)
    scratch = [((T,) + inner.shape, f32)] + [((2 * n, D), bf)] * 3
    scratch += [((H, n, 3 * Hd), bf), ((n, D), f32), (shape, bf), (shape, bf)]
    scratch += [((4, 16, D), f32), ((T + F + C - 3, 16, D), f32), ((3,) + small, f32), ((T + F * C - 2,) + small, f32)]
    scratch += [((T, D, D), bf), grads[1] if weights else (small, bf)]
    scratch += [((R, D), bf), ((R, 3 * Hd), bf)] if weights else [(small, bf)] * 2
    scratch += [(tables.shape[1:], f32), (biases.shape[1:], f32)]
    scratch = [pltpu.VMEM(s, d) for s, d in scratch]
    scratch += [
        pltpu.SemaphoreType.DMA((320,)),
        pltpu.SemaphoreType.DMA((320,)),
        pltpu.SemaphoreType.DMA((64,)),
        pltpu.SemaphoreType.REGULAR((2,)),
    ]
    if weights:
        scratch += reduce_lands(REDUCE_H + REDUCE_G + REDUCE_A, F, C, H, D, R)
    return pl.pallas_call(
        functools.partial(block_kernel, F, C, T, R, n, weights, PLAN),
        out_shape=[jax.ShapeDtypeStruct(s, d) for s, d in outs],
        in_specs=[HBM] * (2 + len(wholes) + len(raw)) + [VMEM] * 2 + [HBM] * 2,
        out_specs=out_specs,
        scratch_shapes=scratch,
        compiler_params=pltpu.CompilerParams(collective_id=1, has_side_effects=True, vmem_limit_bytes=LIMIT),
    )(tokens, cotangent, *wholes, *raw, gains, inner, tables, biases)


def matrices(raw, sums):
    heads, hidden = raw[0].shape[2], raw[6].shape[2]
    base, wide = 4 * heads, heads * 2 // 3

    def of_heads(g):
        a, b = sums[:, g * wide : (g + 1) * wide], 4 * wide + g * (heads - wide)
        return jnp.concatenate([a, sums[:, b : b + heads - wide]], axis=1)

    f = [sums[:, base + i * hidden : base + (i + 1) * hidden] for i in range(3)]
    return [
        [tuple(r[i] for r in raw[0:3]) + (of_heads(i),) for i in range(3)],
        [tuple(r[...] for r in raw[3:6]) + (of_heads(3).T,)],
        [tuple(r[i] for r in raw[6:9]) + (f[i],) for i in range(2)],
        [tuple(r[...] for r in raw[9:12]) + (f[2],)],
    ]


def squares(pieces):
    a = b = 0.0
    for w, m, v, g in pieces:
        u = moments(g, m, v)[2] + DECAY * w
        a = a + jnp.sum(w * w, keepdims=True)
        b = b + jnp.sum(u * u, keepdims=True)
    return a, b


def step_kernel(T, *refs):
    raw, (sums, norms, small, bo, tg), rest = refs[:12], refs[12:17], refs[17:]
    lg, lm, lv, ig, im, iv = rest[:6]
    bo_out, tg_out = rest[6:8]
    outs, (lg_out, lm_out, lv_out, ig_out, im_out, iv_out, trust) = rest[8:20], rest[20:27]
    for j in range(bo.shape[0]):
        tg_out[:, j, :] = tg[j].astype(f32)
    bo_out[...] = jnp.swapaxes(bo[...].astype(f32), 0, 1).astype(bf)
    size = jnp.sqrt(norms[:, 0:1])
    for i, pieces in enumerate(matrices(raw, sums)):
        ratio = size[2 * i : 2 * i + 1] / size[2 * i + 1 : 2 * i + 2]
        for j, (w, m, v, g) in enumerate(pieces):
            m, v, u = moments(g, m, v)
            w = w - RATE * ratio * (u + DECAY * w)
            for k, value in enumerate((w, m, v)):
                if outs[3 * i + k].ndim == 3:
                    outs[3 * i + k][j] = value
                else:
                    outs[3 * i + k][...] = value
        trust[i : i + 1, 0:1] = size[2 * i : 2 * i + 1]
        trust[i : i + 1, 1:2] = size[2 * i + 1 : 2 * i + 2]
    hidden = ig.shape[1]
    me = lax.axis_index("tp")
    mine = small[8:10, 0:hidden]
    for t in range(1, T):
        mine = jnp.where(me == t, small[8 + 2 * t : 10 + 2 * t, 0:hidden], mine)
    for grad, old, new in (
        (small[0:4, :], (lg, lm, lv), (lg_out, lm_out, lv_out)),
        (mine, (ig, im, iv), (ig_out, im_out, iv_out)),
    ):
        m, v, u = moments(grad, old[1][...], old[2][...])
        new[0][...] = old[0][...] - RATE_GAINS * u
        new[1][...] = m
        new[2][...] = v

def moments(gradient, moment, square):
    moment = BETA_ONE * moment + (1.0 - BETA_ONE) * gradient
    square = BETA_TWO * square + (1.0 - BETA_TWO) * gradient * gradient
    update = (
        moment / (1.0 - BETA_ONE**STEP) / (jnp.sqrt(square / (1.0 - BETA_TWO**STEP)) + EPS_ADAM)
    )
    return (moment, square, update)


def body(
    F, C, T,
    tokens, cotangent, layer_gains, layer_first, layer_second, inner_gains, inner_first, inner_second,
    attend_weight, attend_first, attend_second, merge_weight, merge_first, merge_second,
    expand_weight, expand_first, expand_second, shrink_weight, shrink_first, shrink_second,
):
    bf, f32 = jnp.bfloat16, jnp.float32
    D = tokens.shape[-1]
    R = attend_weight.shape[1]
    rows = tokens.shape[1]
    J = C * T // 2
    assert J == tokens.shape[0]
    n = -(-J * rows // 48) * 48
    heads = attend_weight.shape[2]
    hidden = expand_weight.shape[2]
    fast = R % 16 == 0
    both = [rotary_tables(low, J, rows, n) for low in range(2)]
    tables, biases = (jnp.asarray(np.stack(parts)) for parts in zip(*both))
    raw = (
        attend_weight, attend_first, attend_second, merge_weight, merge_first, merge_second,
        expand_weight, expand_first, expand_second, shrink_weight.T, shrink_first.T, shrink_second.T,
    )
    wholes = ()
    if not fast:
        wide = heads * 2 // 3
        four = [raw[0][0], raw[0][1], raw[0][2], raw[3].T]
        pack_a = jnp.concatenate([w[:, :wide] for w in four] + [w[:, wide:] for w in four], axis=1).astype(bf)
        pack_f = jnp.concatenate([raw[6][0], raw[6][1], raw[9]], axis=1).astype(bf)
        wholes = tuple(
            lax.all_gather(lax.all_gather(p, ("fsdp", "ctx"), axis=0, tiled=True), "tp", axis=0)
            for p in (pack_a, pack_f)
        )
    out = block_call(
        F, C, T, R, n, fast, tokens, cotangent, wholes, raw, layer_gains, inner_gains, tables, biases
    )
    bo, tg, sums, small, norms = out[:5]
    if not fast:
        sums = jnp.concatenate([out[-1], out[-2]], axis=2).astype(f32)
        same = [[t for t in range(T) if t % 2 == k] for k in range(2)]
        sums = lax.psum_scatter(sums, "tp", scatter_dimension=0, axis_index_groups=same, tiled=False)
        sums = lax.psum_scatter(sums, ("fsdp", "ctx"), scatter_dimension=0, tiled=True)
        parts = []
        for pieces in matrices(raw, sums):
            parts += [a[0, 0] for a in squares(pieces)]
        parts = lax.psum(jnp.stack(parts), ("fsdp", "ctx", "tp"))
        norms = jnp.broadcast_to(parts[:, None], (8, 128))
    gains = (layer_gains, layer_first, layer_second, inner_gains, inner_first, inner_second)
    turned = (rows, J, D)
    outs = [(turned, bf), (turned, f32)] + [(a.shape, f32) for a in raw + gains] + [((4, 2), f32)]
    outs = local_call(functools.partial(step_kernel, T), [*raw, sums, norms, small, bo, tg, *gains], outs)
    outs = list(outs)
    outs[:2] = [a.transpose(1, 0, 2) for a in outs[:2]]
    return tuple(a.T if 11 <= i < 14 else a for i, a in enumerate(outs))


def solution(mesh):
    tok = P("fsdp", ("ctx", "tp"), None)
    wide = P(None, ("fsdp", "ctx"), "tp")
    tall = P("tp", ("fsdp", "ctx"))
    split = P(None, "tp")
    sizes = (mesh.shape["fsdp"], mesh.shape["ctx"], mesh.shape["tp"])
    return jax.shard_map(
        functools.partial(body, *sizes),
        mesh=mesh,
        in_specs=(tok, tok, P(), P(), P(), split, split, split)
        + (wide,) * 3 + (tall,) * 3 + (wide,) * 3 + (tall,) * 3,
        out_specs=(tok, tok) + (wide,) * 3 + (tall,) * 3 + (wide,) * 3 + (tall,) * 3
        + (P(),) * 3 + (split,) * 3 + (P(),),
        check_vma=False,
    )
```

```python
import functools
import jax
import jax.numpy as jnp
import numpy as np
from jax import lax
from jax.experimental import pallas as pl
from jax.experimental.pallas import tpu as pltpu
from jax.sharding import PartitionSpec as P

HD = 64
GRID = 32
STEP = 5
VALID = 1025
BETA_ONE = 0.5
BETA_TWO = 0.5
EPS_ADAM = 1e-06
DECAY = 0.01
RATE = 0.5
RATE_GAINS = 0.3
MESH = pl.DeviceIdType.MESH
f32 = jnp.float32
bf = jnp.bfloat16


class Place:
    def __init__(self, F, C, T):
        self.F, self.C, self.T, self.H = F, C, T, T // 2
        self.f = lax.axis_index("fsdp")
        self.c = lax.axis_index("ctx")
        self.t = lax.axis_index("tp")
        self.low = lax.rem(self.t, 2)
        self.high = lax.div(self.t, 2)
        self.pair = self.c * self.H + self.high
        self.pairs = C * self.H
        self.sibling = {"tp": self.t + 1 - 2 * self.low}
        self.xs = [lax.rem(self.f + k, F) for k in range(F)]
        self.ys = [lax.rem(self.high + k, self.H) for k in range(self.H)]
        self.zs = [lax.rem(self.c + k, C) for k in range(C)]

    def at_x(self, k):
        return {"fsdp": self.xs[k]}

    def at_y(self, k):
        return {"tp": self.ys[k] * 2 + self.low}

    def at_z(self, k):
        return {"ctx": self.zs[k]}

    def pair_at(self, k):
        i = lax.rem(self.pair + k, self.pairs)
        return i, {"ctx": lax.div(i, self.H), "tp": lax.rem(i, self.H) * 2 + self.low}

    def tees(self):
        return [{"tp": lax.rem(self.t + k, self.T)} for k in range(1, self.T)]

    def everyone(self):
        return [
            {"fsdp": self.xs[a], "ctx": self.zs[b], "tp": lax.rem(self.t + d, self.T)}
            for a in range(self.F) for b in range(self.C) for d in range(self.T) if a + b + d
        ]

    def partners(self, with_x):
        out = self.tees() + [
            {"ctx": self.zs[c], "tp": self.ys[y] * 2 + self.low} for c in range(1, self.C) for y in range(self.H)
        ]
        if with_x:
            out += [{"fsdp": self.xs[a], "ctx": self.zs[b]} for a in range(1, self.F) for b in range(self.C)]
        return out


def hail(partners):
    barrier = pltpu.get_barrier_semaphore()
    for partner in partners:
        pl.semaphore_signal(barrier, inc=1, device_id=partner, device_id_type=MESH)


def heard(partners):
    pl.semaphore_wait(pltpu.get_barrier_semaphore(), len(partners))


class Sems:
    def __init__(self, send, recv):
        self.send, self.recv, self.n = send, recv, 0

    def remote(self, src, dst, device):
        i = self.n
        self.n += 1
        return pltpu.make_async_remote_copy(
            src, dst, self.send.at[i], self.recv.at[i], device_id=device, device_id_type=MESH
        )

    def local(self, src, dst):
        i = self.n
        self.n += 1
        return pltpu.make_async_copy(src, dst, self.send.at[i])


class Exchange:
    def __init__(self, place, sems, src, dst):
        self.own = sems.local(src.at[place.pair], dst.at[place.pair])
        self.copies = []
        for k in range(1, place.pairs):
            i, device = place.pair_at(k)
            self.copies.append(sems.remote(src.at[i], dst.at[place.pair], device))

    def start(self, first=0, last=None):
        for copy in ([self.own] + self.copies)[first:last]:
            copy.start()

    def wait(self):
        self.own.wait()
        for copy in self.copies:
            copy.wait_recv()

    def finish(self):
        for copy in self.copies:
            copy.wait_send()


class Gather:
    def __init__(self, place, sems, pack, whole, cols, first):
        P, R = place, pack.shape[0]
        C, F, H = P.C, P.F, P.H
        n = C * R
        window = pl.ds(*cols)

        def push(t, row, rows, device):
            block = whole.at[t, pl.ds(pl.multiple_of(row, 16), rows), window]
            return sems.remote(block, block, device)

        row = (P.f * C + P.c) * R
        base = P.f * n
        self.own = sems.local(
            pack.at[:, window], whole.at[P.t, pl.ds(pl.multiple_of(row, 16), R), window]
        )
        chain = []
        for j in range(1, C):
            right = push(P.t, (P.f * C + jnp.maximum(P.c - j + 1, 0)) * R, R, P.at_z(1))
            left = push(P.t, (P.f * C + jnp.minimum(P.c + j - 1, C - 1)) * R, R, P.at_z(C - 1))
            chain.append([
                (right, jnp.logical_and(P.c + 1 < C, P.c - j + 1 >= 0), P.c - j >= 0),
                (left, jnp.logical_and(P.c >= 1, P.c + j - 1 < C), P.c + j < C),
            ])
        self.chain = chain
        tees = [y * 2 + P.low for y in P.ys]
        if first == "y":
            second = [push(P.t, base, n, P.at_y(k)) for k in range(1, H)]
            third = [push(t, base, n, P.at_x(k)) for k in range(1, F) for t in tees]
            over_3 = [push(t, base, n, P.sibling) for t in tees[1:]]
            over_4 = [push(t, P.xs[k] * n, n, P.sibling) for k in range(1, F) for t in tees]
        else:
            second = [push(P.t, base, n, P.at_x(k)) for k in range(1, F)]
            third = [push(P.t, 0, n * F, P.at_y(k)) for k in range(1, H)]
            over_3 = [push(P.t, P.xs[k] * n, n, P.sibling) for k in range(1, F)]
            over_4 = [push(t, 0, n * F, P.sibling) for t in tees[1:]]
        over_2 = [push(P.t, base, n, P.sibling)]
        none = [[] for _ in chain]
        self.waits = none + [[], second, third]
        self.starts = none + [second + over_2, third + over_3, over_4]
        self.sent_over = over_2 + over_3 + over_4

    def stage(self, s):
        if s == 0:
            self.own.wait()
        if 0 < s <= len(self.chain):
            for copy, _, gets in self.chain[s - 1]:
                pl.when(gets)(copy.wait_recv)
        for copy in self.waits[s]:
            copy.wait_recv()
        if s < len(self.chain):
            for copy, sends, _ in self.chain[s]:
                pl.when(sends)(copy.start)
        for copy in self.starts[s]:
            copy.start()

    def finish(self):
        for copy in self.sent_over:
            copy.wait_recv()

    def settle(self):
        for step in self.chain:
            for copy, sends, _ in step:
                pl.when(sends)(copy.wait_send)
        for group in self.starts:
            for copy in group:
                copy.wait_send()


def by_rows(rows, step, body):
    def it(i, _):
        body(pl.multiple_of(i * step, step), step)
        return 0

    lax.fori_loop(0, rows // step, it, 0)


class Reduce:
    def __init__(self, place, sems, view, D, width, first, lands, out, out_col, R):
        P, n = place, place.C * R
        C, F, H = P.C, P.F, P.H
        L1, L2, L3 = lands
        self.out, self.to, self.R = out, pl.ds(out_col, width), R
        base = pl.multiple_of(P.f * n, 16)
        mine = pl.multiple_of(base + P.c * R, 16)
        self.copies = [[], [], []]

        def rows(u, start, count):
            return view(u, pl.ds(start, count))

        def send(stage, src, dst, device):
            self.copies[stage].append(sems.remote(src, dst, device))

        if first == "x":
            for k in range(1, F):
                for u in range(H):
                    send(0, rows(u, pl.multiple_of(P.xs[k] * n, 16), n), L1.at[k - 1, u], P.at_x(k))
            for k in range(1, H):
                send(1, rows(P.ys[k], base, n), L2.at[k - 1], P.at_y(k))
            self.adds = [
                [(rows(u, base, n), [L1.at[k - 1, u] for k in range(1, F)]) for u in range(H)],
                [(rows(P.high, base, n), [L2.at[k - 1] for k in range(1, H)])],
            ]
        else:
            for k in range(1, H):
                send(0, rows(P.ys[k], 0, D), L1.at[k - 1], P.at_y(k))
            for k in range(1, F):
                send(1, rows(P.high, pl.multiple_of(P.xs[k] * n, 16), n), L2.at[k - 1], P.at_x(k))
            self.adds = [
                [(rows(P.high, 0, D), [L1.at[k - 1] for k in range(1, H)])],
                [(rows(P.high, base, n), [L2.at[k - 1] for k in range(1, F)])],
            ]
        for k in range(1, C):
            send(2, rows(P.high, pl.multiple_of(base + P.zs[k] * R, 16), R), L3.at[k - 1], P.at_z(k))
        self.last = (rows(P.high, mine, R), [L3.at[k - 1] for k in range(1, C)])

    def stage(self, s):
        if s > 0:
            for copy in self.copies[s - 1]:
                copy.wait_recv()
        if s in (1, 2):
            for dst, lands in self.adds[s - 1]:

                def add(r, k, dst=dst, lands=lands):
                    v = dst[pl.ds(r, k), :].astype(f32)
                    for land in lands:
                        v = v + land[pl.ds(r, k), :].astype(f32)
                    dst[pl.ds(r, k), :] = v.astype(bf)

                by_rows(dst.shape[0], 96, add)
        if s == 3:
            dst, lands = self.last
            v = dst[...].astype(f32)
            for land in lands:
                v = v + land[...].astype(f32)
            self.out[:, self.to] = v
        else:
            for copy in self.copies[s]:
                copy.start()

    def settle(self):
        for group in self.copies:
            for copy in group:
                copy.wait_send()


def reduce_lands(parts, F, C, H, D, R):
    out = []
    for (_, n), first in parts:
        if first == "x":
            out += [(F - 1, H, C * R, n), (H - 1, C * R, n)]
        else:
            out += [(H - 1, D, n), (F - 1, C * R, n)]
        out.append((C - 1, R, n))
    return [pltpu.VMEM(s, bf) for s in out]
EPS=1e-6
def dot(a,b): return jnp.dot(a,b,preferred_element_type=f32)
def dot_t(a,b): return lax.dot_general(a,b,(((1,),(1,)),((),())),preferred_element_type=f32)
def dot_l(a,b): return lax.dot_general(a,b,(((0,),(0,)),((),())),preferred_element_type=f32)

def chunks(rows, step, body):
    def it(i,_):
        body(pl.ds(pl.multiple_of(i*step,step),step)); return 0
    lax.fori_loop(0,rows//step,it,0)

def norm(v):
    mean=jnp.mean(v,axis=-1,keepdims=True)
    var=jnp.mean(v*v,axis=-1,keepdims=True)-mean*mean
    inv=lax.rsqrt(var+EPS)
    return (v-mean)*inv, inv

def spread(src3, dst):
    J,r,D=src3.shape
    n=dst.shape[0]
    pad=n-J*r
    if pad: dst[n-16:n,:]=jnp.zeros((16,D),f32)
    for j in range(J):
        dst[j*r:(j+1)*r,:]=src3[j].astype(f32)

def join(WA, g, dst, T):
    def it(i,_):
        s=pl.ds(pl.multiple_of(i*96,96),96)
        for t in range(T):
            dst[s,128*t:128*t+128]=WA[t,s,128*g:128*g+128]
        for u in range(T//2):
            c=pl.ds(512+128*(g//2),128)
            a=WA[2*u,s,c].astype(f32); b=WA[2*u+1,s,c].astype(f32)
            if g%2==0: b=pltpu.roll(b,64,1)
            else: a=pltpu.roll(a,64,1)
            dst[s,128*(T+u):128*(T+u)+128]=jnp.where(lanes(96,0),a,b).astype(bf)
        return 0
    lax.fori_loop(0,WA.shape[1]//96,it,0)

def turn(v, cos, sa, sb):
    n=v.shape[1]
    out=[]
    for i in range(n//128):
        a=v[:,i*128:(i+1)*128]
        out.append(a*cos+pltpu.roll(a,128-16,1)*sa+pltpu.roll(a,16,1)*sb)
    return jnp.concatenate(out,axis=1)

def normal(x, gains, ln1):
    def ln(s):
        v,_=norm(x[s,:])
        ln1[s,:]=(v*gains[0:1,:]+gains[1:2,:]).astype(bf)
    chunks(x.shape[0],48,ln)


def project(ln1, W, cos, sa, sb, dst, scale=None):
    n=ln1.shape[0]//2
    y=dot(ln1[0:n,:],W[...])
    if cos is not None: y=turn(y,cos[...],sa[...],sb[...])
    if scale is not None: y=y*scale
    dst[0:n,:]=y.astype(bf)


def lanes(n, a):
    return (lax.broadcasted_iota(jnp.int32,(n,128),1)//64==a)

def attention(q,K,V,bias,Es,linv,att,before,after):
    n=q.shape[0]; m=K.shape[0]
    def pair(p,_):
        c=pl.ds(pl.multiple_of(p*128,128),128)
        k2=K[:,c]; v2=V[:,c]
        q2=q[:,c]
        o=None; li=[]
        for a in (0,1):
            before(p,a)
            ka=jnp.where(lanes(m,a),k2,jnp.zeros_like(k2))
            va=jnp.where(lanes(m,a),v2,jnp.zeros_like(v2))
            S=dot_t(q2,ka)+bias[0:1,:]
            mx=jnp.max(S,axis=1,keepdims=True)
            e=jnp.exp(S-mx)
            l=1.0/jnp.sum(e,axis=1,keepdims=True)
            eb=e.astype(bf)
            Es[a]=eb
            after(p,a)
            oa=dot(eb,va)*l
            o=oa if o is None else o+oa
            li.append(l)
        att[:,c]=o.astype(bf)
        linv[:,c]=jnp.where(lanes(n,0),li[0],li[1])
        return 0
    lax.fori_loop(0,q.shape[1]//128,pair,0)

def merge(att,Wm,x,mid,gains,ln2,n):
    mid[...]=x[...]+dot_t(att[...],Wm[...])
    def ln(s):
        v,_=norm(mid[s,:])
        ln2[s,:]=(v*gains[2:3,:]+gains[3:4,:]).astype(bf)
    chunks(n,48,ln)

def norm_back(src, e_src, gain, add, dst, lay, row):
    n=src.shape[0]
    lay[row:row+2,:]=jnp.zeros((2,src.shape[1]),f32)
    def it(s):
        a,inv=norm(src[s,:]); e=e_src[s,:]
        lay[row:row+1,:]+=jnp.sum(e*a,axis=0,keepdims=True)
        lay[row+1:row+2,:]+=jnp.sum(e,axis=0,keepdims=True)
        eg=e*gain
        d=add[s,:].astype(f32)+inv*(eg-jnp.mean(eg,axis=1,keepdims=True)-a*jnp.mean(eg*a,axis=1,keepdims=True))
        dst[s,:]=d.astype(dst.dtype)
    chunks(n,48,it)


VMEM = pl.BlockSpec(memory_space=pltpu.VMEM)
HBM = pl.BlockSpec(memory_space=pl.ANY)
LIMIT = 60 * 2**20


def local_call(body, ins, outs, scratch=(), flops=0):
    return pl.pallas_call(
        body,
        out_shape=[jax.ShapeDtypeStruct(s, d) for s, d in outs],
        in_specs=[VMEM] * len(ins),
        out_specs=[VMEM] * len(outs),
        scratch_shapes=[pltpu.VMEM(s, d) for s, d in scratch],
        compiler_params=pltpu.CompilerParams(vmem_limit_bytes=LIMIT),
    )(*ins)


def rotary_tables(low, pairs, rows, total):
    quarter = HD // 4

    def places(half):
        return ((np.arange(pairs)[:, None] * 2 + half) * rows + np.arange(rows)).reshape(-1)

    def bias(half):
        out = np.full((total,), -1e30, np.float32)
        out[: pairs * rows] = np.where(places(half) < VALID, 0.0, -1e30)
        return out

    positions = places(low)
    inside = (positions >= 1) & (positions <= GRID * GRID)
    patch = np.where(inside, positions - 1, 0)
    frequency = 10000.0 ** (-np.arange(quarter) / quarter)
    row_angle = (patch // GRID)[:, None] * frequency
    column_angle = (patch % GRID)[:, None] * frequency
    angles = np.zeros((total, HD))
    angles[: pairs * rows] = np.concatenate([row_angle, row_angle, column_angle, column_angle], axis=-1)
    angles = np.concatenate([angles, angles], axis=-1)
    sine = np.sin(angles)
    first = (np.arange(2 * HD) // quarter) % 2 == 0
    turns = np.stack([np.cos(angles), np.where(first, -sine, 0.0), np.where(first, 0.0, sine)])
    return turns.astype(np.float32), np.concatenate([bias(low), bias(1 - low)])[None]


GATHER_A = (((0, 384), "y"), ((384, 384), "x"))
GATHER_F = tuple(((256 * i, 256), k) for i, k in enumerate("yxyxyx"))
FIRST_F = 4
REDUCE_H = (((1024, 256), "x"), ((1280, 256), "y"))
REDUCE_G = (((0, 256), "x"), ((256, 256), "y"), ((512, 256), "x"), ((768, 256), "y"))
REDUCE_A = (((0, 256), "x"), ((256, 256), "y"), ((512, 128), "x"), ((640, 128), "y"))
PLAN = {
    "start": ("A00", "A10"),
    "line1": ("A01", "A11", "F00", "F10"),
    "line2": ("A02", "A12", "F01", "F11"),
    "z": ("A03", "A13", "F02", "F12"),
    "early": ("A04", "A14", "F03", "F13", "F20", "F30", "F40", "F50"),
    "tokens": ("F21", "F31", "F41", "F51"),
    "last": ("A05", "A15", "F22", "F32", "F42", "F52"),
    "k": ("F04", "F14"),
    "v": ("F23", "F33"),
    "q": ("F43", "F53"),
    "p1": ("cot",),
    "p2": ("F24", "F34"),
    "o3": ("F05", "F15"),
    "o5": ("F44", "F54"),
    "merged": ("F25", "F35"),
    "ones": ("F45", "F55"),
    "shrunk": ("H00", "H10"),
    "expanded0": ("H01", "H11", "G00"),
    "expanded1": ("G10",),
    "expanded2": ("G20",),
    "expanded3": ("G30",),
    "back1": ("H02", "H12", "G01"),
    "back3": ("G11",),
    "back4": ("G21", "H03", "H13"),
    "back5": ("G12",),
    "looped": ("G31", "G02"),
    "main": ("B00", "B10", "G22"),
    "tailed": ("G32",),
    "tail": ("B20", "B30"),
    "back_out": ("B01", "B11"),
    "hop0": ("B21", "B31"),
    "hop1": ("B02", "B12"),
    "hop2": ("B22", "B32", "G03", "G13", "G23", "G33"),
    "end": ("B03", "B13", "B23", "B33"),
}


def mine_and_theirs(tiles, low):
    a, b = tiles
    return jnp.where(low == 0, a, b), jnp.where(low == 0, b, a)


def halves(tile, low):
    other = pltpu.roll(tile, 64, 1)
    return jnp.where(low == 0, tile, other), jnp.where(low == 0, other, tile)


def block_kernel(F, C, T, R, n, weights, plan, tok, cot, *rest):
    if weights:
        WF_in = None
    else:
        (WA_in, WF_in), rest = rest[:2], rest[2:]
    raw, rest = rest[:12], rest[12:]
    gains, inner, tables, biases = rest[:4]
    bo_out, tg_out, sums, small, norms = rest[4:9]
    WF, x_h, ln1_h, q_h, K_h, V_h, E, linv_h, att_h = rest[9:18]
    W_h = rest[18:22]
    rest = rest[22:]
    if not weights:
        (GF, GA), rest = rest[:2], rest[2:]
    (IG, LN2, CT, GB, XO, mid, cin, tg, SM, SML, NV, NVL, big, GA_s, pa, pf, turns, bias, send, recv, local, free) = rest[:22]
    lands = rest[22:]
    place = Place(F, C, T)
    H, low, sib = place.H, place.low, place.sibling
    sems = Sems(send, recv)
    partners = place.everyone() if weights else place.partners(True)
    hail(partners)
    bo = cin
    J, r, D = bo.shape
    Hd = IG.shape[2]
    tiles = D // 128
    main = T * 128
    wide = D // T * 2 // 3
    top, bottom = pl.ds(0, n), pl.ds(n, n)
    nlocal = [0]
    ig = IG

    def slots(count):
        nlocal[0] += count
        return nlocal[0] - count

    def fetch(src, dst):
        copy = pltpu.make_async_copy(src, dst, local.at[slots(1)])
        copy.start()
        return copy

    cos, sa, sb = (turns.at[k] for k in range(3))
    if weights:
        GA = GA_s

        def GF(u, rows, start, size):
            return big.at[2 * u + start // D, rows, pl.ds(start % D, size)]

        WA = big
    else:
        WA = WA_in

    tokens = Exchange(place, sems, tok, tg)
    cots = Exchange(place, sems, cot, cin)
    swap_ln2 = sems.remote(LN2.at[top], LN2.at[bottom], sib)
    swap_ct = sems.remote(CT.at[top], CT.at[bottom], sib)
    swap_gb = sems.remote(GB.at[top], GB.at[bottom], sib)
    back_bo = Exchange(place, sems, bo, bo_out)
    back_tg = Exchange(place, sems, tg, tg_out)
    share = [sems.remote(inner, IG.at[place.t], device) for device in place.tees()]
    groups = {"A": [], "F": [], "H": [], "G": [], "B": []}
    if weights:
        for key, pack, whole, parts in (("A", pa, WA, GATHER_A), ("F", pf, WF, GATHER_F)):
            groups[key] = [Gather(place, sems, pack, whole, cols, first) for cols, first in parts]
        i = 0
        for key, parts in (("H", REDUCE_H), ("G", REDUCE_G), ("B", REDUCE_A)):
            for (start, size), first in parts:
                if key == "B":
                    view = lambda u, rows, c=pl.ds(start, size): GA.at[u, rows, c]
                    col = start
                else:
                    view = lambda u, rows, start=start, size=size: GF(u, rows, start, size)
                    col = D + start
                groups[key].append(
                    Reduce(place, sems, view, D, size, first, lands[3 * i : 3 * i + 3], sums, col, R)
                )
                i += 1

    def at(point):
        for step in plan.get(point, ()) if weights else ():
            if step == "cot":
                cots.start()
                continue
            groups[step[0]][int(step[1])].stage(int(step[2]))

    def at_loop(name, index, count):
        for k in range(count):
            if weights and plan.get(f"{name}{k}"):

                @pl.when(index == k)
                def _(k=k):
                    at(f"{name}{k}")

    def wait_all(key):
        for g in groups[key]:
            g.finish()

    def forward(x, ln1, q, K, V, Wq, Wk, Wv, Wm, att, linv, Es, *states):
        Ws = (Wq, Wk, Wv, Wm)
        tabs = [fetch(tables.at[low], turns), fetch(biases.at[low], bias)]
        if weights:
            gets = [fetch(raw[k], states[i]) for i, k in enumerate((0, 3, 6, 9))]
            for copy in gets:
                copy.wait()
            aw, mw, ew, sw = states
            four = [aw[0], aw[1], aw[2], mw[...].T]
            for g, w in enumerate(four):
                pa[:, wide * g : wide * (g + 1)] = w[:, :wide].astype(bf)
            for g in (0, 2):
                pair = [w[:, wide:] for w in four[g : g + 2]]
                pa[:, 4 * wide + 64 * g : 4 * wide + 64 * g + 128] = jnp.concatenate(pair, axis=1).astype(bf)
            for g, w in enumerate((ew[0], ew[1], sw[...])):
                pf[:, Hd * g : Hd * (g + 1)] = w.astype(bf)
            for g in groups["A"] + groups["F"]:
                g.own.start()
        heard(partners)
        IG[place.t] = inner[...]
        at("start")
        for copy in share:
            copy.start()
        at("line1")
        at("line2")
        tokens.start()
        if not weights:
            cots.start()
        at("z")
        at("early")
        tokens.wait()
        at("tokens")
        spread(tg, x)
        normal(x, gains, ln1)
        swap_ln1 = sems.remote(ln1.at[top], XO.at[1, :, pl.ds(0, D)], sib)
        swap_ln1.start()
        at("normed")
        if weights:
            at("last")
            wait_all("A")
        else:
            whole = pltpu.make_async_copy(WA_in, big, local.at[slots(1)])
            whole.start()
            whole.wait()
        saves = [fetch(x, x_h), fetch(ln1.at[top], ln1_h.at[top])]
        swap = [sems.remote(X.at[top], XO.at[0, :, pl.ds(o, D)], sib) for X, o in ((K, 0), (V, D))]
        for copy in tabs:
            copy.wait()
        join(big, 1, Wk, T)
        project(ln1, Wk, cos, sa, sb, K)
        swap[0].start()
        at("k")
        join(big, 2, Wv, T)
        project(ln1, Wv, None, None, None, V)
        swap[1].start()
        at("v")
        join(big, 0, Wq, T)
        project(ln1, Wq, cos, sa, sb, q, 0.125)
        join(big, 3, Wm, T)
        at("q")
        saves += [fetch(a, b) for a, b in zip(Ws, W_h)] + [fetch(q, q_h)]
        for copy, X in zip(swap, (K, V)):
            copy.wait_recv()
        K[bottom, :] = XO[0, :, 0:D]
        V[bottom, :] = XO[0, :, D : 2 * D]
        saves += [fetch(K, K_h), fetch(V, V_h)]
        swap_ln1.wait_recv()
        saves += [fetch(XO.at[1, :, pl.ds(0, D)], ln1_h.at[bottom])]
        e0 = slots(2)

        def put_e(h):
            slot = lax.rem(h, 2)
            return pltpu.make_async_copy(Es.at[slot], E.at[h], local.at[e0 + slot])

        def before(p, a):
            at_loop("p" if a == 0 else "o", p, tiles)

            @pl.when(p > 0)
            def _():
                put_e(2 * p + a - 2).wait()

        def after(p, a):
            put_e(2 * p + a).start()

        attention(q, K, V, bias, Es, linv, att, before, after)
        at("attended")
        late = [fetch(linv, linv_h), fetch(att, att_h)]
        merge(att, Wm, x, mid, gains, LN2, n)
        swap_ln2.start()
        at("merged")
        for h in (2 * tiles - 2, 2 * tiles - 1):
            put_e(h).wait()
        for copy in saves + late:
            copy.wait()
        for copy in swap + [swap_ln1]:
            copy.wait_send()
        pl.semaphore_signal(free.at[0], inc=1, device_id=sib, device_id_type=MESH)

    pl.run_scoped(
        forward,
        pltpu.VMEM((n, D), f32),
        pltpu.VMEM((2 * n, D), bf),
        pltpu.VMEM((n, D), bf),
        pltpu.VMEM((2 * n, D), bf),
        pltpu.VMEM((2 * n, D), bf),
        *[pltpu.VMEM((D, D), bf)] * 4,
        pltpu.VMEM((n, D), bf),
        pltpu.VMEM((n, D), f32),
        pltpu.VMEM((2, n, 2 * n), bf),
        *[pltpu.VMEM(raw[k].shape, f32) for k in (0, 3, 6, 9)],
    )
    tokens.finish()
    for part in groups["A"]:
        part.settle()

    def feed(WFv, gate, up, act, gh, out, XT):
        w0 = slots(2)
        WF_from = WF if weights else WF_in

        def get_w(t, start, size):
            slot = lax.rem(t, 2)
            return pltpu.make_async_copy(
                WF_from.at[t, :, pl.ds(start, size)], WFv.at[slot, :, pl.ds(0, size)], local.at[w0 + slot]
            )

        def through(body, start, size, init):
            def step(t, c):
                get_w(t, start, size).wait()
                c = body(t, lax.rem(t, 2), c)

                @pl.when(t + 2 < T)
                def _():
                    get_w(t + 2, start, size).start()

                return c

            return lax.fori_loop(0, T, step, init)

        def ahead(start, size):
            for t in range(2):
                get_w(t, start, size).start()

        def swaps(cols):
            return [sems.remote(XT.at[2 * u + 1 - low, :, cols], XO.at[u, :, cols], sib) for u in range(H)]

        def pass_on(copies, t):
            for u, copy in enumerate(copies):

                @pl.when(t == 2 * u + 1 - low)
                def _(copy=copy):
                    copy.start()

        swap_h = swaps(pl.ds(2 * Hd, Hd))
        swap_g = swaps(pl.ds(0, 2 * Hd))
        at("feed")
        for g in groups["F"][:FIRST_F]:
            g.finish()
        ahead(0, 2 * Hd)
        def one(t, slot, c):
            at_loop("one", t, T)
            s0, s1 = c
            gu = dot(LN2[top, :], WFv[slot])
            g, u = gu[:, :Hd], gu[:, Hd:]
            a = g * jax.nn.sigmoid(g) * u
            gate[t] = g.astype(gate.dtype)
            up[t] = u.astype(up.dtype)
            act[t] = a
            return s0 + jnp.sum(a, axis=1, keepdims=True), s1 + jnp.sum(a * a, axis=1, keepdims=True)

        z = jnp.zeros((n, 1), f32)
        s0, s1 = through(one, 0, 2 * Hd, (z, z))
        at("ones")
        for g in groups["F"][FIRST_F:]:
            g.finish()
        ahead(2 * Hd, Hd)
        width = T * Hd
        mean = s0 / width
        inv = lax.rsqrt(s1 / width - mean * mean + EPS)
        SM[0] = jnp.zeros(SM.shape[1:], f32)
        cots.wait()
        spread(cin, out)
        CT[top, :] = out[...].astype(bf)
        swap_ct.start()
        out[...] = mid[...]
        pl.semaphore_wait(free.at[0], 1)
        for copy in share:
            copy.wait()

        def two(t, slot, c):
            r0, r1 = c
            n3 = (act[t] - mean) * inv
            act[t] = n3
            gt = ig[t, 0:1, :]
            hid = (n3 * gt + ig[t, 1:2, :]).astype(bf)
            XT[t, :, 2 * Hd : 3 * Hd] = hid
            pass_on(swap_h, t)
            out[...] += dot_t(hid, WFv[slot, :, 0:Hd])
            h = dot(CT[top, :], WFv[slot, :, 0:Hd])
            SM[0, pl.ds(8 + 2 * t, 1), 0:Hd] = jnp.sum(h * n3, axis=0, keepdims=True)
            SM[0, pl.ds(9 + 2 * t, 1), 0:Hd] = jnp.sum(h, axis=0, keepdims=True)
            e = h * gt
            gh[t] = e.astype(gh.dtype)
            return r0 + jnp.sum(e, axis=1, keepdims=True), r1 + jnp.sum(e * n3, axis=1, keepdims=True)

        r0, r1 = through(two, 2 * Hd, Hd, (z, z))
        ahead(0, 2 * Hd)
        r0, r1 = r0 / width, r1 / width
        swap_ct.wait_recv()
        swap_ln2.wait_recv()

        def put_f(u, start, value):
            if weights:
                GF(u, pl.ds(0, D), start, value.shape[1])[...] = value.astype(bf)
            else:
                GF[u, :, start : start + value.shape[1]] = value.astype(bf)

        for u in range(H):
            swap_h[u].wait_recv()
            t = 2 * u + low
            c = pl.ds(2 * Hd, Hd)
            put_f(u, 2 * Hd, dot_l(CT[top, :], XT[t, :, c]) + dot_l(CT[bottom, :], XO[u, :, c]))
        at("shrunk")
        for j in range(J):
            bo[j] = out[j * r : (j + 1) * r, :].astype(bf)
        back_bo.start()
        gln2 = out
        gln2[...] = jnp.zeros(gln2.shape, f32)

        def three(t, slot, _):
            at_loop("three", t, T)
            ga = inv * (gh[t].astype(f32) - r0 - act[t] * r1)
            g, u = gate[t].astype(f32), up[t].astype(f32)
            s = jax.nn.sigmoid(g)
            gg = (ga * u * s * (1.0 + g * (1.0 - s))).astype(bf)
            gu = (ga * g * s).astype(bf)
            XT[t, :, 0:Hd] = gg
            XT[t, :, Hd : 2 * Hd] = gu
            pass_on(swap_g, t)
            gln2[...] += dot_t(XT[t, :, 0 : 2 * Hd], WFv[slot])
            return 0

        through(three, 0, 2 * Hd, 0)
        at("threes")
        for u in range(H):
            swap_g[u].wait_recv()
            t = 2 * u + low
            for k in range(4):
                c = pl.ds(k * Hd // 2, Hd // 2)
                put_f(u, k * Hd // 2, dot_l(LN2[top, :], XT[t, :, c]) + dot_l(LN2[bottom, :], XO[u, :, c]))
                if u == H - 1:
                    at(f"expanded{k}")
        norm_back(mid, gln2, gains[2:3, :], CT, GB, SM.at[0], 2)
        swap_gb.start()
        at("fed")
        for copy in swap_h + swap_g + [swap_ln2, swap_ct]:
            copy.wait_send()
        pl.semaphore_signal(free.at[1], inc=1, device_id=sib, device_id_type=MESH)

    pl.run_scoped(
        feed,
        pltpu.VMEM((2, D, 2 * Hd), bf),
        pltpu.VMEM((T, n, Hd), bf),
        pltpu.VMEM((T, n, Hd), bf),
        pltpu.VMEM((T, n, Hd), f32),
        pltpu.VMEM((T, n, Hd), f32),
        pltpu.VMEM((n, D), f32),
        pltpu.VMEM((T, n, 3 * Hd), bf),
    )
    cots.finish()

    def attend(qv, lv, av, Wmv, gatt, dq, dK, dV, sK, sV, XT, LN1, Wqv, Wkv, Wvv):
        e0 = slots(2)

        cuts = [pl.ds(0, main), pl.ds(main, D - main)]
        give = [
            [sems.remote(S.at[:, cut], XO.at[0, :, pl.ds(off + cut.start, cut.size)], sib) for off, S in ((0, sK), (D, sV))]
            for cut in cuts
        ]
        swap_a = [
            [sems.remote(XT.at[1, u, :, cut], XO.at[1, :, pl.ds(H * cut.start + u * cut.size, cut.size)], sib) for u in range(H)]
            for cut in cuts
        ]
        Kv, Vv = LN2, CT
        Gq, Gk, Gv = gatt, qv, Kv

        def gradients(p, c):
            co, si, sj = cos[p, :], -sa[p, :], -sb[p, :]
            k0, v0 = pl.ds(c.start, c.size), pl.ds(D + c.start, c.size)
            g_q = turn(dq[p, c], co, si, sj)
            g_k = turn(dK[p, c] + XO[0, p, k0].astype(f32), co, si, sj)
            g_v = dV[p, c] + XO[0, p, v0].astype(f32)
            return g_q, g_k, g_v, av[p, c].astype(f32)

        def keep(p, c, values):
            for ref, v in zip((Gq, Gk, Gv), values):
                ref[p, c] = v.astype(bf)

        def main_rows(i, _):
            p = pl.ds(pl.multiple_of(i * 48, 48), 48)
            values = gradients(p, cuts[0])
            keep(p, cuts[0], values)
            for u in range(H):
                for g, v in enumerate(values):
                    two = v[:, 256 * u : 256 * u + 128], v[:, 256 * u + 128 : 256 * u + 256]
                    for side, z in enumerate(mine_and_theirs(two, low)):
                        XT[side, u, p, 128 * g : 128 * g + 128] = z.astype(bf)
            return 0

        def tail_rows(i, _):
            p = pl.ds(pl.multiple_of(i * 48, 48), 48)
            values = gradients(p, cuts[1])
            keep(p, cuts[1], values)
            first = lanes(48, 0)
            for u in range(H):
                split = [halves(v[:, 128 * u : 128 * u + 128], low) for v in values]
                for g in (0, 1):
                    (a0, b0), (a1, b1) = split[2 * g], split[2 * g + 1]
                    c = pl.ds(main + 128 * g, 128)
                    XT[0, u, p, c] = jnp.where(first, a0, b1).astype(bf)
                    XT[1, u, p, c] = jnp.where(first, b0, a1).astype(bf)
            return 0

        def weight_grad(k):
            for copy in swap_a[k]:
                copy.wait_recv()
            cut = cuts[k]
            for u in range(H):
                m = XT[0, u, :, cut]
                o = XO[1, :, H * cut.start + u * cut.size : H * cut.start + (u + 1) * cut.size]
                w = cut.size // 4
                if k == 0:
                    d = dot_l(LN1[top, :], m[:, : 3 * w]) + dot_l(LN1[bottom, :], o[:, : 3 * w])
                    e = dot_l(GB[top, :], m[:, 3 * w :]) + dot_l(GB[bottom, :], o[:, 3 * w :])
                    GA[u, :, 0 : 3 * w] = d.astype(bf)
                    GA[u, :, 3 * w : 4 * w] = e.astype(bf)
                else:
                    d = dot_l(LN1[top, :], m) + dot_l(LN1[bottom, :], o)
                    e = dot_l(GB[top, :], m) + dot_l(GB[bottom, :], o)
                    lane = lax.broadcasted_iota(jnp.int32, d.shape, 1)
                    GA[u, :, cut] = jnp.where(lane < 3 * w, d, e).astype(bf)

        def pairs(Es):
            def get_e(h):
                slot = lax.rem(h, 2)
                return pltpu.make_async_copy(E.at[h], Es.at[slot], local.at[e0 + slot])

            for h in range(2):
                get_e(h).start()
            gets = [fetch(a, b) for a, b in ((W_h[3], Wmv), (q_h, qv), (K_h, Kv), (V_h, Vv), (att_h, av), (linv_h, lv))]
            late = [fetch(a, b) for a, b in ((ln1_h, LN1), (W_h[0], Wqv), (W_h[1], Wkv), (W_h[2], Wvv))]
            gets[0].wait()
            gatt[...] = dot(GB[top, :], Wmv[...]).astype(bf)
            for copy in gets[1:]:
                copy.wait()

            def pair(p, _):
                at_loop("back", p, tiles)

                @pl.when(p == tiles - 1)
                def _():
                    for copy in give[0]:
                        copy.wait_recv()
                    lax.fori_loop(0, n // 48, main_rows, 0)
                    for copy in swap_a[0]:
                        copy.start()

                c = pl.ds(pl.multiple_of(p * 128, 128), 128)
                k2, v2, q2 = Kv[:, c], Vv[:, c], qv[:, c]
                dob = (gatt[:, c].astype(f32) * lv[:, c]).astype(bf)
                dl = dob.astype(f32) * av[:, c].astype(f32)
                m = 2 * n
                dqv = dkv = dvv = None
                for a in (0, 1):
                    ka = jnp.where(lanes(m, a), k2, jnp.zeros_like(k2))
                    va = jnp.where(lanes(m, a), v2, jnp.zeros_like(v2))
                    qa = jnp.where(lanes(n, a), q2, jnp.zeros_like(q2))
                    da = jnp.where(lanes(n, a), dob, jnp.zeros_like(dob))
                    delta = jnp.sum(jnp.where(lanes(n, a), dl, 0.0), axis=1, keepdims=True)
                    get_e(2 * p + a).wait()
                    e = Es[a]
                    dS = (e.astype(f32) * (dot_t(dob, va) - delta)).astype(bf)
                    x1, x2, x3 = dot(dS, ka), dot_l(dS, qa), dot_l(e, da)

                    @pl.when(p + 1 < tiles)
                    def _(a=a):
                        get_e(2 * p + 2 + a).start()

                    dqv = x1 if a == 0 else dqv + x1
                    dkv = x2 if a == 0 else dkv + x2
                    dvv = x3 if a == 0 else dvv + x3
                dq[:, c] = dqv * 0.125
                dK[:, c] = dkv[:n]
                dV[:, c] = dvv[:n]
                sK[:, c] = dkv[n:].astype(bf)
                sV[:, c] = dvv[n:].astype(bf)

                @pl.when(p == main // 128 - 1)
                def _():
                    pl.semaphore_wait(free.at[1], 1)
                    for copy in give[0]:
                        copy.start()

                return 0

            lax.fori_loop(0, tiles, pair, 0)
            return late

        def run(Es):
            late = pairs(Es)
            for copy in give[1]:
                copy.start()
            at("looped")
            for copy in late:
                copy.wait()

        pl.run_scoped(run, pltpu.VMEM((2, n, 2 * n), bf))
        swap_gb.wait_recv()
        weight_grad(0)
        at("main")
        for copy in give[1]:
            copy.wait_recv()
        lax.fori_loop(0, n // 48, tail_rows, 0)
        for copy in swap_a[1]:
            copy.start()
        at("tailed")

        def final(*rawv):
            states = [fetch(a, b) for a, b in zip(raw, rawv)] if weights else []
            gln1, tok, xv = dK, dq, lv
            get_x = fetch(x_h, xv)
            gln1[...] = dot_t(Gq[...], Wqv[...])
            gln1[...] += dot_t(Gk[...], Wkv[...])
            weight_grad(1)
            at("tail")
            gln1[...] += dot_t(Gv[top, :], Wvv[...])
            get_x.wait()
            norm_back(xv, gln1, gains[0:1, :], GB, tok, SM.at[0], 0)
            for j in range(J):
                tg[j] = tok[j * r : (j + 1) * r, :].astype(bf)
            back_tg.start()
            at("back_out")
            hops = [
                place.tees(),
                [place.at_x(k) for k in range(1, F)],
                [place.at_z(k) for k in range(1, C)],
            ]
            landed = 0
            for s, devices in enumerate(hops):
                copies = [sems.remote(SM.at[s], SML.at[landed + i], d) for i, d in enumerate(devices)]
                for copy in copies:
                    copy.start()
                at(f"hop{s}")
                total = SM[s]
                for i, copy in enumerate(copies):
                    copy.wait_recv()
                    total = total + SML[landed + i]
                for copy in copies:
                    copy.wait_send()
                landed += len(copies)
                SM[s + 1] = total
            small[...] = SM[len(hops)]
            if weights:
                for copy in states:
                    copy.wait()
                at("end")
                for i, pieces in enumerate(matrices(rawv, sums)):
                    for k, total in enumerate(squares(pieces)):
                        NV[0, 2 * i + k : 2 * i + k + 1, :] = jnp.broadcast_to(total, (1, 128))
                copies = [sems.remote(NV.at[0], NVL.at[i], d) for i, d in enumerate(partners)]
                for copy in copies:
                    copy.start()
                total = NV[0]
                for i, copy in enumerate(copies):
                    copy.wait_recv()
                    total = total + NVL[i]
                norms[...] = total
                for copy in copies:
                    copy.wait_send()
            else:
                norms[...] = jnp.zeros(norms.shape, f32)
            for copy in swap_a[0] + swap_a[1] + give[0] + give[1]:
                copy.wait_send()

        pl.run_scoped(final, *[pltpu.VMEM(a.shape, f32) for a in raw])

    pl.run_scoped(
        attend,
        pltpu.VMEM((n, D), bf),
        pltpu.VMEM((n, D), f32),
        pltpu.VMEM((n, D), bf),
        pltpu.VMEM((D, D), bf),
        pltpu.VMEM((n, D), bf),
        *[pltpu.VMEM((n, D), f32)] * 3,
        *[pltpu.VMEM((n, D), bf)] * 2,
        pltpu.VMEM((2, H, n, D), bf),
        pltpu.VMEM((2 * n, D), bf),
        *[pltpu.VMEM((D, D), bf)] * 3,
    )
    for key in "FHGB":
        for part in groups[key]:
            part.settle()
    for back in (back_bo, back_tg):
        back.wait()
        back.finish()
    swap_gb.wait_send()


def block_call(F, C, T, R, n, weights, tokens, cotangent, wholes, raw, gains, inner, tables, biases):
    shape = tokens.shape
    J, r, D = shape
    H, Hd = T // 2, inner.shape[1]
    heads = D // T
    nh = D // HD
    outs = [(shape, bf), (shape, bf), ((R, 4 * heads + 3 * Hd), f32), ((16, D), f32), ((8, 128), f32)]
    out_specs = [HBM, HBM, VMEM, VMEM, VMEM]
    saved = [((T, D, 3 * Hd) if weights else (8, 128), bf), ((n, D), f32), ((2 * n, D), bf), ((n, D), bf)]
    saved += [((2 * n, D), bf)] * 2 + [((nh, n, 2 * n), bf), ((n, D), f32), ((n, D), bf)] + [((D, D), bf)] * 4
    outs += saved
    out_specs += [HBM] * len(saved)
    grads = [((H, D, 3 * Hd), bf), ((H, D, D), bf)]
    if not weights:
        outs += grads
        out_specs += [VMEM, VMEM]
    small = (8, 128)
    scratch = [((T,) + inner.shape, f32)] + [((2 * n, D), bf)] * 3
    scratch += [((H, n, 3 * Hd), bf), ((n, D), f32), (shape, bf), (shape, bf)]
    everyone = F * C * T - 1 if weights else 1
    scratch += [((4, 16, D), f32), ((T + F + C - 3, 16, D), f32), ((1,) + small, f32), ((everyone,) + small, f32)]
    scratch += [((T, D, D), bf), grads[1] if weights else (small, bf)]
    scratch += [((R, D), bf), ((R, 3 * Hd), bf)] if weights else [(small, bf)] * 2
    scratch += [(tables.shape[1:], f32), (biases.shape[1:], f32)]
    scratch = [pltpu.VMEM(s, d) for s, d in scratch]
    scratch += [
        pltpu.SemaphoreType.DMA((320,)),
        pltpu.SemaphoreType.DMA((320,)),
        pltpu.SemaphoreType.DMA((64,)),
        pltpu.SemaphoreType.REGULAR((2,)),
    ]
    if weights:
        scratch += reduce_lands(REDUCE_H + REDUCE_G + REDUCE_A, F, C, H, D, R)
    return pl.pallas_call(
        functools.partial(block_kernel, F, C, T, R, n, weights, PLAN),
        out_shape=[jax.ShapeDtypeStruct(s, d) for s, d in outs],
        in_specs=[HBM] * (2 + len(wholes) + len(raw)) + [VMEM] * 2 + [HBM] * 2,
        out_specs=out_specs,
        scratch_shapes=scratch,
        compiler_params=pltpu.CompilerParams(collective_id=1, has_side_effects=True, vmem_limit_bytes=LIMIT),
    )(tokens, cotangent, *wholes, *raw, gains, inner, tables, biases)


def matrices(raw, sums):
    heads, hidden = raw[0].shape[2], raw[6].shape[2]
    base, wide = 4 * heads, heads * 2 // 3

    def of_heads(g):
        a, b = sums[:, g * wide : (g + 1) * wide], 4 * wide + g * (heads - wide)
        return jnp.concatenate([a, sums[:, b : b + heads - wide]], axis=1)

    f = [sums[:, base + i * hidden : base + (i + 1) * hidden] for i in range(3)]
    return [
        [tuple(r[i] for r in raw[0:3]) + (of_heads(i),) for i in range(3)],
        [tuple(r[...] for r in raw[3:6]) + (of_heads(3).T,)],
        [tuple(r[i] for r in raw[6:9]) + (f[i],) for i in range(2)],
        [tuple(r[...] for r in raw[9:12]) + (f[2],)],
    ]


def squares(pieces):
    a = b = 0.0
    for w, m, v, g in pieces:
        u = moments(g, m, v)[2] + DECAY * w
        a = a + jnp.sum(w * w, keepdims=True)
        b = b + jnp.sum(u * u, keepdims=True)
    return a, b


def step_kernel(T, *refs):
    raw, (sums, norms, small, bo, tg), rest = refs[:12], refs[12:17], refs[17:]
    lg, lm, lv, ig, im, iv = rest[:6]
    bo_out, tg_out = rest[6:8]
    outs, (lg_out, lm_out, lv_out, ig_out, im_out, iv_out, trust) = rest[8:20], rest[20:27]
    for j in range(bo.shape[0]):
        tg_out[:, j, :] = tg[j].astype(f32)
    bo_out[...] = jnp.swapaxes(bo[...].astype(f32), 0, 1).astype(bf)
    size = jnp.sqrt(norms[:, 0:1])
    for i, pieces in enumerate(matrices(raw, sums)):
        ratio = size[2 * i : 2 * i + 1] / size[2 * i + 1 : 2 * i + 2]
        for j, (w, m, v, g) in enumerate(pieces):
            m, v, u = moments(g, m, v)
            w = w - RATE * ratio * (u + DECAY * w)
            for k, value in enumerate((w, m, v)):
                if outs[3 * i + k].ndim == 3:
                    outs[3 * i + k][j] = value
                else:
                    outs[3 * i + k][...] = value
        trust[i : i + 1, 0:1] = size[2 * i : 2 * i + 1]
        trust[i : i + 1, 1:2] = size[2 * i + 1 : 2 * i + 2]
    hidden = ig.shape[1]
    me = lax.axis_index("tp")
    mine = small[8:10, 0:hidden]
    for t in range(1, T):
        mine = jnp.where(me == t, small[8 + 2 * t : 10 + 2 * t, 0:hidden], mine)
    for grad, old, new in (
        (small[0:4, :], (lg, lm, lv), (lg_out, lm_out, lv_out)),
        (mine, (ig, im, iv), (ig_out, im_out, iv_out)),
    ):
        m, v, u = moments(grad, old[1][...], old[2][...])
        new[0][...] = old[0][...] - RATE_GAINS * u
        new[1][...] = m
        new[2][...] = v

def moments(gradient, moment, square):
    moment = BETA_ONE * moment + (1.0 - BETA_ONE) * gradient
    square = BETA_TWO * square + (1.0 - BETA_TWO) * gradient * gradient
    update = (
        moment / (1.0 - BETA_ONE**STEP) / (jnp.sqrt(square / (1.0 - BETA_TWO**STEP)) + EPS_ADAM)
    )
    return (moment, square, update)


def body(
    F, C, T,
    tokens, cotangent, layer_gains, layer_first, layer_second, inner_gains, inner_first, inner_second,
    attend_weight, attend_first, attend_second, merge_weight, merge_first, merge_second,
    expand_weight, expand_first, expand_second, shrink_weight, shrink_first, shrink_second,
):
    bf, f32 = jnp.bfloat16, jnp.float32
    D = tokens.shape[-1]
    R = attend_weight.shape[1]
    rows = tokens.shape[1]
    J = C * T // 2
    assert J == tokens.shape[0]
    n = -(-J * rows // 48) * 48
    heads = attend_weight.shape[2]
    hidden = expand_weight.shape[2]
    fast = R % 16 == 0
    both = [rotary_tables(low, J, rows, n) for low in range(2)]
    tables, biases = (jnp.asarray(np.stack(parts)) for parts in zip(*both))
    raw = (
        attend_weight, attend_first, attend_second, merge_weight, merge_first, merge_second,
        expand_weight, expand_first, expand_second, shrink_weight.T, shrink_first.T, shrink_second.T,
    )
    wholes = ()
    if not fast:
        wide = heads * 2 // 3
        four = [raw[0][0], raw[0][1], raw[0][2], raw[3].T]
        pack_a = jnp.concatenate([w[:, :wide] for w in four] + [w[:, wide:] for w in four], axis=1).astype(bf)
        pack_f = jnp.concatenate([raw[6][0], raw[6][1], raw[9]], axis=1).astype(bf)
        wholes = tuple(
            lax.all_gather(lax.all_gather(p, ("fsdp", "ctx"), axis=0, tiled=True), "tp", axis=0)
            for p in (pack_a, pack_f)
        )
    out = block_call(
        F, C, T, R, n, fast, tokens, cotangent, wholes, raw, layer_gains, inner_gains, tables, biases
    )
    bo, tg, sums, small, norms = out[:5]
    if not fast:
        sums = jnp.concatenate([out[-1], out[-2]], axis=2).astype(f32)
        same = [[t for t in range(T) if t % 2 == k] for k in range(2)]
        sums = lax.psum_scatter(sums, "tp", scatter_dimension=0, axis_index_groups=same, tiled=False)
        sums = lax.psum_scatter(sums, ("fsdp", "ctx"), scatter_dimension=0, tiled=True)
        parts = []
        for pieces in matrices(raw, sums):
            parts += [a[0, 0] for a in squares(pieces)]
        parts = lax.psum(jnp.stack(parts), ("fsdp", "ctx", "tp"))
        norms = jnp.broadcast_to(parts[:, None], (8, 128))
    gains = (layer_gains, layer_first, layer_second, inner_gains, inner_first, inner_second)
    turned = (rows, J, D)
    outs = [(turned, bf), (turned, f32)] + [(a.shape, f32) for a in raw + gains] + [((4, 2), f32)]
    outs = local_call(functools.partial(step_kernel, T), [*raw, sums, norms, small, bo, tg, *gains], outs)
    outs = list(outs)
    outs[:2] = [a.transpose(1, 0, 2) for a in outs[:2]]
    return tuple(a.T if 11 <= i < 14 else a for i, a in enumerate(outs))


def solution(mesh):
    tok = P("fsdp", ("ctx", "tp"), None)
    wide = P(None, ("fsdp", "ctx"), "tp")
    tall = P("tp", ("fsdp", "ctx"))
    split = P(None, "tp")
    sizes = (mesh.shape["fsdp"], mesh.shape["ctx"], mesh.shape["tp"])
    return jax.shard_map(
        functools.partial(body, *sizes),
        mesh=mesh,
        in_specs=(tok, tok, P(), P(), P(), split, split, split)
        + (wide,) * 3 + (tall,) * 3 + (wide,) * 3 + (tall,) * 3,
        out_specs=(tok, tok) + (wide,) * 3 + (tall,) * 3 + (wide,) * 3 + (tall,) * 3
        + (P(),) * 3 + (split,) * 3 + (P(),),
        check_vma=False,
    )
```
